32 devices in a mesh: section: 2 (over x), dp: 4 (over z), mp: 4 (over y, core).
Axes of the slice: x: 2, y: 2, z: 4, core: 2. Of those that a mesh axis runs over, the one named last changes fastest.
Arguments:
- inputs: bfloat16 [2, 2, 4096, 512], P('section', None, ('dp', 'mp')), may hold values from -6 to 6
- cotangent: bfloat16 [2, 2, 4096, 512], P('section', None, ('dp', 'mp')), may hold values from -6 to 6
- expert_ids: int32 [2, 2, 4096, 1], P('section', None, ('dp', 'mp')), may hold values from 0 to 7; in each aligned block of 256 rows (0 to 255, 256 to 511, ..., all dimensions but the last counted through in order) at most 48 rows name the same one
- self_proj: bfloat16 [2, 512, 8, 256], P('section', None, 'mp')
- cross_proj: bfloat16 [2, 512, 8, 128], P('section', None, 'mp')
- gains: float32 [2, 3, 512], P('section'), may hold values from 0.5 to 1.5
- w_in: bfloat16 [2, 8, 512, 2048], P('section', 'mp'), may hold values from -0.25 to 0.25
- w_out: bfloat16 [2, 8, 2048, 512], P('section', 'mp'), may hold values from -0.1875 to 0.1875
Outputs:
- outputs: bfloat16 [2, 2, 4096, 512], P('section', None, ('dp', 'mp'))
- input_grad: float32 [2, 2, 4096, 512], P('section', None, ('dp', 'mp'))
- self_grad: float32 [2, 512, 8, 256], P('section', None, 'mp')
- cross_grad: float32 [2, 512, 8, 128], P('section', None, 'mp')
- gain_grad: float32 [2, 3, 512], P('section')
- w_in_grad: float32 [2, 8, 512, 2048], P('section', 'mp')
- w_out_grad: float32 [2, 8, 2048, 512], P('section', 'mp')
The draws below stay inside these ranges and needn't reach their ends.
Inputs may be any that keep to these rules, and one draw needn't show every extreme that they name: `expert_ids`: in the 256 rows of one device in one micro-batch (aligned blocks of the rows of both layers taken in order) no expert is named by more than 48 rows, a bound that some block reaches.
All inputs are finite; a program needn't handle non-finite values.
Results may differ from the reference program's by a relative error of at most 0.023.
Values may be sent and summed in bfloat16 or wider, within the bound.
No kernel may reach another device: no remote copies, remote signals or barrier semaphores. Data moves between devices by JAX's collectives and lax.ppermute only.
A program may use at most 256 MiB of HBM per device.

```python
import math
from functools import partial
import jax
import jax.numpy as jnp
import numpy as np
from jax import lax

D = 512
H = 8
HS = 64
FF = 2048
SEQ = 1024
MB = 2
TOK_DEV = 256
EXPERTS = 8
CAP = 48
TOKENS = 4096


def draw_self_proj(key, part):
    key = jax.random.fold_in(key, 11)
    base = jax.random.normal(key, (2, D, H, 4 * HS), jnp.float32)
    column = jnp.arange(4 * HS)
    scale = jnp.where(column >= 3 * HS, 12.0 * (H * HS) ** (-0.5), D ** (-0.5))
    return (base * scale).astype(jnp.bfloat16)


def draw_cross_proj(key, part):
    key = jax.random.fold_in(key, 12)
    base = jax.random.normal(key, (2, D, H, 2 * HS), jnp.float32)
    column = jnp.arange(2 * HS)
    layer = jnp.arange(2)
    outer = jnp.logical_and(layer[:, None] == 1, column[None, :] >= HS)
    scale = jnp.where(outer, 12.0 * (H * HS) ** (-0.5), D ** (-0.5)).reshape(2, 1, 1, 2 * HS)
    return (base * scale).astype(jnp.bfloat16)


def shard_levels(own_key, shape, split, smallest, high):
    level = 1.0
    for dim, blocks in split:
        draws = jax.random.uniform(jax.random.fold_in(jax.random.fold_in(own_key, 6), dim), (blocks,), jnp.float32, smallest / len(split), high / len(split))
        level = level * jnp.repeat(jnp.exp(draws), shape[dim] // blocks).reshape((-1,) + (1,) * (len(shape) - 1 - dim))
    return level


def assign_block(key, own, number, rows, amount, top, most, lean):
    order = jax.random.permutation(key, amount)
    packed, usual = shares(amount, rows * top, most, lean, True), shares(amount, rows * top, most, lean, False)
    places = jnp.arange(amount)

    def named(tallies, turn):
        used = int((tallies > 0).sum())
        fixed = max(1, used // 4)
        shifted = fixed + (places - fixed + turn * (used - fixed)) % max(1, amount - fixed)
        return jnp.zeros((amount,), jnp.int32).at[order[jnp.where(places < fixed, places, shifted)]].set(jnp.asarray(tallies, jnp.int32))

    tallies = jnp.where(number % 4 == 0, named(packed, number // 4), named(usual, number - number // 4 - 1))
    mixed = jax.random.permutation(jax.random.fold_in(own, 3), amount)
    source_of, taker = mixed[0:amount // 2 * 2:2], mixed[1:amount // 2 * 2:2]
    slack = jnp.minimum(tallies[source_of] - 1, most - tallies[taker]) // 2
    slack = jnp.where((source_of == order[0]) | (taker == order[0]) | (tallies[taker] == 0), 0, jnp.maximum(slack, 0))
    shifted = jax.random.randint(jax.random.fold_in(own, 4), (amount // 2,), 0, 1 << 20) % (slack + 1)
    tallies = tallies.at[source_of].add(-shifted).at[taker].add(shifted)
    members = jnp.searchsorted(jnp.cumsum(tallies), jnp.arange(rows * top), side="right").astype(jnp.int32)
    table = members.reshape(top, rows).T
    table = table[jax.random.permutation(jax.random.fold_in(own, 1), rows)]
    turn = jax.random.randint(jax.random.fold_in(own, 2), (rows, 1), 0, top)
    return jnp.take_along_axis(table, (jnp.arange(top)[None, :] + turn) % top, axis=1)


def shares(count, total, reach, skew, full):
    weights = [(1 << 20) // math.isqrt(grade ** skew) + 1 for grade in range(1, count + 1)]
    largest = reach if full else min(reach, max(-(-total // count), total * weights[0] // sum(weights)))
    least = 1 if total - largest >= count - 1 else 0
    given, rest = [largest] + [least] * (count - 1), total - largest - least * (count - 1)
    while rest > 0:
        candidates = [i for i in range(1, count) if given[i] < largest] or [i for i in range(1, count) if given[i] < reach]
        pool, remaining = sum([weights[i] for i in candidates]), rest
        for i in candidates:
            addition = min(reach - given[i], max(1, remaining * weights[i] // pool), rest)
            given[i] = given[i] + addition
            rest = rest - addition
    return np.array(given)


def gaussian(key, extent, scale, bound, shards=(), kind=jnp.bfloat16):
    drawn = scale * jax.random.normal(key, extent, jnp.float32)
    if shards:
        drawn = drawn * shard_levels(key, extent, shards, -0.22, 0.18)
    return jnp.clip(drawn, -bound, bound).astype(kind)


def setup_inputs(seed: int = 0) -> dict:
    splits = jax.random.split(jax.random.key(seed), 9)
    inputs = gaussian(splits[0], (2, MB, TOKENS, D), 1.0, 6.0, ((0, 2), (2, 16)))
    cotangent = gaussian(splits[1], (2, MB, TOKENS, D), 1.0, 6.0, ((0, 2), (2, 16)))
    expert_ids_keys = jax.random.split(jax.random.fold_in(splits[2], 1), 2 * MB * TOKENS // TOK_DEV)
    expert_ids_turns = jax.random.permutation(jax.random.fold_in(splits[2], 3), 2 * MB * TOKENS // TOK_DEV)
    expert_ids = jax.vmap(lambda own, number: assign_block(jax.random.fold_in(splits[2], 2), own, number, TOK_DEV, EXPERTS, 1, CAP, 2))(expert_ids_keys, expert_ids_turns).reshape((2, MB, TOKENS, 1))
    self_proj = draw_self_proj(jax.random.fold_in(splits[8], 71), 0)
    cross_proj = draw_cross_proj(jax.random.fold_in(splits[8], 71), 0)
    gains = jnp.clip(1.0 + 0.1 * jax.random.normal(splits[5], (2, 3, D), jnp.float32), 0.5, 1.5)
    w_in = gaussian(splits[6], (2, EXPERTS, D, FF), D ** -0.5, 0.25, ((0, 2), (1, 4)))
    w_out = gaussian(splits[7], (2, EXPERTS, FF, D), (FF // 2) ** -0.5, 0.1875, ((0, 2), (1, 4)))
    return {"inputs": inputs, "cotangent": cotangent, "expert_ids": expert_ids, "self_proj": self_proj, "cross_proj": cross_proj, "gains": gains, "w_in": w_in, "w_out": w_out}


EPS = 1e-05
NEG = -1000000000.0
HIGH = lax.Precision.HIGHEST

@jax.custom_vjp
def low(v):
    return lax.optimization_barrier(v.astype(jnp.bfloat16)).astype(jnp.float32)

@jax.custom_vjp
def low_back(v):
    return v

def low_keep(v):
    return (low(v), None)

def low_pass(kept, grad):
    return (grad,)

def back_keep(v):
    return (v, None)

def back_low(kept, grad):
    return (low(grad),)
low.defvjp(low_keep, low_pass)
low_back.defvjp(back_keep, back_low)

def rounded(values):
    return low(low_back(values))

def layer_norm(values, gain):
    centre = lax.optimization_barrier(jnp.mean(values, axis=-1, keepdims=True))
    centred = values - centre
    spread = lax.optimization_barrier(jnp.mean(centred * centred, axis=-1, keepdims=True))
    return centred * lax.rsqrt(spread + EPS) * gain

def attend_sequence(queries, keys, values, causal):
    places = jnp.arange(SEQ)
    allowed = places[None, :] <= places[:, None]
    if not causal:
        allowed = jnp.ones_like(allowed)
    raw = jnp.einsum('qhe,khe->hqk', queries, keys, precision=HIGH) * HS ** (-0.5)
    scores = jnp.where(allowed[None], low_back(raw), NEG)
    weights = jax.nn.softmax(scores, axis=-1)
    return rounded(jnp.einsum('hqk,khe->qhe', low(weights), values, precision=HIGH))

def attention(queries, keys, values, causal):
    number = queries.shape[0] // SEQ
    shaped = tuple((t.reshape(number, SEQ, H, HS) for t in (queries, keys, values)))
    block = jax.checkpoint(lambda parts: attend_sequence(parts[0], parts[1], parts[2], causal))
    return lax.map(block, shaped).reshape(-1, H, HS)

def self_block(residual, gain, weight, causal):
    normed = low(layer_norm(residual, gain))
    projected = rounded(jnp.einsum('td,dhf->thf', normed, weight[:, :, :3 * HS], precision=HIGH))
    heads = attention(projected[..., :HS], projected[..., HS:2 * HS], projected[..., 2 * HS:], causal)
    return residual + low_back(jnp.einsum('the,dhe->td', heads, weight[:, :, 3 * HS:], precision=HIGH))

def one_expert(parts):
    taken, expert_in, expert_out = parts
    before = low_back(jnp.dot(taken, expert_in, precision=HIGH))
    hidden = low(jax.nn.gelu(before))
    return rounded(jnp.dot(hidden, expert_out, precision=HIGH))

def expert_block(residual, gain, labels, first, second):
    normed = rounded(layer_norm(residual, gain))
    blocks = labels.reshape(-1, TOK_DEV)
    number = blocks.shape[0]
    hot = (blocks[:, :, None] == jnp.arange(EXPERTS)[None, None, :]).astype(jnp.int32)
    slot = lax.optimization_barrier(jnp.sum((jnp.cumsum(hot, axis=1) - hot) * hot, axis=2))
    place = blocks * CAP + slot
    target = (jnp.arange(number)[:, None] * (EXPERTS * CAP) + place).reshape(-1).astype(jnp.int32)
    sources = jnp.full((number * EXPERTS * CAP,), number * TOK_DEV, jnp.int32)
    sources = sources.at[target].set(jnp.arange(number * TOK_DEV, dtype=jnp.int32))
    padded = jnp.concatenate([normed, jnp.zeros((1, D), normed.dtype)], axis=0)
    grouped = padded[sources].reshape(number, EXPERTS, CAP, D).transpose(1, 0, 2, 3).reshape(EXPERTS, number * CAP, D)
    results = lax.map(jax.checkpoint(one_expert), (grouped, first, second))
    flat = results.reshape(EXPERTS, number, CAP, D).transpose(1, 0, 2, 3).reshape(-1, D)
    return residual + flat[target]

def memory_keys(memory, gain, weight):
    normed = low(layer_norm(memory, gain))
    return rounded(jnp.einsum('td,dhf->thf', normed, weight, precision=HIGH))

def cross_block(residual, gain, weight, keys_values):
    normed = low(layer_norm(residual, gain))
    queries = rounded(jnp.einsum('td,dhe->the', normed, weight[:, :, :HS], precision=HIGH))
    heads = attention(queries, keys_values[..., :HS], keys_values[..., HS:], False)
    return residual + low_back(jnp.einsum('the,dhe->td', heads, weight[:, :, HS:], precision=HIGH))

def forward(labels, inputs, self_proj, cross_proj, gains, w_in, w_out):
    source = inputs[0].reshape(-1, D)
    target = inputs[1].reshape(-1, D)
    hidden = self_block(source, gains[0, 0], self_proj[0], False)
    memory = expert_block(hidden, gains[0, 2], labels[0], w_in[0], w_out[0])
    keys_values = memory_keys(memory, gains[0, 1], cross_proj[0])
    hidden = self_block(target, gains[1, 0], self_proj[1], True)
    hidden = cross_block(hidden, gains[1, 1], cross_proj[1], keys_values)
    result = expert_block(hidden, gains[1, 2], labels[1], w_in[1], w_out[1])
    return jnp.stack([memory, result]).reshape(inputs.shape)

def reference(inputs, cotangent, expert_ids, self_proj, cross_proj, gains, w_in, w_out):
    labels = expert_ids.reshape(2, -1)
    floats = [t.astype(jnp.float32) for t in (inputs, self_proj, cross_proj, gains, w_in, w_out)]
    outputs, pullback = jax.vjp(partial(forward, labels), *floats)
    gradients = pullback(cotangent.astype(jnp.float32))
    return (outputs.astype(jnp.bfloat16), gradients[0], gradients[1], gradients[2], gradients[3], gradients[4], gradients[5])
```

```python
import functools

import jax
import jax.numpy as jnp
from jax import lax
from jax.experimental import pallas as pl
from jax.experimental.pallas import tpu as pltpu
from jax.sharding import PartitionSpec as P

SEQ = 1024
EPS = 1e-05
NEG = -1000000000.0
BF = jnp.bfloat16
F32 = jnp.float32
QB = 256


def dot(a, b, ca=1, cb=0):
    return lax.dot_general(a, b, (((ca,), (cb,)), ((), ())), preferred_element_type=F32)


def norm_parts(rows):
    centred = rows - jnp.mean(rows, axis=-1, keepdims=True)
    inverse = lax.rsqrt(jnp.mean(centred * centred, axis=-1, keepdims=True) + EPS)
    return centred * inverse, inverse


def norm_back(upstream, unit, inverse, gain):
    scaled = upstream * gain
    inner = (
        scaled
        - jnp.mean(scaled, axis=-1, keepdims=True)
        - unit * jnp.mean(scaled * unit, axis=-1, keepdims=True)
    )
    return inverse * inner, jnp.sum(upstream * unit, axis=0, keepdims=True)


def gelu_parts(z):
    square = z * z
    t = jnp.tanh(z * (0.7978845608028654 + (0.7978845608028654 * 0.044715) * square))
    half = 0.5 + 0.5 * t
    slope = half + (0.5 * z) * (1.0 - t * t) * (
        0.7978845608028654 + (3.0 * 0.7978845608028654 * 0.044715) * square
    )
    return z * half, slope


def gelu_value(z):
    t = jnp.tanh(z * (0.7978845608028654 + (0.7978845608028654 * 0.044715) * (z * z)))
    return z * (0.5 + 0.5 * t)


def causal_keep(rows, cols, first):
    r = lax.broadcasted_iota(jnp.int32, (rows, cols), 0) + first
    return lax.broadcasted_iota(jnp.int32, (rows, cols), 1) <= r


def attend_tile(q, k, v, first):
    s = dot(q, k, 1, 1) * (q.shape[1] ** -0.5)
    if first is not None:
        s = jnp.where(causal_keep(s.shape[0], s.shape[1], first), s, NEG)
    peak = jnp.max(s, axis=-1, keepdims=True)
    p = jnp.exp(s - peak)
    total = jnp.sum(p, axis=-1, keepdims=True)
    o = dot(p.astype(BF), v) / total
    return o.astype(BF), peak + jnp.log(total)


def attend_tile_back(q, k, v, do, o, lse, first):
    scale = q.shape[1] ** -0.5
    s = dot(q, k, 1, 1) * scale
    if first is not None:
        s = jnp.where(causal_keep(s.shape[0], s.shape[1], first), s, NEG)
    p = jnp.exp(s - lse)
    inner = jnp.sum(do.astype(F32) * o.astype(F32), axis=-1, keepdims=True)
    dp = dot(do, v, 1, 1)
    ds = (p * (dp - inner)).astype(BF)
    dq = dot(ds, k) * scale
    dk = dot(ds, q, 0, 0) * scale
    dv = dot(p.astype(BF), do, 0, 0)
    return dq, dk, dv


def params(mb=48):
    return pltpu.CompilerParams(vmem_limit_bytes=mb << 20)


SM = pl.BlockSpec(memory_space=pltpu.SMEM)
VM = pl.BlockSpec(memory_space=pltpu.VMEM)


def call(body, scal, ins, outs, scratch=(), flops=0, mb=48):
    shapes = [jax.ShapeDtypeStruct(s, d) for s, d in outs]
    moved = sum(a.size * a.dtype.itemsize for a in list(ins) + shapes)
    return pl.pallas_call(
        body,
        out_shape=shapes,
        in_specs=[SM] + [VM] * len(ins),
        out_specs=[VM] * len(outs),
        scratch_shapes=list(scratch),
        compiler_params=params(mb),
        cost_estimate=pl.CostEstimate(flops=flops, bytes_accessed=moved, transcendentals=0),
    )(scal, *ins)


def place_body(n, el, capp, scal, labels, out):
    me = scal[0]
    tokens = labels.shape[1]
    r = lax.broadcasted_iota(jnp.int32, (tokens, tokens), 0)
    c = lax.broadcasted_iota(jnp.int32, (tokens, tokens), 1)
    lower = (c < r).astype(BF)
    experts = n * el
    for m in range(labels.shape[0]):
        lab = labels[m]
        hot = lab == lax.broadcasted_iota(jnp.int32, (tokens, experts), 1)
        hot = jnp.where(hot, 1.0, 0.0)
        before = dot(lower, hot.astype(BF))
        slot = jnp.sum(before * hot, axis=1, keepdims=True).astype(jnp.int32)
        where = ((lab // el) ^ me) * (el * capp) + (lab % el) * capp + slot
        wide = jnp.where(
            where == lax.broadcasted_iota(jnp.int32, (tokens, n * el * capp), 1), 1.0, 0.0
        )
        out[m] = wide.T.astype(BF)


def send_slots(d_ref, rows, outs):
    size = outs[0].shape[0]
    for j, out in enumerate(outs):
        out[...] = dot(d_ref[j * size : (j + 1) * size, :], rows).astype(BF)


def self_fwd_body(n, hl, hs, scal, *refs):
    xs, (g, w), refs = refs[:n], refs[n : n + 2], refs[n + 2 :]
    a, qkv, o, lse = refs[:4]
    parts = refs[4:]
    me, dec = scal[0], scal[1]
    tokens = xs[0].shape[0]
    group = n * tokens
    hw = hl * hs
    for j in range(n):
        unit, _ = norm_parts(xs[j][...].astype(F32))
        a[pl.ds((me ^ j) * tokens, tokens), :] = (unit * g[...]).astype(BF)
    qkv[...] = dot(a[...], w[:, : 3 * hw]).astype(BF)

    def run(causal):
        lane = lax.broadcasted_iota(jnp.int32, (QB, 128), 1)
        for base in range(0, group, SEQ):
            for first in range(0, SEQ, QB):
                rows = slice(base + first, base + first + QB)
                keys = slice(base, base + (first + QB if causal else SEQ))
                stats = jnp.zeros((QB, 128), F32)
                for h in range(hl):
                    q = qkv[rows, h * hs : (h + 1) * hs]
                    k = qkv[keys, hw + h * hs : hw + (h + 1) * hs]
                    v = qkv[keys, 2 * hw + h * hs : 2 * hw + (h + 1) * hs]
                    out, logs = attend_tile(q, k, v, first if causal else None)
                    o[rows, h * hs : (h + 1) * hs] = out
                    stats = jnp.where(lane == h, logs, stats)
                lse[rows, :] = stats

    pl.when(dec == 1)(lambda: run(True))
    pl.when(dec == 0)(lambda: run(False))
    for j in range(n):
        rows = o[pl.ds((me ^ j) * tokens, tokens), :]
        parts[j][...] = dot(rows, w[:, 3 * hw :], 1, 1).astype(BF)


def self_bwd_body(n, hl, hs, scal, *refs):
    gs, refs = refs[:n], refs[n:]
    a, qkv, o, lse, g, w = refs[:6]
    parts, (dw, dgain), (dso, do, dqkv, acc) = refs[6 : 6 + n], refs[6 + n : 8 + n], refs[8 + n :]
    me, dec = scal[0], scal[1]
    tokens = gs[0].shape[0]
    group = n * tokens
    hw = hl * hs
    for j in range(n):
        dso[pl.ds((me ^ j) * tokens, tokens), :] = gs[j][...]
    do[...] = dot(dso[...], w[:, 3 * hw :]).astype(BF)

    def run(causal):
        for base in range(0, group, SEQ):
            for h in range(hl):
                acc[...] = jnp.zeros_like(acc)
                for first in range(0, SEQ, QB):
                    rows = slice(base + first, base + first + QB)
                    width = first + QB if causal else SEQ
                    keys = slice(base, base + width)
                    cols = slice(h * hs, (h + 1) * hs)
                    k = qkv[keys, hw + h * hs : hw + (h + 1) * hs]
                    v = qkv[keys, 2 * hw + h * hs : 2 * hw + (h + 1) * hs]
                    dq, dk, dv = attend_tile_back(
                        qkv[rows, cols],
                        k,
                        v,
                        do[rows, cols],
                        o[rows, cols],
                        lse[rows, h : h + 1],
                        first if causal else None,
                    )
                    dqkv[rows, cols] = dq.astype(BF)
                    acc[0, :width, :] += dk
                    acc[1, :width, :] += dv
                keys = slice(base, base + SEQ)
                dqkv[keys, hw + h * hs : hw + (h + 1) * hs] = acc[0].astype(BF)
                dqkv[keys, 2 * hw + h * hs : 2 * hw + (h + 1) * hs] = acc[1].astype(BF)

    pl.when(dec == 1)(lambda: run(True))
    pl.when(dec == 0)(lambda: run(False))
    total = jnp.zeros((1, a.shape[1]), F32)
    for j in range(n):
        rows = pl.ds((me ^ j) * tokens, tokens)
        da = dot(dqkv[rows, :], w[:, : 3 * hw], 1, 1)
        parts[j][...] = da.astype(BF)
        total += jnp.sum(da * a[rows, :].astype(F32), axis=0, keepdims=True)
    dgain[...] = total / g[...]
    dw[:, : 3 * hw] = dot(a[...], dqkv[...], 0, 0)
    dw[:, 3 * hw :] = dot(dso[...], o[...], 0, 0)


def after_self_body(n, pieces, scal, *refs):
    x, refs = refs[0], refs[1:]
    ps, (g2, d, cot), (h1,), outs = (
        refs[:pieces],
        refs[pieces : pieces + 3],
        refs[pieces + 3 : pieces + 4],
        refs[pieces + 4 :],
    )
    rows = x[...].astype(F32)
    for p in ps:
        rows = rows + p[...].astype(F32)
    h1[...] = rows
    unit, _ = norm_parts(rows)
    u = (unit * g2[...]).astype(BF)
    chosen = jnp.where(scal[1] == 0, u.astype(F32), cot[...].astype(F32)).astype(BF)
    send_slots(d, chosen, outs)


def memory_body(n, scal, *refs):
    rs, (h1, d, g1), (y, m) = refs[:n], refs[n : n + 3], refs[n + 3 :]

    @pl.when(scal[1] == 0)
    def _():
        stacked = jnp.concatenate([r[...] for r in rs], axis=0)
        rows = h1[...] + dot(d[...], stacked, 0, 0)
        y[...] = rows
        unit, _ = norm_parts(rows)
        m[...] = (unit * g1[...]).astype(BF)


def final_body(n, scal, *refs):
    rs, (h2, d, ye), (out,) = refs[:n], refs[n : n + 3], refs[n + 3 :]

    @pl.when(scal[1] == 0)
    def _():
        out[...] = ye[...].astype(BF)

    @pl.when(scal[1] == 1)
    def _():
        stacked = jnp.concatenate([r[...] for r in rs], axis=0)
        out[...] = (h2[...] + dot(d[...], stacked, 0, 0)).astype(BF)


def cross_fwd_body(n, per, hl, hs, scal, *refs):
    ms, wx, wkv = refs[:per], refs[per : per + n], refs[per + n : per + 2 * n]
    h1, g1, g2, d = refs[per + 2 * n : per + 2 * n + 4]
    refs = refs[per + 2 * n + 4 :]
    h2, c, mem, qc, kv, oc, lse = refs[:7]
    outs = refs[7:]
    hw = hl * hs
    tokens = h1.shape[0]

    @pl.when(scal[1] == 1)
    def _():
        for j in range(per):
            mem[j * tokens : (j + 1) * tokens, :] = ms[j][...]
        unit, _ = norm_parts(h1[...])
        c[...] = (unit * g1[...]).astype(BF)
        stats = jnp.zeros((tokens, 128), F32)
        lane = lax.broadcasted_iota(jnp.int32, (tokens, 128), 1)
        total = h1[...]
        for j in range(n):
            qc[:, j * hw : (j + 1) * hw] = dot(c[...], wx[j][:, :hw]).astype(BF)
            kv[:, 2 * j * hw : 2 * (j + 1) * hw] = dot(mem[...], wkv[j][...]).astype(BF)
            for h in range(hl):
                at = j * hw + h * hs
                k = kv[:, 2 * j * hw + h * hs : 2 * j * hw + (h + 1) * hs]
                v = kv[:, (2 * j + 1) * hw + h * hs : (2 * j + 1) * hw + (h + 1) * hs]
                out, logs = attend_tile(qc[:, at : at + hs], k, v, None)
                oc[:, at : at + hs] = out
                stats = jnp.where(lane == j * hl + h, logs, stats)
            total = total + dot(oc[:, j * hw : (j + 1) * hw], wx[j][:, hw:], 1, 1)
        lse[...] = stats
        h2[...] = total
        unit, _ = norm_parts(total)
        send_slots(d, (unit * g2[...]).astype(BF), outs)


def cross_bwd_body(n, per, hl, hs, scal, *refs):
    dus, wx, wkv = refs[:n], refs[n : 2 * n], refs[2 * n : 3 * n]
    h2, g2, d, cot, qc, kv, oc, lse = refs[3 * n : 3 * n + 8]
    refs = refs[3 * n + 8 :]
    dh2, dco, dqc, dkv, dgain = refs[:5]
    dms, (doc,) = refs[5 : 5 + per], refs[5 + per :]
    hw = hl * hs
    tokens = h2.shape[0]

    @pl.when(scal[1] == 0)
    def _():
        dgain[...] = jnp.zeros_like(dgain)

    @pl.when(scal[1] == 1)
    def _():
        stacked = jnp.concatenate([r[...] for r in dus], axis=0)
        unit, inverse = norm_parts(h2[...])
        back, gained = norm_back(dot(d[...], stacked, 0, 0), unit, inverse, g2[...])
        dgain[...] = gained
        total = cot[...].astype(F32) + back
        dh2[...] = total
        dco[...] = total.astype(BF)
        for j in range(n):
            doc[:, j * hw : (j + 1) * hw] = dot(dco[...], wx[j][:, hw:]).astype(BF)
            for h in range(hl):
                at = j * hw + h * hs
                k = slice(2 * j * hw + h * hs, 2 * j * hw + (h + 1) * hs)
                v = slice((2 * j + 1) * hw + h * hs, (2 * j + 1) * hw + (h + 1) * hs)
                dq, dk, dv = attend_tile_back(
                    qc[:, at : at + hs],
                    kv[:, k],
                    kv[:, v],
                    doc[:, at : at + hs],
                    oc[:, at : at + hs],
                    lse[:, j * hl + h : j * hl + h + 1],
                    None,
                )
                dqc[:, at : at + hs] = dq.astype(BF)
                dkv[:, k] = dk.astype(BF)
                dkv[:, v] = dv.astype(BF)
        for i in range(per):
            rows = slice(i * tokens, (i + 1) * tokens)
            total = 0.0
            for j in range(n):
                total += dot(dkv[rows, 2 * j * hw : 2 * (j + 1) * hw], wkv[j][...], 1, 1)
            dms[i][...] = total.astype(BF)


def cross_late_body(n, hl, hs, scal, *refs):
    wx = refs[:n]
    dh2, dco, dqc, dkv, oc, c, mem, h1, g1 = refs[n : n + 9]
    dh1, dwx, dwkv, dgain = refs[n + 9 :]
    hw = hl * hs

    @pl.when(scal[1] == 1)
    def _():
        dc = jnp.zeros(h1.shape, F32)
        for j in range(n):
            dc += dot(dqc[:, j * hw : (j + 1) * hw], wx[j][:, :hw], 1, 1)
        unit, inverse = norm_parts(h1[...])
        back, gained = norm_back(dc, unit, inverse, g1[...])
        dh1[...] = dh2[...] + back
        dgain[...] = gained
        dq = dot(c[...], dqc[...], 0, 0)
        de = dot(dco[...], oc[...], 0, 0)
        for j in range(n):
            dwx[j, :, :hw] = dq[:, j * hw : (j + 1) * hw]
            dwx[j, :, hw:] = de[:, j * hw : (j + 1) * hw]
        dk = dot(mem[...], dkv[...], 0, 0)
        for j in range(n):
            dwkv[j] = dk[:, 2 * j * hw : 2 * (j + 1) * hw]


def memory_back_body(n, pieces, scal, *refs):
    ps, (y, g1, cot, d), (dy, dgain), outs = (
        refs[:pieces],
        refs[pieces : pieces + 4],
        refs[pieces + 4 : pieces + 6],
        refs[pieces + 6 :],
    )

    @pl.when(scal[1] == 0)
    def _():
        dm = ps[0][...].astype(F32)
        for p in ps[1:]:
            dm = dm + p[...].astype(F32)
        unit, inverse = norm_parts(y[...])
        back, gained = norm_back(dm, unit, inverse, g1[...])
        dgain[...] = gained
        rows = cot[...].astype(F32) + back
        dy[...] = rows
        send_slots(d, rows.astype(BF), outs)


def before_self_body(n, scal, *refs):
    dus, (d, dy, h1, g2, given), (dh1, dso, dgain) = refs[:n], refs[n : n + 5], refs[n + 5 :]

    @pl.when(scal[1] == 0)
    def _():
        stacked = jnp.concatenate([r[...] for r in dus], axis=0)
        unit, inverse = norm_parts(h1[...])
        back, gained = norm_back(dot(d[...], stacked, 0, 0), unit, inverse, g2[...])
        rows = dy[...] + back
        dh1[...] = rows
        dso[...] = rows.astype(BF)
        dgain[...] = gained

    @pl.when(scal[1] == 1)
    def _():
        dh1[...] = given[...]
        dso[...] = given[...].astype(BF)
        dgain[...] = jnp.zeros_like(dgain)


def finish_body(pieces, scal, *refs):
    ps, (dh1, x, g0), (out,) = refs[:pieces], refs[pieces : pieces + 3], refs[pieces + 3 :]
    da = ps[0][...].astype(F32)
    for p in ps[1:]:
        da = da + p[...].astype(F32)
    unit, inverse = norm_parts(x[...].astype(F32))
    back, _ = norm_back(da, unit, inverse, g0[...])
    out[...] = dh1[...] + back


def expert_body(n, el, capp, steps, active, mode, scal, *refs):
    us, refs = refs[:n], refs[n:]
    drs = ()
    if mode != "fwd":
        drs, refs = refs[:n], refs[n:]
    (wi, wo), refs = refs[:2], refs[2:]
    rs, dus = (), ()
    if mode != "back":
        rs, refs = refs[:n], refs[n:]
    if mode != "fwd":
        dus, refs = refs[:n], refs[n:]
    scratch = list(refs)
    e, f = pl.program_id(0), pl.program_id(1)
    u = scratch.pop(0)
    dr = scratch.pop(0) if drs else None
    racc = scratch.pop(0) if rs else None
    dacc = scratch.pop(0) if dus else None

    @pl.when(scal[1] == active)
    def _():
        at = pl.ds(pl.multiple_of(e * capp, 16), capp)

        @pl.when(f == 0)
        def _():
            for j in range(n):
                u[j * capp : (j + 1) * capp, :] = us[j][at, :]
                if drs:
                    dr[j * capp : (j + 1) * capp, :] = drs[j][at, :]
            if rs:
                racc[...] = jnp.zeros_like(racc)
            if dus:
                dacc[...] = jnp.zeros_like(dacc)

        z = dot(u[...], wi[0])
        if not drs:
            g = gelu_value(z)
        else:
            g, slope = gelu_parts(z)
        if rs:
            racc[...] += dot(g.astype(BF), wo[0])
        if dus:
            dg = dot(dr[...], wo[0], 1, 1)
            dz = (dg * slope).astype(BF)
            dacc[...] += dot(dz, wi[0], 1, 1)

        @pl.when(f == steps - 1)
        def _():
            for j in range(n):
                if rs:
                    rs[j][at, :] = racc[j * capp : (j + 1) * capp, :].astype(BF)
                if dus:
                    dus[j][at, :] = dacc[j * capp : (j + 1) * capp, :].astype(BF)


def experts(scal, us, drs, w_in, w_out, capp, active, mode):
    n, el = len(us), w_in.shape[0]
    width, ff = w_in.shape[1:]
    block = 512
    steps = ff // block
    rows = n * capp
    whole = pl.BlockSpec((el * capp, width), lambda e, f, s: (0, 0))

    def on(s):
        return jnp.where(s[1] == active, 1, 0)

    outs = n * (2 if mode == "both" else 1)
    scratch = [pltpu.VMEM((rows, width), BF)] * (1 if mode == "fwd" else 2)
    scratch += [pltpu.VMEM((rows, width), F32)] * (2 if mode == "both" else 1)
    products = {"fwd": 2, "both": 4, "back": 3}[mode]
    result = pl.pallas_call(
        functools.partial(expert_body, n, el, capp, steps, active, mode),
        grid_spec=pltpu.PrefetchScalarGridSpec(
            num_scalar_prefetch=1,
            grid=(el, steps),
            in_specs=[whole] * (len(us) + len(drs))
            + [
                pl.BlockSpec((1, width, block), lambda e, f, s: (e * on(s), 0, f * on(s))),
                pl.BlockSpec((1, block, width), lambda e, f, s: (e * on(s), f * on(s), 0)),
            ],
            out_specs=[whole] * outs,
            scratch_shapes=scratch,
        ),
        out_shape=[jax.ShapeDtypeStruct((el * capp, width), BF)] * outs,
        compiler_params=params(),
        cost_estimate=pl.CostEstimate(
            flops=products * 2 * el * rows * width * ff,
            bytes_accessed=2 * 2 * el * width * ff,
            transcendentals=0,
        ),
    )(scal, *us, *drs, w_in, w_out)
    return [result[i : i + n] for i in range(0, outs, n)]


def expert_grad_body(micro, chunk, *refs):
    us, drs, (wi, wo), (dwi, dwo) = (
        refs[:micro],
        refs[micro : 2 * micro],
        refs[2 * micro : 2 * micro + 2],
        refs[2 * micro + 2 :],
    )
    lead, _, capp, width = us[0].shape
    first = True
    for m in range(micro):
        for at in range(0, lead, chunk):
            u = us[m][at : at + chunk, 0].reshape(chunk * capp, width)
            dr = drs[m][at : at + chunk, 0].reshape(chunk * capp, width)
            z = dot(u, wi[0])
            g, slope = gelu_parts(z)
            dz = (dot(dr, wo[0], 1, 1) * slope).astype(BF)
            di = dot(u, dz, 0, 0)
            do = dot(g.astype(BF), dr, 0, 0)
            if first:
                dwi[0] = di
                dwo[0] = do
            else:
                dwi[0] += di
                dwo[0] += do
            first = False


def expert_grads(us, drs, w_in, w_out):
    micro = len(us)
    lead, el, capp, width = us[0].shape
    ff = w_in.shape[2]
    block = 256
    chunk = min(lead, max(1, 768 // capp))
    while lead % chunk:
        chunk -= 1
    rows = pl.BlockSpec((lead, 1, capp, width), lambda e, f: (0, e, 0, 0))
    into = pl.BlockSpec((1, width, block), lambda e, f: (e, 0, f))
    back = pl.BlockSpec((1, block, width), lambda e, f: (e, f, 0))
    return pl.pallas_call(
        functools.partial(expert_grad_body, micro, chunk),
        grid=(el, ff // block),
        in_specs=[rows] * (2 * micro) + [into, back],
        out_specs=[into, back],
        out_shape=[jax.ShapeDtypeStruct(w_in.shape, F32), jax.ShapeDtypeStruct(w_out.shape, F32)],
        compiler_params=params(),
        cost_estimate=pl.CostEstimate(
            flops=8 * micro * lead * el * capp * width * ff,
            bytes_accessed=6 * 2 * el * width * ff,
            transcendentals=0,
        ),
    )(*us, *drs, w_in, w_out)


def on_device(inputs, cotangent, expert_ids, self_proj, cross_proj, gains, w_in, w_out):
    micro, tokens, width = inputs.shape[1:]
    n = lax.axis_size("mp")
    dps = lax.axis_size("dp")
    hl = self_proj.shape[2]
    hs = self_proj.shape[3] // 4
    hw = hl * hs
    el = w_in.shape[1]
    capacity = max(2, 3 * tokens // (2 * n * el))
    capp = -(-capacity // 16) * 16
    slots = el * capp
    per = SEQ // tokens
    group = n * tokens
    me = lax.axis_index("mp")
    decoder = lax.axis_index("section") == 1
    scal = jnp.stack([me, lax.axis_index("section")]).astype(jnp.int32)
    first_weight, second_weight = w_in[0], w_out[0]
    gain = [gains[0, i : i + 1] for i in range(3)]
    ENC, DEC, ALL = (0,), (1,), (0, 1)

    def swap(x, k, sections=ALL):
        pairs = [(s * n + i, s * n + (i ^ k)) for s in sections for i in range(n)]
        return lax.ppermute(x, ("section", "mp"), pairs)

    def gather(x, count, sections=ALL):
        blocks = {0: x}
        bit = count // 2
        while bit:
            blocks.update({j ^ bit: swap(b, bit, sections) for j, b in list(blocks.items())})
            bit //= 2
        return [blocks[j] for j in range(count)]

    def scatter(blocks, sections=ALL):
        live = {j: [b] for j, b in enumerate(blocks)}
        bit = 1
        while bit < len(blocks):
            for j in [j for j in live if j & bit]:
                pieces = live.pop(j)
                out = pieces[0]
                if len(pieces) > 1:
                    out = sum(p.astype(F32) for p in pieces).astype(BF)
                live[j ^ bit].append(swap(out, bit, sections))
            bit *= 2
        return live[0]

    def exchange(blocks, sections=ALL):
        return [blocks[0]] + [swap(blocks[j], j, sections) for j in range(1, n)]

    def to_decoder(x):
        return lax.ppermute(x, "section", [(0, 1)])

    def to_encoder(x):
        return lax.ppermute(x, "section", [(1, 0)])

    xs = [inputs[0, m] for m in range(micro)]
    cots = [cotangent[0, m] for m in range(micro)]
    ws = self_proj[0].reshape(width, hl, 4, hs).transpose(0, 2, 1, 3).reshape(width, 4 * hw)
    wc = cross_proj[0].reshape(width, hl, 2, hs).transpose(0, 2, 1, 3).reshape(width, 2 * hw)
    routes = call(
        functools.partial(place_body, n, el, capp),
        scal,
        [expert_ids[0]],
        [((micro, n * slots, tokens), BF)],
    )[0]
    routes = [routes[m] for m in range(micro)]
    M = range(micro)

    row, wide = ((tokens, width), BF), ((tokens, width), F32)
    x_all = [gather(xs[m], n) for m in M]
    saved, self_parts = [], []
    for m in M:
        res = call(
            functools.partial(self_fwd_body, n, hl, hs),
            scal,
            [*x_all[m], gain[0], ws],
            [((group, width), BF), ((group, 3 * hw), BF), ((group, hw), BF), ((group, 128), F32)]
            + [row] * n,
            flops=2 * group * width * 4 * hw + 4 * 4 * group * SEQ * hw,
        )
        saved.append(res[:4])
        self_parts.append(scatter(res[4:]))
    h1, first_slots = [], []
    for m in M:
        res = call(
            functools.partial(after_self_body, n, len(self_parts[m])),
            scal,
            [xs[m], *self_parts[m], gain[2], routes[m], cots[m]],
            [wide] + [((slots, width), BF)] * n,
            flops=2 * n * slots * tokens * width,
        )
        h1.append(res[0])
        first_slots.append(exchange(res[1:]))

    wx_all = gather(wc, n, DEC)
    wkv_all = gather(to_decoder(wc), n, DEC)
    ye, mem_all = [], []
    for m in M:
        (r,) = experts(scal, first_slots[m], (), first_weight, second_weight, capp, 0, "fwd")
        r = exchange(r, ENC)
        y, mem = call(
            functools.partial(memory_body, n),
            scal,
            [*r, h1[m], routes[m], gain[1]],
            [wide, row],
            flops=2 * n * slots * tokens * width,
        )
        ye.append(y)
        mem_all.append(gather(to_decoder(mem), per, DEC))

    crossed, second_slots = [], []
    for m in M:
        res = call(
            functools.partial(cross_fwd_body, n, per, hl, hs),
            scal,
            [*mem_all[m], *wx_all, *wkv_all, h1[m], gain[1], gain[2], routes[m]],
            [
                wide,
                row,
                ((SEQ, width), BF),
                ((tokens, n * hw), BF),
                ((SEQ, 2 * n * hw), BF),
                ((tokens, n * hw), BF),
                ((tokens, 128), F32),
            ]
            + [((slots, width), BF)] * n,
            flops=4 * SEQ * width * n * hw + 4 * 4 * tokens * SEQ * n * hw,
        )
        crossed.append(res[:7])
        second_slots.append(exchange(res[7:], DEC))

    outs, dus = [], []
    for m in M:
        r, du = experts(
            scal, second_slots[m], first_slots[m], first_weight, second_weight, capp, 1, "both"
        )
        dus.append(exchange(du, DEC))
        r = exchange(r, DEC)
        outs.append(
            call(
                functools.partial(final_body, n),
                scal,
                [*r, crossed[m][0], routes[m], ye[m]],
                [row],
            )[0]
        )

    dms, late, gain_parts = [], [], [[], [], []]
    for m in M:
        h2, c, mem, qc, kv, oc, lse = crossed[m]
        res = call(
            functools.partial(cross_bwd_body, n, per, hl, hs),
            scal,
            [*dus[m], *wx_all, *wkv_all, h2, gain[2], routes[m], cots[m], qc, kv, oc, lse],
            [
                wide,
                row,
                ((tokens, n * hw), BF),
                ((SEQ, 2 * n * hw), BF),
                ((1, width), F32),
            ]
            + [row] * per,
            scratch=[pltpu.VMEM((tokens, n * hw), BF)],
            flops=4 * SEQ * width * n * hw + 4 * 10 * tokens * SEQ * n * hw,
        )
        dh2, dco, dqc, dkv, gained = res[:5]
        gain_parts[2].append(gained)
        pieces = scatter(res[5:], DEC)
        dms.append(to_encoder(sum(p.astype(F32) for p in pieces).astype(BF)))
        late.append(
            call(
                functools.partial(cross_late_body, n, hl, hs),
                scal,
                [*wx_all, dh2, dco, dqc, dkv, oc, c, mem, h1[m], gain[1]],
                [
                    wide,
                    ((n, width, 2 * hw), F32),
                    ((n, width, 2 * hw), F32),
                    ((1, width), F32),
                ],
                flops=8 * SEQ * width * n * hw,
            )
        )

    dys, third_slots, memory_gain = [], [], []
    for m in M:
        res = call(
            functools.partial(memory_back_body, n, 1),
            scal,
            [dms[m], ye[m], gain[1], cots[m], routes[m]],
            [wide, ((1, width), F32)] + [((slots, width), BF)] * n,
        )
        dys.append(res[0])
        memory_gain.append(res[1])
        third_slots.append(exchange(res[2:], ENC))
    dh1, dso = [], []
    for m in M:
        (du,) = experts(
            scal, first_slots[m], third_slots[m], first_weight, second_weight, capp, 0, "back"
        )
        du = exchange(du, ENC)
        res = call(
            functools.partial(before_self_body, n),
            scal,
            [*du, routes[m], dys[m], h1[m], gain[2], late[m][0]],
            [wide, row, ((1, width), F32)],
        )
        dh1.append(res[0])
        dso.append(gather(res[1], n))
        gain_parts[2].append(res[2])

    def rows_of(blocks):
        whole = jnp.stack(blocks).reshape(n, el, capp, width)
        return lax.all_gather(whole, "dp", axis=0, tiled=True)

    u_rows = [
        rows_of([jnp.where(decoder, b, a) for a, b in zip(first_slots[m], second_slots[m])])
        for m in M
    ]
    dr_rows = [
        rows_of([jnp.where(decoder, b, a) for a, b in zip(third_slots[m], first_slots[m])])
        for m in M
    ]

    input_grads, self_grads = [], []
    for m in M:
        a, qkv, o, lse = saved[m]
        res = call(
            functools.partial(self_bwd_body, n, hl, hs),
            scal,
            [*dso[m], a, qkv, o, lse, gain[0], ws],
            [row] * n + [((width, 4 * hw), F32), ((1, width), F32)],
            scratch=[
                pltpu.VMEM((group, width), BF),
                pltpu.VMEM((group, hw), BF),
                pltpu.VMEM((group, 3 * hw), BF),
                pltpu.VMEM((2, SEQ, hs), F32),
            ],
            flops=2 * group * width * 8 * hw + 4 * 10 * group * SEQ * hw,
        )
        pieces = scatter(res[:n])
        self_grads.append(res[n])
        gain_parts[0].append(res[n + 1])
        input_grads.append(
            call(
                functools.partial(finish_body, len(pieces)),
                scal,
                [*pieces, dh1[m], xs[m], gain[0]],
                [wide],
            )[0]
        )

    def small_sum(x):
        for axis in ("mp", "dp"):
            count = lax.axis_size(axis)
            bit = 1
            while bit < count:
                x = x + lax.ppermute(x, axis, [(i, i ^ bit) for i in range(count)])
                bit *= 2
        return x

    gain_parts[1] = [jnp.where(decoder, late[m][3], memory_gain[m]) for m in M]
    gain_total = small_sum(jnp.concatenate([sum(p) for p in gain_parts], axis=0))

    self_total = sum(self_grads).astype(BF)
    self_total = lax.psum(self_total, "dp").astype(F32)
    dwx = sum(late[m][1] for m in M).astype(BF)
    dwkv = sum(late[m][2] for m in M).astype(BF)
    dwx = sum(p.astype(F32) for p in scatter([dwx[j] for j in range(n)], DEC)).astype(BF)
    dwkv = sum(p.astype(F32) for p in scatter([dwkv[j] for j in range(n)], DEC)).astype(BF)
    cross_total = jnp.where(decoder, dwx, to_encoder(dwkv))
    cross_total = lax.psum(cross_total, "dp").astype(F32)

    first_total, second_total = expert_grads(u_rows, dr_rows, first_weight, second_weight)

    self_total = self_total.reshape(width, 4, hl, hs).transpose(0, 2, 1, 3)
    cross_total = cross_total.reshape(width, 2, hl, hs).transpose(0, 2, 1, 3)
    return (
        jnp.stack(outs)[None],
        jnp.stack(input_grads)[None],
        self_total.reshape(1, width, hl, 4 * hs),
        cross_total.reshape(1, width, hl, 2 * hs),
        gain_total[None],
        first_total[None],
        second_total[None],
    )


def solution(mesh):
    rows = P("section", None, ("dp", "mp"), None)
    heads = P("section", None, "mp", None)
    expert = P("section", "mp", None, None)
    return jax.shard_map(
        on_device,
        mesh=mesh,
        in_specs=(rows, rows, rows, heads, heads, P("section", None, None), expert, expert),
        out_specs=(rows, rows, heads, heads, P("section", None, None), expert, expert),
        check_vma=False,
    )
```

```python
import functools

import jax
import jax.numpy as jnp
from jax import lax
from jax.experimental import pallas as pl
from jax.experimental.pallas import tpu as pltpu
from jax.sharding import PartitionSpec as P

SEQ = 1024
EPS = 1e-05
ROOT = 0.7978845608028654
NEG = -1000000000.0
BF = jnp.bfloat16
F32 = jnp.float32
QB = 256


def dot(a, b, ca=1, cb=0):
    return lax.dot_general(a, b, (((ca,), (cb,)), ((), ())), preferred_element_type=F32)


def norm_parts(rows):
    centred = rows - jnp.mean(rows, axis=-1, keepdims=True)
    inverse = lax.rsqrt(jnp.mean(centred * centred, axis=-1, keepdims=True) + EPS)
    return centred * inverse, inverse


def norm_back(upstream, unit, inverse, gain):
    scaled = upstream * gain
    inner = (
        scaled
        - jnp.mean(scaled, axis=-1, keepdims=True)
        - unit * jnp.mean(scaled * unit, axis=-1, keepdims=True)
    )
    return inverse * inner, jnp.sum(upstream * unit, axis=0, keepdims=True)


def gelu_parts(z):
    square = z * z
    t = jnp.tanh(z * (0.7978845608028654 + (0.7978845608028654 * 0.044715) * square))
    half = 0.5 + 0.5 * t
    slope = half + (0.5 * z) * (1.0 - t * t) * (
        0.7978845608028654 + (3.0 * 0.7978845608028654 * 0.044715) * square
    )
    return z * half, slope


def gelu_value(z):
    t = jnp.tanh(z * (0.7978845608028654 + (0.7978845608028654 * 0.044715) * (z * z)))
    return z * (0.5 + 0.5 * t)


LOG2E = 1.4426950408889634


def attend_tile(q, k, v, first):
    s = dot(q, k, 1, 1) * (q.shape[1] ** -0.5 * LOG2E)
    if first is not None:
        r = lax.broadcasted_iota(jnp.int32, s.shape, 0) + first
        s = jnp.where(lax.broadcasted_iota(jnp.int32, s.shape, 1) <= r, s, NEG)
    peak = jnp.max(s, axis=-1, keepdims=True)
    p = jnp.exp2(s - peak)
    total = jnp.sum(p, axis=-1, keepdims=True)
    o = dot(p.astype(BF), v) / total
    return o.astype(BF), peak + jnp.log2(total)


def attend_tile_back(q, k, v, do, lse, inner, first):
    s = dot(k, q, 1, 1) * (q.shape[1] ** -0.5 * LOG2E)
    if first is not None:
        c = lax.broadcasted_iota(jnp.int32, s.shape, 1) + first
        s = jnp.where(lax.broadcasted_iota(jnp.int32, s.shape, 0) <= c, s, NEG)
    p = jnp.exp2(s - lse)
    ds = (p * (dot(v, do, 1, 1) - inner)).astype(BF)
    return p.astype(BF), ds


def by_lane(columns):
    lane = lax.broadcasted_iota(jnp.int32, (columns[0].shape[0], 128), 1)
    wide = jnp.zeros((columns[0].shape[0], 128), F32)
    for i, column in enumerate(columns):
        wide = jnp.where(lane == i, column, wide)
    return wide


def row_products(a, b):
    return jnp.sum(a.astype(F32) * b.astype(F32), axis=-1, keepdims=True)


SM = pl.BlockSpec(memory_space=pltpu.SMEM)
VM = pl.BlockSpec(memory_space=pltpu.VMEM)
HB = pl.BlockSpec(memory_space=pltpu.HBM)
ANY = pl.BlockSpec(memory_space=pl.ANY)


class Far:
    def __init__(self, array, *index, later=False):
        self.array, self.index, self.later = array, index, later
        self.shape, self.dtype = array.shape[len(index) :], array.dtype


class Raw:
    def __init__(self, array):
        self.array, self.shape, self.dtype = array, array.shape, array.dtype


class Arriving:
    def __init__(self, ref, index, buffer, sem):
        source = ref.at[index] if index else ref
        self.copy, self.buffer, self.waited = (
            pltpu.make_async_copy(source, buffer, sem),
            buffer,
            False,
        )
        self.shape = buffer.shape
        self.started = False

    def start(self):
        if not self.started:
            self.copy.start()
            self.started = True

    def ready(self):
        self.start()
        if not self.waited:
            self.copy.wait()
            self.waited = True
        return self.buffer

    def __getitem__(self, at):
        return self.ready()[at]


class Leaving:
    def __init__(self, ref, buffer, sem):
        self.copy, self.buffer, self.sent = pltpu.make_async_copy(buffer, ref, sem), buffer, False
        self.shape, self.dtype = buffer.shape, buffer.dtype

    def send(self):
        if not self.sent:
            self.copy.start()
            self.sent = True

    def __getitem__(self, at):
        return self.buffer[at]

    def __setitem__(self, at, value):
        self.buffer[at] = value


def ready_all(*refs):
    for ref in refs:
        if isinstance(ref, Arriving):
            ref.ready()


def start_all(*refs):
    for ref in refs:
        if isinstance(ref, Arriving):
            ref.start()


def pinned(array):
    return pltpu.with_memory_space_constraint(array, pltpu.HBM)


def stays(array):
    return array.shape == (8, 128) or array.ndim > 2


def nbytes(shape, dtype):
    size = jnp.dtype(dtype).itemsize
    for x in shape[:-1]:
        size *= x
    return size * (-(-shape[-1] // 128) * 128)


def call(body, scal, ins, outs, scratch=(), flops=0, extra=13, after=(), active=None):
    far_in = [k for k, x in enumerate(ins) if isinstance(x, Far)]
    far_out = [k for k, x in enumerate(outs) if len(x) > 2 and x[2]]
    shapes = [
        jax.ShapeDtypeStruct(*x) if len(x) == 2 else pltpu.HBM(*x[:2]) if x[2] else pltpu.VMEM(*x[:2])
        for x in outs
    ]
    shapes.append(pltpu.HBM((8, 128), F32))
    buffers = [pltpu.VMEM(ins[k].shape, ins[k].dtype) for k in far_in]
    buffers += [pltpu.VMEM(outs[k][0], outs[k][1]) for k in far_out]
    sems = [pltpu.SemaphoreType.DMA(())] * len(buffers)
    count, waits = 1 + len(ins), len(after)
    held = sum(nbytes(b.shape, b.dtype) for b in buffers + list(scratch) if "sem" not in str(b.dtype))
    moved = sum(nbytes(a.shape, a.dtype) for a in list(ins) + shapes)

    def whole(*refs):
        scal, in_refs = refs[0], list(refs[1:count])
        rest = refs[count + waits :]
        out_refs, rest = list(rest[: len(outs)]), rest[len(outs) + 1 :]
        own, rest = rest[: len(scratch)], rest[len(scratch) :]
        space, signals = rest[: len(buffers)], rest[len(buffers) :]

        def run():
            arrivals, departures = [], []
            for at, k in enumerate(far_in):
                in_refs[k] = Arriving(in_refs[k], ins[k].index, space[at], signals[at])
                arrivals.append(in_refs[k])
                if not ins[k].later:
                    in_refs[k].start()
            for at, k in enumerate(far_out, len(far_in)):
                out_refs[k] = Leaving(out_refs[k], space[at], signals[at])
                departures.append(out_refs[k])
            body(scal, *in_refs, *out_refs, *own)
            for a in arrivals:
                a.ready()
            for d in departures:
                d.send()
            for d in departures:
                d.copy.wait()

        if active is None:
            run()
        else:
            pl.when(scal[1] == active)(run)

    specs = [HB if isinstance(x, (Far, Raw)) else VM for x in ins]
    arrays = [pinned(x.array) if isinstance(x, (Far, Raw)) else x for x in ins]
    after = [pinned(a) if stays(a) else a for a in after]
    return pl.pallas_call(
        whole,
        out_shape=shapes,
        in_specs=[SM] + specs + [HB if stays(a) else VM for a in after],
        out_specs=[HB if len(x) > 2 and x[2] else VM for x in outs] + [HB],
        scratch_shapes=list(scratch) + buffers + sems,
        compiler_params=pltpu.CompilerParams(vmem_limit_bytes=held + (extra << 20)),
        cost_estimate=pl.CostEstimate(flops=flops, bytes_accessed=moved, transcendentals=0),
        name=getattr(body, "func", body).__name__,
    )(scal, *arrays, *after)


def place_body(n, el, capp, scal, labels, *outs):
    me = scal[0]
    tokens = labels.shape[1]
    r = lax.broadcasted_iota(jnp.int32, (tokens, tokens), 0)
    c = lax.broadcasted_iota(jnp.int32, (tokens, tokens), 1)
    lower = (c < r).astype(BF)
    experts = n * el
    for m in range(labels.shape[0]):
        lab = labels[m]
        hot = lab == lax.broadcasted_iota(jnp.int32, (tokens, experts), 1)
        hot = jnp.where(hot, 1.0, 0.0)
        before = dot(lower, hot.astype(BF))
        slot = jnp.sum(before * hot, axis=1, keepdims=True).astype(jnp.int32)
        where = ((lab // el) ^ me) * (el * capp) + (lab % el) * capp + slot
        wide = jnp.where(
            where == lax.broadcasted_iota(jnp.int32, (tokens, n * el * capp), 1), 1.0, 0.0
        )
        outs[m][...] = wide.T.astype(BF)


def send_slots(d_ref, rows, outs):
    size = outs[0].shape[0]
    for j, out in enumerate(outs):
        out[...] = dot(d_ref[j * size : (j + 1) * size, :], rows).astype(BF)


def self_fwd_body(n, hl, hs, scal, *refs):
    xs, (gains, w), refs = refs[:n], refs[n : n + 2], refs[n + 2 :]
    a, qkv, o, lse = refs[:4]
    parts = refs[4:]
    me, dec = scal[0], scal[1]
    tokens = xs[0].shape[0]
    group = n * tokens
    hw = hl * hs
    g = gains[0, 0:1]
    for j in range(n):
        unit, _ = norm_parts(xs[j][...].astype(F32))
        a[pl.ds((me ^ j) * tokens, tokens), :] = (unit * g).astype(BF)
    a.send()
    qkv[...] = dot(a[...], w[:, : 3 * hw]).astype(BF)
    qkv.send()

    def run(causal):
        for base in range(0, group, SEQ):
            logs = {}
            for h in range(hl):
                cols = slice(h * hs, (h + 1) * hs)
                k = qkv[base : base + SEQ, hw + h * hs : hw + (h + 1) * hs]
                v = qkv[base : base + SEQ, 2 * hw + h * hs : 2 * hw + (h + 1) * hs]
                for first in range(0, SEQ, QB):
                    rows = slice(base + first, base + first + QB)
                    width = first + QB if causal else SEQ
                    o[rows, cols], logs[first, h] = attend_tile(
                        qkv[rows, cols], k[:width], v[:width], first if causal else None
                    )
            for first in range(0, SEQ, QB):
                lse[base + first : base + first + QB, :] = by_lane(
                    [logs[first, h] for h in range(hl)]
                )

    pl.when(dec == 1)(lambda: run(True))
    pl.when(dec == 0)(lambda: run(False))
    for j in range(n):
        rows = o[pl.ds((me ^ j) * tokens, tokens), :]
        parts[j][...] = dot(rows, w[:, 3 * hw :], 1, 1).astype(BF)


def self_bwd_body(n, hl, hs, add, scal, *refs):
    gs, refs = refs[:n], refs[n:]
    a, qkv, o, lse, gains, w = refs[:6]
    olds, refs = refs[6 : 6 + add], [*refs[:6], *refs[6 + add :]]
    parts, (dw, dgain) = refs[6 : 6 + n], refs[6 + n : 8 + n]
    dso, do, dqkv, ps, dss = refs[8 + n :]
    me, dec = scal[0], scal[1]
    tokens = gs[0].shape[0]
    group = n * tokens
    hw = hl * hs
    scale = hs**-0.5
    for j in range(n):
        dso[pl.ds((me ^ j) * tokens, tokens), :] = gs[j][...]
    do[...] = dot(dso[...], w[:, 3 * hw :]).astype(BF)
    ready_all(o, lse, qkv)
    start_all(a, *olds)

    def run(causal):
        for base in range(0, group, SEQ):
            keys = slice(base, base + SEQ)
            rows_of = [slice(base + f, base + f + QB) for f in range(0, SEQ, QB)]
            logs = [lse[rows, :].T for rows in rows_of]
            inners = [
                by_lane(
                    [
                        row_products(
                            do[rows, h * hs : (h + 1) * hs], o[rows, h * hs : (h + 1) * hs]
                        )
                        for h in range(hl)
                    ]
                ).T
                for rows in rows_of
            ]
            dqs = []
            for h in range(hl):
                cols = slice(h * hs, (h + 1) * hs)
                q, dh = qkv[keys, cols], do[keys, cols]
                k = qkv[keys, hw + h * hs : hw + (h + 1) * hs]
                v = qkv[keys, 2 * hw + h * hs : 2 * hw + (h + 1) * hs]
                for i, first in enumerate(range(0, SEQ, QB)):
                    width = first + QB if causal else SEQ
                    block = slice(first, first + QB)
                    p, ds = attend_tile_back(
                        q[block],
                        k[:width],
                        v[:width],
                        dh[block],
                        logs[i][h : h + 1],
                        inners[i][h : h + 1],
                        first if causal else None,
                    )
                    ps[:width, block] = p
                    dss[:width, block] = ds
                kt = (k.astype(F32) * scale).astype(BF).T
                if causal:
                    dk = [dot(dss[f : f + QB, f:], q[f:]) for f in range(0, SEQ, QB)]
                    dv = [dot(ps[f : f + QB, f:], dh[f:]) for f in range(0, SEQ, QB)]
                    dk, dv = jnp.concatenate(dk, axis=0), jnp.concatenate(dv, axis=0)
                    dq = [
                        dot(kt[:, : f + QB], dss[: f + QB, f : f + QB]) for f in range(0, SEQ, QB)
                    ]
                    dqs.append(jnp.concatenate(dq, axis=1))
                else:
                    dk, dv = dot(dss[...], q), dot(ps[...], dh)
                    dqs.append(dot(kt, dss[...]))
                dqkv[keys, hw + h * hs : hw + (h + 1) * hs] = (dk * scale).astype(BF)
                dqkv[keys, 2 * hw + h * hs : 2 * hw + (h + 1) * hs] = dv.astype(BF)
            dqkv[keys, :hw] = jnp.concatenate(dqs, axis=0).T.astype(BF)

    pl.when(dec == 1)(lambda: run(True))
    pl.when(dec == 0)(lambda: run(False))
    total = jnp.zeros((1, a.shape[1]), F32)
    for j in range(n):
        rows = pl.ds((me ^ j) * tokens, tokens)
        da = dot(dqkv[rows, :], w[:, : 3 * hw], 1, 1)
        parts[j][...] = da.astype(BF)
        total += jnp.sum(da * a[rows, :].astype(F32), axis=0, keepdims=True)
    dgain[...] = total / gains[0, 0:1]
    grads = dot(a[...], dqkv[...], 0, 0), dot(dso[...], o[...], 0, 0)
    for h in range(hl):
        for t in range(4):
            at = (t % 3) * hw + h * hs
            to = slice((4 * h + t) * hs, (4 * h + t + 1) * hs)
            part = grads[0][:, at : at + hs] if t < 3 else grads[1][:, h * hs : (h + 1) * hs]
            dw[:, to] = ((part + olds[0][:, to]) if add else part).astype(dw.dtype)


def after_self_body(n, pieces, scal, *refs):
    x, refs = refs[0], refs[1:]
    ps, (gains, d, cot), (h1,), outs = (
        refs[:pieces],
        refs[pieces : pieces + 3],
        refs[pieces + 3 : pieces + 4],
        refs[pieces + 4 :],
    )
    rows = x[...].astype(F32)
    for p in ps:
        rows = rows + p[...].astype(F32)
    h1[...] = rows
    h1.send()
    unit, _ = norm_parts(rows)
    u = (unit * gains[0, 2:3]).astype(BF)
    chosen = jnp.where(scal[1] == 0, u.astype(F32), cot[...].astype(F32)).astype(BF)
    send_slots(d, chosen, outs)


def memory_body(n, scal, *refs):
    rs, (h1, d, gains), (y, m) = refs[:n], refs[n : n + 3], refs[n + 3 :]
    stacked = jnp.concatenate([r[...] for r in rs], axis=0)
    rows = h1[...] + dot(d[...], stacked, 0, 0)
    y[...] = rows
    y.send()
    unit, _ = norm_parts(rows)
    m[...] = (unit * gains[0, 1:2]).astype(BF)


def final_body(n, micro, scal, *refs):
    out = refs[-1]
    for m in range(micro):
        rs, (h2, d, ye) = refs[:n], refs[n : n + 3]
        refs = refs[n + 3 :]
        ready_all(h2, d, ye)

        @pl.when(scal[1] == 0)
        def _():
            out[0, m] = ye[...].astype(BF)

        @pl.when(scal[1] == 1)
        def _():
            stacked = jnp.concatenate([r[...] for r in rs], axis=0)
            out[0, m] = (h2[...] + dot(d[...], stacked, 0, 0)).astype(BF)


def cross_fwd_body(n, per, hl, hs, scal, *refs):
    ms, refs = refs[:per], refs[per:]
    wx, wkv, (h1, gains, d), refs = refs[:n], refs[n : 2 * n], refs[2 * n : 2 * n + 3], refs[2 * n + 3 :]
    h2, c, mem, qc, kv, oc, lse = refs[:7]
    outs = refs[7:]
    hw = hl * hs
    tokens = h1.shape[0]
    for j in range(per):
        mem[j * tokens : (j + 1) * tokens, :] = ms[j][...]
    mem.send()
    unit, _ = norm_parts(h1[...])
    start_all(*wkv)
    c[...] = (unit * gains[0, 1:2]).astype(BF)
    c.send()
    for j in range(n):
        qc[:, j * hw : (j + 1) * hw] = dot(c[...], wx[j][:, :hw]).astype(BF)
    qc.send()
    for j in range(n):
        kv[:, 2 * j * hw : 2 * (j + 1) * hw] = dot(mem[...], wkv[j][...]).astype(BF)
    kv.send()
    total = h1[...]
    logs = []
    for j in range(n):
        for h in range(hl):
            at = j * hw + h * hs
            k = kv[:, 2 * j * hw + h * hs : 2 * j * hw + (h + 1) * hs]
            v = kv[:, (2 * j + 1) * hw + h * hs : (2 * j + 1) * hw + (h + 1) * hs]
            oc[:, at : at + hs], log = attend_tile(qc[:, at : at + hs], k, v, None)
            logs.append(log)
        total = total + dot(oc[:, j * hw : (j + 1) * hw], wx[j][:, hw:], 1, 1)
    oc.send()
    lse[...] = by_lane(logs)
    lse.send()
    h2[...] = total
    h2.send()
    unit, _ = norm_parts(total)
    send_slots(d, (unit * gains[0, 2:3]).astype(BF), outs)


def cross_bwd_body(n, per, hl, hs, scal, *refs):
    dus, wx, wkv, refs = refs[:n], refs[n : 2 * n], refs[2 * n : 3 * n], refs[3 * n :]
    h2, gains, d, cot, qc, kv, oc, lse = refs[:8]
    refs = refs[8:]
    dh2, dco, dqc, dkv, dgain = refs[:5]
    dms, (doc,) = refs[5 : 5 + per], refs[5 + per :]
    hw = hl * hs
    tokens = h2.shape[0]
    stacked = jnp.concatenate([r[...] for r in dus], axis=0)
    unit, inverse = norm_parts(h2[...])
    start_all(*wx, oc, lse, qc, kv, *wkv)
    back, gained = norm_back(dot(d[...], stacked, 0, 0), unit, inverse, gains[0, 2:3])
    dgain[...] = gained
    total = cot[...].astype(F32) + back
    dh2[...] = total
    dh2.send()
    dco[...] = total.astype(BF)
    dco.send()
    for j in range(n):
        doc[:, j * hw : (j + 1) * hw] = dot(dco[...], wx[j][:, hw:]).astype(BF)
    logs = lse[...].T
    places = [slice(i * hs, (i + 1) * hs) for i in range(n * hl)]
    inner = by_lane([row_products(doc[:, at], oc[:, at]) for at in places]).T
    scale = hs**-0.5
    dqs = []
    for i, at in enumerate(places):
        j, h = i // hl, i % hl
        k_at = slice(2 * j * hw + h * hs, 2 * j * hw + (h + 1) * hs)
        v_at = slice((2 * j + 1) * hw + h * hs, (2 * j + 1) * hw + (h + 1) * hs)
        q, k, do = qc[:, at], kv[:, k_at], doc[:, at]
        p, ds = attend_tile_back(q, k, kv[:, v_at], do, logs[i : i + 1], inner[i : i + 1], None)
        dkv[:, k_at] = (dot(ds, q) * scale).astype(BF)
        dkv[:, v_at] = dot(p, do).astype(BF)
        dqs.append(dot((k.astype(F32) * scale).astype(BF).T, ds))
    dkv.send()
    dqc[...] = jnp.concatenate(dqs, axis=0).T.astype(BF)
    dqc.send()
    for i in range(per):
        rows = slice(i * tokens, (i + 1) * tokens)
        total = 0.0
        for j in range(n):
            total += dot(dkv[rows, 2 * j * hw : 2 * (j + 1) * hw], wkv[j][...], 1, 1)
        dms[i][...] = total.astype(BF)


def cross_late_body(n, hl, hs, scal, *refs):
    wx, (dh2, dco, dqc, dkv, oc, c, mem, h1, gains) = refs[:n], refs[n : n + 9]
    dh1, dwx, dwkv, dgain = refs[n + 9 :]
    hw = hl * hs
    dc = jnp.zeros(h1.shape, F32)
    for j in range(n):
        dc += dot(dqc[:, j * hw : (j + 1) * hw], wx[j][:, :hw], 1, 1)
    unit, inverse = norm_parts(h1[...])
    back, gained = norm_back(dc, unit, inverse, gains[0, 1:2])
    dh1[...] = dh2[...] + back
    dh1.send()
    dgain[...] = gained
    ct, dt, mt = c[...].T, dco[...].T, mem[...].T
    for j in range(n):
        dq = dot(ct, dqc[:, j * hw : (j + 1) * hw])
        de = dot(dt, oc[:, j * hw : (j + 1) * hw])
        dkv_j = dot(mt, dkv[:, 2 * j * hw : 2 * (j + 1) * hw])
        for h in range(hl):
            at, to = slice(h * hs, (h + 1) * hs), 2 * h * hs
            dwx[j, :, to : to + hs] = dq[:, at].astype(BF)
            dwx[j, :, to + hs : to + 2 * hs] = de[:, at].astype(BF)
            dwkv[j, :, to : to + hs] = dkv_j[:, at].astype(BF)
            dwkv[j, :, to + hs : to + 2 * hs] = dkv_j[:, hw + h * hs : hw + (h + 1) * hs].astype(BF)


def memory_back_body(n, scal, *refs):
    (dm, y, gains, cot, d), (dy, dgain), outs = refs[:5], refs[5:7], refs[7:]
    unit, inverse = norm_parts(y[...])
    back, gained = norm_back(dm[...].astype(F32), unit, inverse, gains[0, 1:2])
    dgain[...] = gained
    rows = cot[...].astype(F32) + back
    dy[...] = rows
    dy.send()
    send_slots(d, rows.astype(BF), outs)


def before_self_body(n, scal, *refs):
    dus, (d, dy, h1, gains, given), (dh1, dso, dgain) = refs[:n], refs[n : n + 5], refs[n + 5 :]
    ready_all(gains, h1, d, dy, given)

    @pl.when(scal[1] == 0)
    def _():
        stacked = jnp.concatenate([r[...] for r in dus], axis=0)
        unit, inverse = norm_parts(h1[...])
        back, gained = norm_back(dot(d[...], stacked, 0, 0), unit, inverse, gains[0, 2:3])
        rows = dy[...] + back
        dh1[...] = rows
        dso[...] = rows.astype(BF)
        dgain[...] = gained

    @pl.when(scal[1] == 1)
    def _():
        dh1[...] = given[...]
        dso[...] = given[...].astype(BF)
        dgain[...] = jnp.zeros(dgain.shape, F32)


def finish_body(pieces, scal, *refs):
    ps, (dh1, x, gains, out) = refs[:pieces], refs[pieces:]
    da = ps[0][...].astype(F32)
    for p in ps[1:]:
        da = da + p[...].astype(F32)
    unit, inverse = norm_parts(x[...].astype(F32))
    back, _ = norm_back(da, unit, inverse, gains[0, 0:1])
    out[...] = dh1[...] + back


def gelu_low(z):
    z = z.astype(BF)

    def c(value):
        return jnp.asarray(value, BF)

    inner = c(ROOT) + c(ROOT * 0.044715) * (z * z)
    half = c(0.5) + c(0.5) * jnp.tanh(z * inner)
    value = z * half
    return value, half + (value - value * half) * (c(6.0) * inner - c(4.0 * ROOT))


def expert_body(n, el, capp, block, mode, scal, *refs):
    us, refs = refs[:n], refs[n:]
    drs = ()
    if mode != "fwd":
        drs, refs = refs[:n], refs[n:]
    (wi_far, wo_far), refs = refs[:2], refs[2:]
    rs, dus = (), ()
    if mode != "back":
        rs, refs = refs[:n], refs[n:]
    if mode != "fwd":
        dus, refs = refs[:n], refs[n:]
    u_all = dr_all = None
    if mode != "back":
        u_all, refs = refs[0], refs[1:]
    if mode != "fwd":
        dr_all, refs = refs[0], refs[1:]
    wi, wo, sems = refs
    steps = wi.shape[2] // block
    copies = []
    for e in range(el):
        for f in range(steps):
            part = slice(f * block, (f + 1) * block)
            sem = e * steps + f
            copies.append(
                (
                    pltpu.make_async_copy(
                        wi_far.at[0, e, :, part], wi.at[e, :, part], sems.at[0, sem]
                    ),
                    pltpu.make_async_copy(
                        wo_far.at[0, e, part, :], wo.at[e, part, :], sems.at[1, sem]
                    ),
                )
            )

    def fetch(k):
        if k < len(copies):
            for copy in copies[k]:
                copy.start()

    fetch(0)
    fetch(1)
    rows_u = [
        jnp.concatenate([us[j][e * capp : (e + 1) * capp, :] for j in range(n)], axis=0)
        for e in range(el)
    ]
    rows_dr = [
        jnp.concatenate([drs[j][e * capp : (e + 1) * capp, :] for j in range(n)], axis=0)
        for e in range(el if drs else 0)
    ]
    for e in range(el):
        if u_all is not None:
            u_all[e] = rows_u[e]
        if dr_all is not None:
            dr_all[e] = rows_dr[e]
    for ref in (u_all, dr_all):
        if ref is not None:
            ref.send()
    for e in range(el):
        racc = dacc = 0.0
        for f in range(steps):
            for copy in copies[e * steps + f]:
                copy.wait()
            fetch(e * steps + f + 2)
            part = slice(f * block, (f + 1) * block)
            wi_f, wo_f = wi[e, :, part], wo[e, part, :]
            z = dot(rows_u[e], wi_f)
            if drs:
                g, slope = gelu_parts(z)
            else:
                g = gelu_value(z)
            if rs:
                racc += dot(g.astype(BF), wo_f)
            if dus:
                dz = (dot(rows_dr[e], wo_f, 1, 1) * slope).astype(BF)
                dacc += dot(dz, wi_f, 1, 1)
        for j in range(n):
            part, at = slice(j * capp, (j + 1) * capp), slice(e * capp, (e + 1) * capp)
            if rs:
                rs[j][at, :] = racc[part].astype(BF)
            if dus:
                dus[j][at, :] = dacc[part].astype(BF)


def experts(step, us, drs, w_in, w_out, capp, active, mode):
    n, el = len(us), w_in.shape[1]
    width, ff = w_in.shape[2:]
    block = 512
    outs = n * (2 if mode == "both" else 1)
    products = {"fwd": 2, "both": 4, "back": 3}[mode]
    result = step(
        functools.partial(expert_body, n, el, capp, block, mode),
        [*us, *drs, Raw(w_in), Raw(w_out)],
        [((el * capp, width), BF)] * outs
        + [((el, n * capp, width), BF, True)] * (2 if mode == "both" else 1),
        scratch=[
            pltpu.VMEM(w_in.shape[1:], BF),
            pltpu.VMEM(w_out.shape[1:], BF),
            pltpu.SemaphoreType.DMA((2, el * ff // block)),
        ],
        flops=products * 2 * el * n * capp * width * ff,
        active=active,
    )
    return [result[i : i + n] for i in range(0, outs, n)], result[outs:]


def expert_grad_body(add, *refs):
    u_ref, dr_ref, wi, wo = refs[:4]
    refs = refs[4:]
    olds, refs = (refs[:2], refs[2:]) if add else ((), refs)
    dwi, dwo, ut = refs[-3:]
    lead, _, rows, width = u_ref.shape
    chunk = 1
    while 2 * chunk * rows <= 1024 and lead % (2 * chunk) == 0:
        chunk *= 2
    size = chunk * rows

    @pl.when(pl.program_id(1) == 0)
    def _():
        for at in range(0, lead, chunk):
            u = u_ref[at : at + chunk, 0].reshape(size, width)
            ut[:, at * rows : at * rows + size] = u.T

    for at in range(0, lead, chunk):
        u = u_ref[at : at + chunk, 0].reshape(size, width)
        dr = dr_ref[at : at + chunk, 0].reshape(size, width)
        g, slope = gelu_low(dot(u, wi[0, 0]))
        dz = dot(dr, wo[0, 0], 1, 1).astype(BF) * slope
        di = dot(ut[:, at * rows : at * rows + size], dz)
        do = dot(g, dr, 0, 0)
        if at:
            dwi[0, 0] += di
            dwo[0, 0] += do
        elif add:
            dwi[0, 0] = olds[0][0, 0] + di
            dwo[0, 0] = olds[1][0, 0] + do
        else:
            dwi[0, 0] = di
            dwo[0, 0] = do


def expert_grads(u, dr, w_in, w_out, olds, after):
    lead, el, rows, width = u.shape
    ff = w_in.shape[3]
    block = 512
    spec = pl.BlockSpec((lead, 1, rows, width), lambda e, f: (0, e, 0, 0))
    into = pl.BlockSpec((1, 1, width, block), lambda e, f: (0, e, 0, f))
    back = pl.BlockSpec((1, 1, block, width), lambda e, f: (0, e, f, 0))
    body = functools.partial(expert_grad_body, bool(olds))
    u, dr, w_in, w_out, *olds = [pinned(x) for x in (u, dr, w_in, w_out, *olds)]
    after = [pinned(a) if stays(a) else a for a in after]
    count = 4 + len(olds)

    def trimmed(*refs):
        ins, rest = refs[:count], refs[count + len(after) :]
        dwi, dwo, _, ut = rest
        body(*ins, dwi, dwo, ut)

    return pl.pallas_call(
        trimmed,
        grid=(el, ff // block),
        in_specs=[spec] * 2
        + [into, back]
        + [into, back][: len(olds)]
        + [HB if stays(a) else VM for a in after],
        out_specs=[into, back, HB],
        out_shape=[
            pltpu.HBM(w_in.shape, F32),
            pltpu.HBM(w_out.shape, F32),
            pltpu.HBM((8, 128), F32),
        ],
        scratch_shapes=[pltpu.VMEM((width, lead * rows), BF)],
        input_output_aliases={4: 0, 5: 1} if olds else {},
        compiler_params=pltpu.CompilerParams(
            vmem_limit_bytes=(22 << 20) + 10 * lead * rows * width
        ),
        cost_estimate=pl.CostEstimate(
            flops=8 * lead * el * rows * width * ff,
            bytes_accessed=6 * 2 * el * width * ff,
            transcendentals=0,
        ),
        name="expert_grads",
    )(u, dr, w_in, w_out, *olds, *after)


def on_device(inputs, cotangent, expert_ids, self_proj, cross_proj, gains, w_in, w_out):
    micro, tokens, width = inputs.shape[1:]
    n = lax.axis_size("mp")
    hl = self_proj.shape[2]
    hs = self_proj.shape[3] // 4
    hw = hl * hs
    el = w_in.shape[1]
    capacity = max(2, 3 * tokens // (2 * n * el))
    capp = -(-capacity // 16) * 16
    slots = el * capp
    per = SEQ // tokens
    group = n * tokens
    M = range(micro)
    decoder = lax.axis_index("section") == 1
    scal = jnp.stack([lax.axis_index("mp"), lax.axis_index("section")]).astype(jnp.int32)
    last = []

    def step(body, ins, outs, **more):
        *res, token = call(body, scal, ins, outs, after=list(last), **more)
        last[:] = [token]
        return res

    def swap(x, k, sections=(0, 1)):
        pairs = [(s * n + i, s * n + (i ^ k)) for s in sections for i in range(n)]
        return lax.ppermute(x, ("section", "mp"), pairs)

    def gather(x, count, sections=(0, 1), gated=False):
        blocks = {0: x}
        bit = count // 2
        while bit:
            blocks.update({j ^ bit: swap(b, bit, sections) for j, b in list(blocks.items())})
            if gated and bit == count // 2:
                (blocks[bit],) = gate([blocks[bit]])
            bit //= 2
        return [blocks[j] for j in range(count)]

    def scatter(blocks, hold=False):
        live = {j: [b] for j, b in enumerate(blocks)}
        bit = 1
        while bit < len(blocks):
            for j in [j for j in live if j & bit]:
                pieces = live.pop(j)
                out = pieces[0]
                if len(pieces) > 1:
                    out = sum(p.astype(F32) for p in pieces).astype(BF)
                    if hold:
                        last.append(out)
                live[j ^ bit].append(swap(out, bit))
            bit *= 2
        return live[0]

    def exchange(blocks):
        return [blocks[0]] + [swap(blocks[j], j) for j in range(1, n)]

    def gate(arrays):
        count = len(arrays)
        waits = list(last)
        *arrays, token = pl.pallas_call(
            lambda *refs: None,
            out_shape=[jax.ShapeDtypeStruct(a.shape, a.dtype) for a in arrays]
            + [pltpu.HBM((8, 128), F32)],
            in_specs=[ANY] * count + [HB if stays(a) else VM for a in waits],
            out_specs=[ANY] * count + [HB],
            input_output_aliases={i: i for i in range(count)},
            name="gate",
        )(*arrays, *[pinned(a) if stays(a) else a for a in waits])
        last[:] = [token]
        return arrays

    def lazy(fars):
        return [Far(f.array, *f.index, later=True) for f in fars]

    def to_decoder(x):
        return lax.ppermute(x, "section", [(0, 1)])

    def to_encoder(x):
        return lax.ppermute(x, "section", [(1, 0)])

    xs = [inputs[0, m] for m in M]
    ws = self_proj[0].reshape(width, hl, 4, hs).transpose(0, 2, 1, 3).reshape(width, 4 * hw)
    wc = cross_proj[0].reshape(width, hl, 2, hs).transpose(0, 2, 1, 3).reshape(width, 2 * hw)
    row, wide, line = ((tokens, width), BF), ((tokens, width), F32, True), ((1, width), F32, True)
    slot = ((slots, width), BF)

    def far(shape, dtype=BF):
        return (shape, dtype, True)

    last.extend([ws, wc])
    routes = step(
        functools.partial(place_body, n, el, capp),
        [expert_ids[0]],
        [far((n * slots, tokens))] * micro,
    )
    routes = [Far(r) for r in routes]
    gain = Far(gains)
    x_far = [Far(inputs, 0, m) for m in M]
    cots = [Far(cotangent, 0, m) for m in M]

    x_all = [gather(xs[m], n, gated=m == 0) for m in M]
    saved, self_parts = [], []
    for m in M:
        res = step(
            functools.partial(self_fwd_body, n, hl, hs),
            [*x_all[m], gain, Far(ws)],
            [
                far((group, width)),
                far((group, 3 * hw)),
                far((group, hw)),
                far((group, 128), F32),
            ]
            + [row] * n,
            flops=2 * group * width * 4 * hw + 4 * 4 * group * SEQ * hw,
        )
        saved.append(res[:4])
        parts = res[4:]
        if m:
            last.extend(self_parts[-1])
            parts = gate(parts)
        self_parts.append(scatter(parts, m < micro - 1))
    h1, first_slots = [], []
    for m in M:
        res = step(
            functools.partial(after_self_body, n, len(self_parts[m])),
            [x_far[m], *self_parts[m], gain, routes[m], cots[m]],
            [wide] + [slot] * n,
            flops=2 * n * slots * tokens * width,
        )
        h1.append(Far(res[0]))
        first_slots.append(exchange(res[1:]))

    wx_all = [Far(b) for b in gather(wc, n, (1,))]
    wkv_all = [Far(b, later=True) for b in gather(to_decoder(wc), n, (1,))]
    ye, mem_all, rs, enc_u = [], [], [], []
    for m in M:
        (r,), (u,) = experts(
            step, first_slots[m], (), w_in, w_out, capp, 0, "fwd"
        )
        rs.append(exchange(r))
        enc_u.append(u)
    for m in M:
        y, mem = step(
            functools.partial(memory_body, n),
            [*rs[m], h1[m], routes[m], gain],
            [wide, row],
            flops=2 * n * slots * tokens * width,
            active=0,
        )
        ye.append(Far(y))
        mem_all.append(gather(to_decoder(mem), per))

    crossed, second_slots = [], []
    for m in M:
        res = step(
            functools.partial(cross_fwd_body, n, per, hl, hs),
            [*mem_all[m], *wx_all, *wkv_all, h1[m], gain, routes[m]],
            [
                wide,
                far((tokens, width)),
                far((SEQ, width)),
                far((tokens, n * hw)),
                far((SEQ, 2 * n * hw)),
                far((tokens, n * hw)),
                far((tokens, 128), F32),
            ]
            + [slot] * n,
            flops=4 * SEQ * width * n * hw + 4 * 4 * tokens * SEQ * n * hw,
            active=1,
        )
        crossed.append([Far(r) for r in res[:7]])
        second_slots.append(exchange(res[7:]))

    rs, dus, dec_u, dec_dr = [], [], [], []
    for m in M:
        (r, du), (u, dr) = experts(
            step,
            second_slots[m],
            [Far(b) for b in first_slots[m]],
            w_in,
            w_out,
            capp,
            1,
            "both",
        )
        dus.append(exchange(du))
        rs.append(r)
        dec_u.append(u)
        dec_dr.append(dr)

    late, gain_parts, kept, pieces = [], [[], [], []], [], []
    for m in M:
        h2, c, mem, qc, kv, oc, lse = crossed[m]
        res = step(
            functools.partial(cross_bwd_body, n, per, hl, hs),
            [*dus[m], *lazy(wx_all), *wkv_all, h2, gain, routes[m], cots[m]]
            + lazy((qc, kv, oc, lse)),
            [wide, far((tokens, width)), far((tokens, n * hw)), far((SEQ, 2 * n * hw)), line]
            + [row] * per,
            scratch=[pltpu.VMEM((tokens, n * hw), BF)],
            flops=4 * SEQ * width * n * hw + 4 * 10 * tokens * SEQ * n * hw,
            active=1,
        )
        kept.append([Far(r) for r in res[:4]])
        gain_parts[2].append(jnp.where(decoder, res[4], 0.0))
        parts = res[5:]
        if m:
            last.extend(pieces[-1])
            parts = gate(parts)
        pieces.append(scatter(parts, m < micro - 1))
    dms = [to_encoder(sum(p.astype(F32) for p in pieces[m]).astype(BF)) for m in M]

    def rows_of(encoder_rows, decoder_rows):
        whole = jnp.where(decoder, decoder_rows, encoder_rows)[None]
        return lax.all_gather(whole, "dp", axis=0, tiled=True)

    u_rows = [rows_of(enc_u[m], dec_u[m]) for m in M]

    memory_gain, dr_rows, dh1, dso, parts_a, self_total = [], [], [], [], [], None

    def experts_back(m):
        res = step(
            functools.partial(memory_back_body, n),
            [dms[m], ye[m], gain, cots[m], routes[m]],
            [wide, line] + [slot] * n,
            active=0,
        )
        memory_gain.append(res[1])
        third = exchange(res[2:])
        (du,), (dr,) = experts(
            step,
            [Far(b) for b in first_slots[m]],
            third,
            w_in,
            w_out,
            capp,
            0,
            "back",
        )
        dr_rows.append(rows_of(dr, dec_dr[m]))
        return res[0], exchange(du)

    def cross_late(m):
        h2, c, mem, qc, kv, oc, lse = crossed[m]
        late.append(
            step(
                functools.partial(cross_late_body, n, hl, hs),
                [*wx_all, *kept[m], oc, c, mem, h1[m], gain],
                [wide, far((n, width, 2 * hw)), far((n, width, 2 * hw)), line],
                flops=8 * SEQ * width * n * hw,
                active=1,
            )
        )

    def before_self(m, dy, du):
        res = step(
            functools.partial(before_self_body, n),
            [*du, routes[m], Far(dy), h1[m], gain, Far(late[m][0])],
            [wide, row, line],
        )
        dh1.append(res[0])
        dso.append(gather(res[1], n))
        gain_parts[2].append(res[2])

    def self_back(m, before):
        a, qkv, o, lse = saved[m]
        res = step(
            functools.partial(self_bwd_body, n, hl, hs, bool(before)),
            [*dso[m], Far(a, later=True)]
            + [Far(x) for x in (qkv, o, lse)]
            + [gain, Far(ws)]
            + [Far(x, later=True) for x in before],
            [row] * n + [far((width, 4 * hw), BF if m == micro - 1 else F32), line],
            scratch=[
                pltpu.VMEM((group, width), BF),
                pltpu.VMEM((group, hw), BF),
                pltpu.VMEM((group, 3 * hw), BF),
                pltpu.VMEM((SEQ, SEQ), BF),
                pltpu.VMEM((SEQ, SEQ), BF),
            ],
            flops=2 * group * width * 8 * hw + 4 * 10 * group * SEQ * hw,
        )
        parts_a.append(scatter(res[:n], m < micro - 1))
        gain_parts[0].append(res[n + 1])
        return [res[n]]

    grads = []
    for m in M:
        dy, du = experts_back(m)
        if m:
            grads = self_back(m - 1, grads)
        cross_late(m)
        before_self(m, dy, du)
    rs = [exchange(r) for r in rs]
    (outs,) = step(
        functools.partial(final_body, n, micro),
        [x for m in M for x in (*rs[m], crossed[m][0], routes[m], ye[m])],
        [((1, micro, tokens, width), BF, True)],
    )
    grads = self_back(micro - 1, grads)

    totals, input_grads = (), []
    for m in M:
        input_grads.append(
            step(
                functools.partial(finish_body, len(parts_a[m])),
                [*parts_a[m], Far(dh1[m]), x_far[m], gain],
                [((tokens, width), F32)],
            )[0]
        )
        *totals, token = expert_grads(u_rows[m], dr_rows[m], w_in, w_out, totals, list(last))
        last[:] = [token]
        if m == 0:
            last.extend(dr_rows)
            grads = gate(grads)
    first_total, second_total = totals

    def small_sum(x):
        for axis in ("mp", "dp"):
            count = lax.axis_size(axis)
            bit = 1
            while bit < count:
                x = x + lax.ppermute(x, axis, [(i, i ^ bit) for i in range(count)])
                bit *= 2
        return x

    gain_parts[1] = [jnp.where(decoder, late[m][3], memory_gain[m]) for m in M]
    gain_total = small_sum(jnp.concatenate([sum(p) for p in gain_parts], axis=0))

    def total_of(parts):
        parts = [sum(p[j].astype(F32) for p in parts).astype(BF) for j in range(n)]
        return sum(p.astype(F32) for p in scatter(parts)).astype(BF)

    (self_total,) = grads
    cross_total = jnp.where(
        decoder,
        total_of([late[m][1] for m in M]),
        to_encoder(total_of([late[m][2] for m in M])),
    )
    self_total = self_total.reshape(width, hl, 4 * hs)
    cross_total = cross_total.reshape(width, hl, 2 * hs)
    self_total, cross_total = lax.psum((self_total, cross_total), "dp")
    return (
        outs,
        jnp.stack(input_grads)[None],
        self_total.astype(F32)[None],
        cross_total.astype(F32)[None],
        gain_total[None],
        first_total,
        second_total,
    )


def solution(mesh):
    rows = P("section", None, ("dp", "mp"), None)
    heads = P("section", None, "mp", None)
    expert = P("section", "mp", None, None)
    return jax.shard_map(
        on_device,
        mesh=mesh,
        in_specs=(rows, rows, rows, heads, heads, P("section", None, None), expert, expert),
        out_specs=(rows, rows, heads, heads, P("section", None, None), expert, expert),
        check_vma=False,
    )
```

```python
import functools

import jax
import jax.numpy as jnp
from jax import lax
from jax.experimental import pallas as pl
from jax.experimental.pallas import tpu as pltpu
from jax.sharding import PartitionSpec as P

SEQ = 1024
EPS = 1e-05
ROOT = 0.7978845608028654
NEG = -1000000000.0
BF = jnp.bfloat16
F32 = jnp.float32
QB = 256


def dot(a, b, ca=1, cb=0):
    return lax.dot_general(a, b, (((ca,), (cb,)), ((), ())), preferred_element_type=F32)


def norm_parts(rows):
    centred = rows - jnp.mean(rows, axis=-1, keepdims=True)
    inverse = lax.rsqrt(jnp.mean(centred * centred, axis=-1, keepdims=True) + EPS)
    return centred * inverse, inverse


def norm_back(upstream, unit, inverse, gain):
    scaled = upstream * gain
    inner = (
        scaled
        - jnp.mean(scaled, axis=-1, keepdims=True)
        - unit * jnp.mean(scaled * unit, axis=-1, keepdims=True)
    )
    return inverse * inner, jnp.sum(upstream * unit, axis=0, keepdims=True)


def gelu_parts(z):
    square = z * z
    t = jnp.tanh(z * (0.7978845608028654 + (0.7978845608028654 * 0.044715) * square))
    half = 0.5 + 0.5 * t
    slope = half + (0.5 * z) * (1.0 - t * t) * (
        0.7978845608028654 + (3.0 * 0.7978845608028654 * 0.044715) * square
    )
    return z * half, slope


def gelu_value(z):
    t = jnp.tanh(z * (0.7978845608028654 + (0.7978845608028654 * 0.044715) * (z * z)))
    return z * (0.5 + 0.5 * t)


LOG2E = 1.4426950408889634


def attend_tile(q, k, v, first):
    s = dot(q, k, 1, 1) * (q.shape[1] ** -0.5 * LOG2E)
    if first is not None:
        r = lax.broadcasted_iota(jnp.int32, s.shape, 0) + first
        s = jnp.where(lax.broadcasted_iota(jnp.int32, s.shape, 1) <= r, s, NEG)
    peak = jnp.max(s, axis=-1, keepdims=True)
    p = jnp.exp2(s - peak)
    total = jnp.sum(p, axis=-1, keepdims=True)
    o = dot(p.astype(BF), v) / total
    return o.astype(BF), peak + jnp.log2(total)


def attend_tile_back(q, k, v, do, lse, inner, first):
    s = dot(k, q, 1, 1) * (q.shape[1] ** -0.5 * LOG2E)
    if first is not None:
        c = lax.broadcasted_iota(jnp.int32, s.shape, 1) + first
        s = jnp.where(lax.broadcasted_iota(jnp.int32, s.shape, 0) <= c, s, NEG)
    p = jnp.exp2(s - lse)
    ds = (p * (dot(v, do, 1, 1) - inner)).astype(BF)
    return p.astype(BF), ds


def by_lane(columns):
    lane = lax.broadcasted_iota(jnp.int32, (columns[0].shape[0], 128), 1)
    wide = jnp.zeros((columns[0].shape[0], 128), F32)
    for i, column in enumerate(columns):
        wide = jnp.where(lane == i, column, wide)
    return wide


def row_products(a, b):
    return jnp.sum(a.astype(F32) * b.astype(F32), axis=-1, keepdims=True)


SM = pl.BlockSpec(memory_space=pltpu.SMEM)
VM = pl.BlockSpec(memory_space=pltpu.VMEM)
HB = pl.BlockSpec(memory_space=pltpu.HBM)
ANY = pl.BlockSpec(memory_space=pl.ANY)


class Far:
    def __init__(self, array, *index, later=False):
        self.array, self.index, self.later = array, index, later
        self.shape, self.dtype = array.shape[len(index) :], array.dtype


class Raw:
    def __init__(self, array):
        self.array, self.shape, self.dtype = array, array.shape, array.dtype


class Arriving:
    def __init__(self, ref, index, buffer, sem):
        source = ref.at[index] if index else ref
        self.copy, self.buffer, self.waited = (
            pltpu.make_async_copy(source, buffer, sem),
            buffer,
            False,
        )
        self.shape = buffer.shape
        self.started = False

    def start(self):
        if not self.started:
            self.copy.start()
            self.started = True

    def ready(self):
        self.start()
        if not self.waited:
            self.copy.wait()
            self.waited = True
        return self.buffer

    def __getitem__(self, at):
        return self.ready()[at]


class Leaving:
    def __init__(self, ref, buffer, sem):
        self.copy, self.buffer, self.sent = pltpu.make_async_copy(buffer, ref, sem), buffer, False
        self.shape, self.dtype = buffer.shape, buffer.dtype

    def send(self):
        if not self.sent:
            self.copy.start()
            self.sent = True

    def __getitem__(self, at):
        return self.buffer[at]

    def __setitem__(self, at, value):
        self.buffer[at] = value


def ready_all(*refs):
    for ref in refs:
        if isinstance(ref, Arriving):
            ref.ready()


def start_all(*refs):
    for ref in refs:
        if isinstance(ref, Arriving):
            ref.start()


def pinned(array):
    return pltpu.with_memory_space_constraint(array, pltpu.HBM)


def stays(array):
    return array.shape == (8, 128) or array.ndim > 2


def nbytes(shape, dtype):
    size = jnp.dtype(dtype).itemsize
    for x in shape[:-1]:
        size *= x
    return size * (-(-shape[-1] // 128) * 128)


def call(body, scal, ins, outs, scratch=(), flops=0, extra=13, after=(), active=None):
    far_in = [k for k, x in enumerate(ins) if isinstance(x, Far)]
    far_out = [k for k, x in enumerate(outs) if len(x) > 2 and x[2]]
    shapes = [
        jax.ShapeDtypeStruct(*x) if len(x) == 2 else pltpu.HBM(*x[:2]) if x[2] else pltpu.VMEM(*x[:2])
        for x in outs
    ]
    shapes.append(pltpu.HBM((8, 128), F32))
    buffers = [pltpu.VMEM(ins[k].shape, ins[k].dtype) for k in far_in]
    buffers += [pltpu.VMEM(outs[k][0], outs[k][1]) for k in far_out]
    sems = [pltpu.SemaphoreType.DMA(())] * len(buffers)
    count, waits = 1 + len(ins), len(after)
    held = sum(nbytes(b.shape, b.dtype) for b in buffers + list(scratch) if "sem" not in str(b.dtype))
    moved = sum(nbytes(a.shape, a.dtype) for a in list(ins) + shapes)

    def whole(*refs):
        scal, in_refs = refs[0], list(refs[1:count])
        rest = refs[count + waits :]
        out_refs, rest = list(rest[: len(outs)]), rest[len(outs) + 1 :]
        own, rest = rest[: len(scratch)], rest[len(scratch) :]
        space, signals = rest[: len(buffers)], rest[len(buffers) :]

        def run():
            arrivals, departures = [], []
            for at, k in enumerate(far_in):
                in_refs[k] = Arriving(in_refs[k], ins[k].index, space[at], signals[at])
                arrivals.append(in_refs[k])
                if not ins[k].later:
                    in_refs[k].start()
            for at, k in enumerate(far_out, len(far_in)):
                out_refs[k] = Leaving(out_refs[k], space[at], signals[at])
                departures.append(out_refs[k])
            body(scal, *in_refs, *out_refs, *own)
            for a in arrivals:
                a.ready()
            for d in departures:
                d.send()
            for d in departures:
                d.copy.wait()

        if active is None:
            run()
        else:
            pl.when(scal[1] == active)(run)

    specs = [HB if isinstance(x, (Far, Raw)) else VM for x in ins]
    arrays = [pinned(x.array) if isinstance(x, (Far, Raw)) else x for x in ins]
    return pl.pallas_call(
        whole,
        out_shape=shapes,
        in_specs=[SM] + specs + [HB if stays(a) else ANY for a in after],
        out_specs=[HB if len(x) > 2 and x[2] else VM for x in outs] + [HB],
        scratch_shapes=list(scratch) + buffers + sems,
        compiler_params=pltpu.CompilerParams(vmem_limit_bytes=held + (extra << 20)),
        cost_estimate=pl.CostEstimate(flops=flops, bytes_accessed=moved, transcendentals=0),
        name=getattr(body, "func", body).__name__,
    )(scal, *arrays, *[pinned(a) if stays(a) else a for a in after])


def gains_body(micro, scal, *refs):
    out = refs[-1]
    ready_all(*refs[:-1])
    first, refs = refs[:micro], refs[micro : -1]
    out[0:1] = sum(r[...] for r in first)
    for section in (0, 1):

        @pl.when(scal[1] == section)
        def _():
            mine = refs[2 * micro * section : 2 * micro * (section + 1)]
            out[1:2] = sum(r[...] for r in mine[:micro])
            out[2:3] = sum(r[...] for r in mine[micro:])


def place_body(n, el, capp, scal, labels, *outs):
    me = scal[0]
    tokens = labels.shape[1]
    r = lax.broadcasted_iota(jnp.int32, (tokens, tokens), 0)
    c = lax.broadcasted_iota(jnp.int32, (tokens, tokens), 1)
    lower = (c < r).astype(BF)
    experts = n * el
    for m in range(labels.shape[0]):
        lab = labels[m]
        hot = lab == lax.broadcasted_iota(jnp.int32, (tokens, experts), 1)
        hot = jnp.where(hot, 1.0, 0.0)
        before = dot(lower, hot.astype(BF))
        slot = jnp.sum(before * hot, axis=1, keepdims=True).astype(jnp.int32)
        where = ((lab // el) ^ me) * (el * capp) + (lab % el) * capp + slot
        wide = jnp.where(
            where == lax.broadcasted_iota(jnp.int32, (tokens, n * el * capp), 1), 1.0, 0.0
        )
        outs[m][...] = wide.T.astype(BF)


def send_slots(d_ref, rows, outs):
    size = outs[0].shape[0]
    for j, out in enumerate(outs):
        out[...] = dot(d_ref[j * size : (j + 1) * size, :], rows).astype(BF)


def self_fwd_body(n, hl, hs, scal, *refs):
    xs, (gains, w), refs = refs[:n], refs[n : n + 2], refs[n + 2 :]
    a, qkv, o, lse = refs[:4]
    parts = refs[4:]
    me, dec = scal[0], scal[1]
    tokens = xs[0].shape[0]
    group = n * tokens
    hw = hl * hs
    g = gains[0, 0:1]
    for j in range(n):
        unit, _ = norm_parts(xs[j][...].astype(F32))
        a[pl.ds((me ^ j) * tokens, tokens), :] = (unit * g).astype(BF)
    a.send()
    qkv[...] = dot(a[...], w[:, : 3 * hw]).astype(BF)
    qkv.send()

    def run(causal):
        for base in range(0, group, SEQ):
            logs = {}
            for h in range(hl):
                cols = slice(h * hs, (h + 1) * hs)
                k = qkv[base : base + SEQ, hw + h * hs : hw + (h + 1) * hs]
                v = qkv[base : base + SEQ, 2 * hw + h * hs : 2 * hw + (h + 1) * hs]
                for first in range(0, SEQ, QB):
                    rows = slice(base + first, base + first + QB)
                    width = first + QB if causal else SEQ
                    o[rows, cols], logs[first, h] = attend_tile(
                        qkv[rows, cols], k[:width], v[:width], first if causal else None
                    )
            for first in range(0, SEQ, QB):
                lse[base + first : base + first + QB, :] = by_lane(
                    [logs[first, h] for h in range(hl)]
                )

    pl.when(dec == 1)(lambda: run(True))
    pl.when(dec == 0)(lambda: run(False))
    for j in range(n):
        rows = o[pl.ds((me ^ j) * tokens, tokens), :]
        parts[j][...] = dot(rows, w[:, 3 * hw :], 1, 1).astype(BF)


def self_bwd_body(n, hl, hs, add, scal, *refs):
    gs, refs = refs[:n], refs[n:]
    a, qkv, o, lse, gains, w = refs[:6]
    olds, refs = refs[6 : 6 + add], [*refs[:6], *refs[6 + add :]]
    parts, (dw, dgain) = refs[6 : 6 + n], refs[6 + n : 8 + n]
    dso, do, dqkv, ps, dss = refs[8 + n :]
    me, dec = scal[0], scal[1]
    tokens = gs[0].shape[0]
    group = n * tokens
    hw = hl * hs
    scale = hs**-0.5
    for j in range(n):
        dso[pl.ds((me ^ j) * tokens, tokens), :] = gs[j][...]
    do[...] = dot(dso[...], w[:, 3 * hw :]).astype(BF)
    ready_all(o, lse, qkv)
    start_all(a, *olds)

    def run(causal):
        for base in range(0, group, SEQ):
            keys = slice(base, base + SEQ)
            rows_of = [slice(base + f, base + f + QB) for f in range(0, SEQ, QB)]
            logs = [lse[rows, :].T for rows in rows_of]
            inners = [
                by_lane(
                    [
                        row_products(
                            do[rows, h * hs : (h + 1) * hs], o[rows, h * hs : (h + 1) * hs]
                        )
                        for h in range(hl)
                    ]
                ).T
                for rows in rows_of
            ]
            dqs = []
            for h in range(hl):
                cols = slice(h * hs, (h + 1) * hs)
                q, dh = qkv[keys, cols], do[keys, cols]
                k = qkv[keys, hw + h * hs : hw + (h + 1) * hs]
                v = qkv[keys, 2 * hw + h * hs : 2 * hw + (h + 1) * hs]
                for i, first in enumerate(range(0, SEQ, QB)):
                    width = first + QB if causal else SEQ
                    block = slice(first, first + QB)
                    p, ds = attend_tile_back(
                        q[block],
                        k[:width],
                        v[:width],
                        dh[block],
                        logs[i][h : h + 1],
                        inners[i][h : h + 1],
                        first if causal else None,
                    )
                    ps[:width, block] = p
                    dss[:width, block] = ds
                kt = (k.astype(F32) * scale).astype(BF).T
                if causal:
                    dk = [dot(dss[f : f + QB, f:], q[f:]) for f in range(0, SEQ, QB)]
                    dv = [dot(ps[f : f + QB, f:], dh[f:]) for f in range(0, SEQ, QB)]
                    dk, dv = jnp.concatenate(dk, axis=0), jnp.concatenate(dv, axis=0)
                    dq = [
                        dot(kt[:, : f + QB], dss[: f + QB, f : f + QB]) for f in range(0, SEQ, QB)
                    ]
                    dqs.append(jnp.concatenate(dq, axis=1))
                else:
                    dk, dv = dot(dss[...], q), dot(ps[...], dh)
                    dqs.append(dot(kt, dss[...]))
                dqkv[keys, hw + h * hs : hw + (h + 1) * hs] = (dk * scale).astype(BF)
                dqkv[keys, 2 * hw + h * hs : 2 * hw + (h + 1) * hs] = dv.astype(BF)
            dqkv[keys, :hw] = jnp.concatenate(dqs, axis=0).T.astype(BF)

    pl.when(dec == 1)(lambda: run(True))
    pl.when(dec == 0)(lambda: run(False))
    total = jnp.zeros((1, a.shape[1]), F32)
    for j in range(n):
        rows = pl.ds((me ^ j) * tokens, tokens)
        da = dot(dqkv[rows, :], w[:, : 3 * hw], 1, 1)
        parts[j][...] = da.astype(BF)
        total += jnp.sum(da * a[rows, :].astype(F32), axis=0, keepdims=True)
    dgain[...] = total / gains[0, 0:1]
    grads = dot(a[...], dqkv[...], 0, 0), dot(dso[...], o[...], 0, 0)
    for h in range(hl):
        for t in range(4):
            at = (t % 3) * hw + h * hs
            to = slice((4 * h + t) * hs, (4 * h + t + 1) * hs)
            part = grads[0][:, at : at + hs] if t < 3 else grads[1][:, h * hs : (h + 1) * hs]
            dw[:, to] = ((part + olds[0][:, to]) if add else part).astype(dw.dtype)


def after_self_body(n, pieces, scal, *refs):
    x, refs = refs[0], refs[1:]
    ps, (gains, d, cot), (h1,), outs = (
        refs[:pieces],
        refs[pieces : pieces + 3],
        refs[pieces + 3 : pieces + 4],
        refs[pieces + 4 :],
    )
    rows = x[...].astype(F32)
    for p in ps:
        rows = rows + p[...].astype(F32)
    h1[...] = rows
    h1.send()
    unit, _ = norm_parts(rows)
    u = (unit * gains[0, 2:3]).astype(BF)
    chosen = jnp.where(scal[1] == 0, u.astype(F32), cot[...].astype(F32)).astype(BF)
    send_slots(d, chosen, outs)


def memory_body(n, scal, *refs):
    rs, (h1, d, gains), (y, m) = refs[:n], refs[n : n + 3], refs[n + 3 :]
    stacked = jnp.concatenate([r[...] for r in rs], axis=0)
    rows = h1[...] + dot(d[...], stacked, 0, 0)
    y[...] = rows
    y.send()
    unit, _ = norm_parts(rows)
    m[...] = (unit * gains[0, 1:2]).astype(BF)


def final_body(n, micro, scal, *refs):
    out = refs[-1]
    for m in range(micro):
        rs, (h2, d, ye) = refs[:n], refs[n : n + 3]
        refs = refs[n + 3 :]
        ready_all(h2, d, ye)

        @pl.when(scal[1] == 0)
        def _():
            out[0, m] = ye[...].astype(BF)

        @pl.when(scal[1] == 1)
        def _():
            stacked = jnp.concatenate([r[...] for r in rs], axis=0)
            out[0, m] = (h2[...] + dot(d[...], stacked, 0, 0)).astype(BF)


def cross_fwd_body(n, per, hl, hs, scal, *refs):
    ms, refs = refs[:per], refs[per:]
    wx, wkv, (h1, gains, d), refs = refs[:n], refs[n : 2 * n], refs[2 * n : 2 * n + 3], refs[2 * n + 3 :]
    h2, c, mem, qc, kv, oc, lse = refs[:7]
    outs = refs[7:]
    hw = hl * hs
    tokens = h1.shape[0]
    for j in range(per):
        mem[j * tokens : (j + 1) * tokens, :] = ms[j][...]
    mem.send()
    unit, _ = norm_parts(h1[...])
    start_all(*wkv)
    c[...] = (unit * gains[0, 1:2]).astype(BF)
    c.send()
    for j in range(n):
        qc[:, j * hw : (j + 1) * hw] = dot(c[...], wx[j][:, :hw]).astype(BF)
    qc.send()
    for j in range(n):
        kv[:, 2 * j * hw : 2 * (j + 1) * hw] = dot(mem[...], wkv[j][...]).astype(BF)
    kv.send()
    total = h1[...]
    logs = []
    for j in range(n):
        for h in range(hl):
            at = j * hw + h * hs
            k = kv[:, 2 * j * hw + h * hs : 2 * j * hw + (h + 1) * hs]
            v = kv[:, (2 * j + 1) * hw + h * hs : (2 * j + 1) * hw + (h + 1) * hs]
            oc[:, at : at + hs], log = attend_tile(qc[:, at : at + hs], k, v, None)
            logs.append(log)
        total = total + dot(oc[:, j * hw : (j + 1) * hw], wx[j][:, hw:], 1, 1)
    oc.send()
    lse[...] = by_lane(logs)
    lse.send()
    h2[...] = total
    h2.send()
    unit, _ = norm_parts(total)
    send_slots(d, (unit * gains[0, 2:3]).astype(BF), outs)


def cross_bwd_body(n, per, hl, hs, scal, *refs):
    dus, wx, wkv, refs = refs[:n], refs[n : 2 * n], refs[2 * n : 3 * n], refs[3 * n :]
    h2, gains, d, cot, qc, kv, oc, lse = refs[:8]
    refs = refs[8:]
    dh2, dco, dqc, dkv, dgain = refs[:5]
    dms, (doc,) = refs[5 : 5 + per], refs[5 + per :]
    hw = hl * hs
    tokens = h2.shape[0]
    stacked = jnp.concatenate([r[...] for r in dus], axis=0)
    unit, inverse = norm_parts(h2[...])
    start_all(*wx, oc, lse, qc, kv, *wkv)
    back, gained = norm_back(dot(d[...], stacked, 0, 0), unit, inverse, gains[0, 2:3])
    dgain[...] = gained
    total = cot[...].astype(F32) + back
    dh2[...] = total
    dh2.send()
    dco[...] = total.astype(BF)
    dco.send()
    for j in range(n):
        doc[:, j * hw : (j + 1) * hw] = dot(dco[...], wx[j][:, hw:]).astype(BF)
    logs = lse[...].T
    places = [slice(i * hs, (i + 1) * hs) for i in range(n * hl)]
    inner = by_lane([row_products(doc[:, at], oc[:, at]) for at in places]).T
    scale = hs**-0.5
    dqs = []
    for i, at in enumerate(places):
        j, h = i // hl, i % hl
        k_at = slice(2 * j * hw + h * hs, 2 * j * hw + (h + 1) * hs)
        v_at = slice((2 * j + 1) * hw + h * hs, (2 * j + 1) * hw + (h + 1) * hs)
        q, k, do = qc[:, at], kv[:, k_at], doc[:, at]
        p, ds = attend_tile_back(q, k, kv[:, v_at], do, logs[i : i + 1], inner[i : i + 1], None)
        dkv[:, k_at] = (dot(ds, q) * scale).astype(BF)
        dkv[:, v_at] = dot(p, do).astype(BF)
        dqs.append(dot((k.astype(F32) * scale).astype(BF).T, ds))
    dkv.send()
    dqc[...] = jnp.concatenate(dqs, axis=0).T.astype(BF)
    dqc.send()
    for i in range(per):
        rows = slice(i * tokens, (i + 1) * tokens)
        total = 0.0
        for j in range(n):
            total += dot(dkv[rows, 2 * j * hw : 2 * (j + 1) * hw], wkv[j][...], 1, 1)
        dms[i][...] = total.astype(BF)


def cross_late_body(n, hl, hs, count, scal, *refs):
    wx, (dh2, dco, dqc, dkv, oc, c, mem, h1, gains) = refs[:n], refs[n : n + 9]
    olds, refs = refs[n + 9 : n + 9 + count], refs[n + 9 + count :]
    dh1, dgain, dws = refs[0], refs[1], refs[2:]
    hw = hl * hs
    dc = jnp.zeros(h1.shape, F32)
    for j in range(n):
        dc += dot(dqc[:, j * hw : (j + 1) * hw], wx[j][:, :hw], 1, 1)
    unit, inverse = norm_parts(h1[...])
    back, gained = norm_back(dc, unit, inverse, gains[0, 1:2])
    dh1[...] = dh2[...] + back
    dh1.send()
    dgain[...] = gained
    ct, dt, mt = c[...].T, dco[...].T, mem[...].T
    for j in range(n):
        dq = dot(ct, dqc[:, j * hw : (j + 1) * hw])
        de = dot(dt, oc[:, j * hw : (j + 1) * hw])
        dkv_j = dot(mt, dkv[:, 2 * j * hw : 2 * (j + 1) * hw])
        for h in range(hl):
            at = slice(h * hs, (h + 1) * hs)
            parts = dq[:, at], de[:, at], dkv_j[:, at], dkv_j[:, hw + h * hs : hw + (h + 1) * hs]
            for t, part in enumerate(parts):
                to = (t // 2) * 2 * hw + (2 * h + t % 2) * hs
                if count:
                    part = part + olds[j][:, to : to + hs].astype(F32)
                dws[j][:, to : to + hs] = part.astype(BF)


def sum_body(scal, *refs):
    total = refs[0][...].astype(F32)
    for ref in refs[1:-1]:
        total = total + ref[...].astype(F32)
    refs[-1][...] = total.astype(refs[-1].dtype)


def halves_body(scal, *refs):
    *parts, left, right = refs
    total = parts[0][...].astype(F32)
    for ref in parts[1:]:
        total = total + ref[...].astype(F32)
    half = total.shape[1] // 2
    left[...] = total[:, :half].astype(BF)
    right[...] = total[:, half:].astype(BF)


def pick_body(scal, first, second, out):
    out[...] = jnp.where(scal[1] == 1, first[...].astype(F32), second[...].astype(F32)).astype(BF)


def memory_back_body(n, scal, *refs):
    (dm, y, gains, cot, d), (dy, dgain), outs = refs[:5], refs[5:7], refs[7:]
    unit, inverse = norm_parts(y[...])
    back, gained = norm_back(dm[...].astype(F32), unit, inverse, gains[0, 1:2])
    dgain[...] = gained
    rows = cot[...].astype(F32) + back
    dy[...] = rows
    dy.send()
    send_slots(d, rows.astype(BF), outs)


def before_self_body(n, scal, *refs):
    dus, (d, dy, h1, gains, given), (dh1, dso, dgain) = refs[:n], refs[n : n + 5], refs[n + 5 :]
    ready_all(gains, h1, d, dy, given)

    @pl.when(scal[1] == 0)
    def _():
        stacked = jnp.concatenate([r[...] for r in dus], axis=0)
        unit, inverse = norm_parts(h1[...])
        back, gained = norm_back(dot(d[...], stacked, 0, 0), unit, inverse, gains[0, 2:3])
        rows = dy[...] + back
        dh1[...] = rows
        dso[...] = rows.astype(BF)
        dgain[...] = gained

    @pl.when(scal[1] == 1)
    def _():
        dh1[...] = given[...]
        dso[...] = given[...].astype(BF)
        dgain[...] = jnp.zeros(dgain.shape, F32)


def finish_body(pieces, micro, scal, *refs):
    gains, out, refs = refs[0], refs[-1], refs[1:-1]
    for m in range(micro):
        ps, (dh1, x), refs = refs[:pieces], refs[pieces : pieces + 2], refs[pieces + 2 :]
        da = ps[0][...].astype(F32)
        for p in ps[1:]:
            da = da + p[...].astype(F32)
        unit, inverse = norm_parts(x[...].astype(F32))
        back, _ = norm_back(da, unit, inverse, gains[0, 0:1])
        out[0, m] = dh1[...] + back


def gelu_low(z):
    z = z.astype(BF)

    def c(value):
        return jnp.asarray(value, BF)

    inner = c(ROOT) + c(ROOT * 0.044715) * (z * z)
    half = c(0.5) + c(0.5) * jnp.tanh(z * inner)
    value = z * half
    return value, half + (value - value * half) * (c(6.0) * inner - c(4.0 * ROOT))


def expert_body(n, el, capp, block, mode, scal, *refs):
    us, refs = refs[:n], refs[n:]
    drs = ()
    if mode != "fwd":
        drs, refs = refs[:n], refs[n:]
    (wi_far, wo_far), refs = refs[:2], refs[2:]
    rs, dus = (), ()
    if mode != "back":
        rs, refs = refs[:n], refs[n:]
    if mode != "fwd":
        dus, refs = refs[:n], refs[n:]
    u_all = dr_all = None
    if mode != "back":
        u_all, refs = refs[0], refs[1:]
    if mode != "fwd":
        dr_all, refs = refs[0], refs[1:]
    wi, wo, sems = refs
    steps = wi.shape[2] // block
    copies = []
    for e in range(el):
        for f in range(steps):
            part = slice(f * block, (f + 1) * block)
            sem = e * steps + f
            copies.append(
                (
                    pltpu.make_async_copy(
                        wi_far.at[0, e, :, part], wi.at[e, :, part], sems.at[0, sem]
                    ),
                    pltpu.make_async_copy(
                        wo_far.at[0, e, part, :], wo.at[e, part, :], sems.at[1, sem]
                    ),
                )
            )

    def fetch(k):
        if k < len(copies):
            for copy in copies[k]:
                copy.start()

    fetch(0)
    fetch(1)
    rows_u = [
        jnp.concatenate([us[j][e * capp : (e + 1) * capp, :] for j in range(n)], axis=0)
        for e in range(el)
    ]
    rows_dr = [
        jnp.concatenate([drs[j][e * capp : (e + 1) * capp, :] for j in range(n)], axis=0)
        for e in range(el if drs else 0)
    ]
    for e in range(el):
        if u_all is not None:
            u_all[e] = rows_u[e]
        if dr_all is not None:
            dr_all[e] = rows_dr[e]
    for ref in (u_all, dr_all):
        if ref is not None:
            ref.send()
    for e in range(el):
        racc = dacc = 0.0
        for f in range(steps):
            for copy in copies[e * steps + f]:
                copy.wait()
            fetch(e * steps + f + 2)
            part = slice(f * block, (f + 1) * block)
            wi_f, wo_f = wi[e, :, part], wo[e, part, :]
            z = dot(rows_u[e], wi_f)
            if drs:
                g, slope = gelu_parts(z)
            else:
                g = gelu_value(z)
            if rs:
                racc += dot(g.astype(BF), wo_f)
            if dus:
                dz = (dot(rows_dr[e], wo_f, 1, 1) * slope).astype(BF)
                dacc += dot(dz, wi_f, 1, 1)
        for j in range(n):
            part, at = slice(j * capp, (j + 1) * capp), slice(e * capp, (e + 1) * capp)
            if rs:
                rs[j][at, :] = racc[part].astype(BF)
            if dus:
                dus[j][at, :] = dacc[part].astype(BF)


def experts(step, us, drs, w_in, w_out, capp, active, mode):
    n, el = len(us), w_in.shape[1]
    width, ff = w_in.shape[2:]
    block = 512
    outs = n * (2 if mode == "both" else 1)
    products = {"fwd": 2, "both": 4, "back": 3}[mode]
    result = step(
        functools.partial(expert_body, n, el, capp, block, mode),
        [*us, *drs, Raw(w_in), Raw(w_out)],
        [((el * capp, width), BF)] * outs
        + [((el, n * capp, width), BF, True)] * (2 if mode == "both" else 1),
        scratch=[
            pltpu.VMEM(w_in.shape[1:], BF),
            pltpu.VMEM(w_out.shape[1:], BF),
            pltpu.SemaphoreType.DMA((2, el * ff // block)),
        ],
        flops=products * 2 * el * n * capp * width * ff,
        active=active,
    )
    return [result[i : i + n] for i in range(0, outs, n)], result[outs:]


def expert_grad_body(add, *refs):
    u_ref, dr_ref, wi, wo = refs[:4]
    refs = refs[4:]
    olds, refs = (refs[:2], refs[2:]) if add else ((), refs)
    dwi, dwo, ut = refs[-3:]
    lead, _, rows, width = u_ref.shape
    chunk = 1
    while 2 * chunk * rows <= 1024 and lead % (2 * chunk) == 0:
        chunk *= 2
    size = chunk * rows

    @pl.when(pl.program_id(1) == 0)
    def _():
        for at in range(0, lead, chunk):
            u = u_ref[at : at + chunk, 0].reshape(size, width)
            ut[:, at * rows : at * rows + size] = u.T

    for at in range(0, lead, chunk):
        u = u_ref[at : at + chunk, 0].reshape(size, width)
        dr = dr_ref[at : at + chunk, 0].reshape(size, width)
        g, slope = gelu_low(dot(u, wi[0, 0]))
        dz = dot(dr, wo[0, 0], 1, 1).astype(BF) * slope
        di = dot(ut[:, at * rows : at * rows + size], dz)
        do = dot(g, dr, 0, 0)
        if at:
            dwi[0, 0] += di
            dwo[0, 0] += do
        elif add:
            dwi[0, 0] = olds[0][0, 0] + di
            dwo[0, 0] = olds[1][0, 0] + do
        else:
            dwi[0, 0] = di
            dwo[0, 0] = do


def expert_grads(u, dr, w_in, w_out, olds, after, first, many, add):
    lead, _, rows, width = u.shape
    ff = w_in.shape[3]
    block = 512
    spec = pl.BlockSpec((lead, 1, rows, width), lambda e, f: (0, first + e, 0, 0))
    into = pl.BlockSpec((1, 1, width, block), lambda e, f: (0, first + e, 0, f))
    back = pl.BlockSpec((1, 1, block, width), lambda e, f: (0, first + e, f, 0))
    body = functools.partial(expert_grad_body, add)
    given = 4 + (len(olds) if add else 0)
    count = 4 + len(olds) + len(after)

    def trimmed(*refs):
        dwi, dwo, _, ut = refs[count:]
        body(*refs[:given], dwi, dwo, ut)

    arrays = [pinned(x) for x in (u, dr, w_in, w_out, *olds)]
    after = [pinned(a) if stays(a) else a for a in after]
    return pl.pallas_call(
        trimmed,
        grid=(many, ff // block),
        in_specs=[spec] * 2
        + [into, back]
        + ([into, back] if add else [HB, HB])[: len(olds)]
        + [HB if stays(a) else ANY for a in after],
        out_specs=[into, back, HB],
        out_shape=[
            pltpu.HBM(w_in.shape, F32),
            pltpu.HBM(w_out.shape, F32),
            pltpu.HBM((8, 128), F32),
        ],
        scratch_shapes=[pltpu.VMEM((width, lead * rows), BF)],
        input_output_aliases={4: 0, 5: 1} if olds else {},
        compiler_params=pltpu.CompilerParams(
            vmem_limit_bytes=(22 << 20) + 10 * lead * rows * width
        ),
        cost_estimate=pl.CostEstimate(
            flops=8 * lead * many * rows * width * ff, bytes_accessed=0, transcendentals=0
        ),
        name="expert_grads",
    )(*arrays, *after)


def on_device(inputs, cotangent, expert_ids, self_proj, cross_proj, gains, w_in, w_out):
    micro, tokens, width = inputs.shape[1:]
    n = lax.axis_size("mp")
    hl = self_proj.shape[2]
    hs = self_proj.shape[3] // 4
    hw = hl * hs
    el = w_in.shape[1]
    capacity = max(2, 3 * tokens // (2 * n * el))
    capp = -(-capacity // 16) * 16
    slots = el * capp
    per = SEQ // tokens
    group = n * tokens
    M = range(micro)
    decoder = lax.axis_index("section") == 1
    scal = jnp.stack([lax.axis_index("mp"), lax.axis_index("section")]).astype(jnp.int32)
    last = []

    def step(body, ins, outs, **more):
        *res, token = call(body, scal, ins, outs, after=list(last), **more)
        last[:] = [token]
        return res

    def swap(x, k, sections=(0, 1)):
        pairs = [(s * n + i, s * n + (i ^ k)) for s in sections for i in range(n)]
        return lax.ppermute(x, ("section", "mp"), pairs)

    def gather(x, count, sections=(0, 1), gated=False):
        blocks = {0: x}
        bit = count // 2
        while bit:
            blocks.update({j ^ bit: swap(b, bit, sections) for j, b in list(blocks.items())})
            if gated and bit == count // 2:
                (blocks[bit],) = gate([blocks[bit]])
            bit //= 2
        return [blocks[j] for j in range(count)]

    def total(pieces, dtype):
        return call(sum_body, scal, pieces, [(pieces[0].shape, dtype)])[0]

    def scatter(blocks, hold=False):
        live = {j: [b] for j, b in enumerate(blocks)}
        bit = 1
        while bit < len(blocks):
            for j in [j for j in live if j & bit]:
                pieces = live.pop(j)
                out = pieces[0]
                if len(pieces) > 1:
                    out = sum(p.astype(F32) for p in pieces).astype(BF)
                    if hold:
                        last.append(out)
                live[j ^ bit].append(swap(out, bit))
            bit *= 2
        return live[0]

    def exchange(blocks):
        return [blocks[0]] + [swap(blocks[j], j) for j in range(1, n)]

    def gate(arrays, waits=(), space=ANY):
        count = len(arrays)
        waits = [*last, *waits]
        *arrays, token = pl.pallas_call(
            lambda *refs: None,
            out_shape=[
                (pltpu.HBM if space is HB else jax.ShapeDtypeStruct)(a.shape, a.dtype)
                for a in arrays
            ]
            + [pltpu.HBM((8, 128), F32)],
            in_specs=[space] * count + [HB if stays(a) else ANY for a in waits],
            out_specs=[space] * count + [HB],
            input_output_aliases={i: i for i in range(count)},
            compiler_params=pltpu.CompilerParams(vmem_limit_bytes=1 << 20),
            name="gate",
        )(
            *[pinned(a) if space is HB else a for a in arrays],
            *[pinned(a) if stays(a) else a for a in waits],
        )
        last[:] = [token]
        return arrays

    def lazy(fars):
        return [Far(f.array, *f.index, later=True) for f in fars]

    def to_decoder(x):
        return lax.ppermute(x, "section", [(0, 1)])

    def to_encoder(x):
        return lax.ppermute(x, "section", [(1, 0)])

    xs = [inputs[0, m] for m in M]
    ws = self_proj[0].reshape(width, hl, 4, hs).transpose(0, 2, 1, 3).reshape(width, 4 * hw)
    wc = cross_proj[0].reshape(width, hl, 2, hs).transpose(0, 2, 1, 3).reshape(width, 2 * hw)
    row, wide, line = ((tokens, width), BF), ((tokens, width), F32, True), ((1, width), F32, True)
    slot = ((slots, width), BF)

    def far(shape, dtype=BF):
        return (shape, dtype, True)

    last.extend([ws, wc])
    routes = step(
        functools.partial(place_body, n, el, capp),
        [expert_ids[0]],
        [far((n * slots, tokens))] * micro,
    )
    routes = [Far(r) for r in routes]
    gain = Far(gains)
    x_far = [Far(inputs, 0, m) for m in M]
    cots = [Far(cotangent, 0, m) for m in M]

    x_all = [gather(xs[m], n, gated=m == 0) for m in M]
    saved, self_parts = [], []
    for m in M:
        res = step(
            functools.partial(self_fwd_body, n, hl, hs),
            [*x_all[m], gain, Far(ws)],
            [
                far((group, width)),
                far((group, 3 * hw)),
                far((group, hw)),
                far((group, 128), F32),
            ]
            + [row] * n,
            flops=2 * group * width * 4 * hw + 4 * 4 * group * SEQ * hw,
        )
        saved.append(res[:4])
        parts = res[4:]
        if m:
            last.extend(self_parts[-1])
            parts = gate(parts)
        self_parts.append(scatter(parts, m < micro - 1))
    h1, first_slots = [], []
    for m in M:
        res = step(
            functools.partial(after_self_body, n, len(self_parts[m])),
            [x_far[m], *self_parts[m], gain, routes[m], cots[m]],
            [wide] + [slot] * n,
            flops=2 * n * slots * tokens * width,
        )
        h1.append(Far(res[0]))
        first_slots.append(exchange(res[1:]))

    wx_all = [Far(b) for b in gather(wc, n, (1,))]
    wkv_all = [Far(b, later=True) for b in gather(to_decoder(wc), n, (1,))]
    ye, mem_all, rs, enc_u = [], [], [], []
    for m in M:
        (r,), (u,) = experts(
            step, first_slots[m], (), w_in, w_out, capp, 0, "fwd"
        )
        rs.append(exchange(r))
        enc_u.append(u)
    for m in M:
        y, mem = step(
            functools.partial(memory_body, n),
            [*rs[m], h1[m], routes[m], gain],
            [wide, row],
            flops=2 * n * slots * tokens * width,
            active=0,
        )
        ye.append(Far(y))
        mem_all.append(gather(to_decoder(mem), per))

    crossed, second_slots = [], []
    for m in M:
        res = step(
            functools.partial(cross_fwd_body, n, per, hl, hs),
            [*mem_all[m], *wx_all, *wkv_all, h1[m], gain, routes[m]],
            [
                wide,
                far((tokens, width)),
                far((SEQ, width)),
                far((tokens, n * hw)),
                far((SEQ, 2 * n * hw)),
                far((tokens, n * hw)),
                far((tokens, 128), F32),
            ]
            + [slot] * n,
            flops=4 * SEQ * width * n * hw + 4 * 4 * tokens * SEQ * n * hw,
            active=1,
        )
        crossed.append([Far(r) for r in res[:7]])
        second_slots.append(exchange(res[7:]))

    rs, dus, dec_u, dec_dr = [], [], [], []
    for m in M:
        (r, du), (u, dr) = experts(
            step,
            second_slots[m],
            [Far(b) for b in first_slots[m]],
            w_in,
            w_out,
            capp,
            1,
            "both",
        )
        dus.append(exchange(du))
        rs.append(r)
        dec_u.append(u)
        dec_dr.append(dr)

    late, gain_parts, kept, pieces = [], [[], [], []], [], []
    for m in M:
        h2, c, mem, qc, kv, oc, lse = crossed[m]
        res = step(
            functools.partial(cross_bwd_body, n, per, hl, hs),
            [*dus[m], *lazy(wx_all), *wkv_all, h2, gain, routes[m], cots[m]]
            + lazy((qc, kv, oc, lse)),
            [wide, far((tokens, width)), far((tokens, n * hw)), far((SEQ, 2 * n * hw)), line]
            + [row] * per,
            scratch=[pltpu.VMEM((tokens, n * hw), BF)],
            flops=4 * SEQ * width * n * hw + 4 * 10 * tokens * SEQ * n * hw,
            active=1,
        )
        kept.append([Far(r) for r in res[:4]])
        gain_parts[2].append(res[4])
        parts = res[5:]
        if m:
            last.extend(pieces[-1])
            parts = gate(parts)
        pieces.append(scatter(parts, m < micro - 1))
    dms = [to_encoder(sum(p.astype(F32) for p in pieces[m]).astype(BF)) for m in M]

    def rows_of(encoder_rows, decoder_rows):
        whole = jnp.where(decoder, decoder_rows, encoder_rows)[None]
        return lax.all_gather(whole, "dp", axis=0, tiled=True)

    u_rows = [rows_of(enc_u[m], dec_u[m]) for m in M]

    memory_gain, dr_rows, dh1, dso, parts_a, self_total = [], [], [], [], [], None

    def experts_back(m):
        res = step(
            functools.partial(memory_back_body, n),
            [dms[m], ye[m], gain, cots[m], routes[m]],
            [wide, line] + [slot] * n,
            active=0,
        )
        memory_gain.append(res[1])
        third = exchange(res[2:])
        (du,), (dr,) = experts(
            step,
            [Far(b) for b in first_slots[m]],
            third,
            w_in,
            w_out,
            capp,
            0,
            "back",
        )
        dr_rows.append(rows_of(dr, dec_dr[m]))
        return res[0], exchange(du)

    def cross_late(m):
        h2, c, mem, qc, kv, oc, lse = crossed[m]
        olds = late[m - 1][2:] if m else []
        late.append(
            step(
                functools.partial(cross_late_body, n, hl, hs, len(olds)),
                [*wx_all, *kept[m], oc, c, mem, h1[m], gain, *[Far(x) for x in olds]],
                [wide, line] + [far((width, 4 * hw))] * n,
                flops=8 * SEQ * width * n * hw,
                active=1,
            )
        )

    def before_self(m, dy, du):
        res = step(
            functools.partial(before_self_body, n),
            [*du, routes[m], Far(dy), h1[m], gain, Far(late[m][0])],
            [wide, row, line],
        )
        dh1.append(res[0])
        dso.append(gather(res[1], n))
        gain_parts[2].append(res[2])

    def self_back(m, before):
        a, qkv, o, lse = saved[m]
        res = step(
            functools.partial(self_bwd_body, n, hl, hs, bool(before)),
            [*dso[m], Far(a, later=True)]
            + [Far(x) for x in (qkv, o, lse)]
            + [gain, Far(ws)]
            + [Far(x, later=True) for x in before],
            [row] * n + [far((width, 4 * hw), BF if m == micro - 1 else F32), line],
            scratch=[
                pltpu.VMEM((group, width), BF),
                pltpu.VMEM((group, hw), BF),
                pltpu.VMEM((group, 3 * hw), BF),
                pltpu.VMEM((SEQ, SEQ), BF),
                pltpu.VMEM((SEQ, SEQ), BF),
            ],
            flops=2 * group * width * 8 * hw + 4 * 10 * group * SEQ * hw,
        )
        parts_a.append(scatter(res[:n], m < micro - 1))
        gain_parts[0].append(res[n + 1])
        return [res[n]]

    grads = []
    for m in M:
        dy, du = experts_back(m)
        if m:
            grads = self_back(m - 1, grads)
        cross_late(m)
        before_self(m, dy, du)
    cross_pieces = scatter(late[-1][2:])
    grads = self_back(micro - 1, grads)
    own, remote = step(halves_body, cross_pieces, [((width, 2 * hw), BF)] * 2)
    remote = to_encoder(remote)
    (gain_total,) = step(
        functools.partial(gains_body, micro),
        [Far(g) for g in (*gain_parts[0], *memory_gain, *gain_parts[2][micro:])]
        + [Far(g) for g in (*[x[1] for x in late], *gain_parts[2][:micro])],
        [((3, width), F32)],
    )

    hops = [(axis, 1 << b) for axis in ("mp", "dp") for b in range(lax.axis_size(axis).bit_length() - 1)]

    def hop(x):
        axis, bit = hops.pop(0)
        return x, lax.ppermute(x, axis, [(i, i ^ bit) for i in range(lax.axis_size(axis))])

    def land(pair):
        return step(sum_body, pair, [((3, width), F32)])[0]

    totals = []

    def grads_of(m, first, many):
        *new, token = expert_grads(
            u_rows[m], dr_rows[m], w_in, w_out, totals, list(last), first, many, m > 0
        )
        totals[:], last[:] = new, [token]

    pair = hop(gain_total)
    grads_of(0, 0, 1)
    (cross_total,) = step(pick_body, [own, remote], [far((width, 2 * hw))])
    sums = lax.psum(tuple(gate([*grads, cross_total], [*u_rows, *dr_rows], HB)), "dp")
    sums = lax.optimization_barrier(sums)
    pair = hop(land(pair))
    rs[0] = exchange(gate(rs[0]))
    grads_of(0, 1, el - 1)
    (input_grads,) = step(
        functools.partial(finish_body, len(parts_a[0]), micro),
        [gain] + [x for i in M for x in (*parts_a[i], Far(dh1[i]), x_far[i])],
        [((1, micro, tokens, width), F32, True)],
    )
    rs[1:] = [exchange(r) for r in rs[1:]]
    for m in range(1, micro):
        for e in range(el):
            pair = hop(land(pair))
            grads_of(m, e, 1)
            if m == 1 and e == 0:
                (outs,) = step(
                    functools.partial(final_body, n, micro),
                    [x for m in M for x in (*rs[m], crossed[m][0], routes[m], ye[m])],
                    [((1, micro, tokens, width), BF, True)],
                )
    gain_total = land(pair)
    while hops:
        gain_total = land(hop(gain_total))
    first_total, second_total = totals
    self_total = sums[0].astype(F32).reshape(width, hl, 4 * hs)
    cross_total = sums[1].astype(F32).reshape(width, hl, 2 * hs)
    return (
        outs,
        input_grads,
        self_total[None],
        cross_total[None],
        gain_total[None],
        first_total,
        second_total,
    )


def solution(mesh):
    rows = P("section", None, ("dp", "mp"), None)
    heads = P("section", None, "mp", None)
    expert = P("section", "mp", None, None)
    return jax.shard_map(
        on_device,
        mesh=mesh,
        in_specs=(rows, rows, rows, heads, heads, P("section", None, None), expert, expert),
        out_specs=(rows, rows, heads, heads, P("section", None, None), expert, expert),
        check_vma=False,
    )
```

```python
import functools

import jax
import jax.numpy as jnp
from jax import lax
from jax.experimental import pallas as pl
from jax.experimental.pallas import tpu as pltpu
from jax.sharding import PartitionSpec as P

SEQ = 1024
EPS = 1e-05
ROOT = 0.7978845608028654
NEG = -1000000000.0
BF = jnp.bfloat16
F32 = jnp.float32
QB = 256
CFG = {'dvm': 1, 'low': 1}


def dot(a, b, ca=1, cb=0):
    return lax.dot_general(a, b, (((ca,), (cb,)), ((), ())), preferred_element_type=F32)


def norm_parts(rows):
    centred = rows - jnp.mean(rows, axis=-1, keepdims=True)
    inverse = lax.rsqrt(jnp.mean(centred * centred, axis=-1, keepdims=True) + EPS)
    return centred * inverse, inverse


def norm_back(upstream, unit, inverse, gain):
    scaled = upstream * gain
    inner = (
        scaled
        - jnp.mean(scaled, axis=-1, keepdims=True)
        - unit * jnp.mean(scaled * unit, axis=-1, keepdims=True)
    )
    return inverse * inner, jnp.sum(upstream * unit, axis=0, keepdims=True)


def gelu_parts(z):
    square = z * z
    t = jnp.tanh(z * (0.7978845608028654 + (0.7978845608028654 * 0.044715) * square))
    half = 0.5 + 0.5 * t
    slope = half + (0.5 * z) * (1.0 - t * t) * (
        0.7978845608028654 + (3.0 * 0.7978845608028654 * 0.044715) * square
    )
    return z * half, slope


def gelu_value(z):
    t = jnp.tanh(z * (0.7978845608028654 + (0.7978845608028654 * 0.044715) * (z * z)))
    return z * (0.5 + 0.5 * t)


LOG2E = 1.4426950408889634


def attend_tile(q, k, v, first):
    s = dot(q, k, 1, 1) * (q.shape[1] ** -0.5 * LOG2E)
    if first is not None:
        r = lax.broadcasted_iota(jnp.int32, s.shape, 0) + first
        s = jnp.where(lax.broadcasted_iota(jnp.int32, s.shape, 1) <= r, s, NEG)
    peak = jnp.max(s, axis=-1, keepdims=True)
    p = jnp.exp2(s - peak)
    total = jnp.sum(p, axis=-1, keepdims=True)
    o = dot(p.astype(BF), v) / total
    return o.astype(BF), peak + jnp.log2(total)


def attend_tile_back(q, k, v, do, lse, inner, first):
    s = dot(k, q, 1, 1) * (q.shape[1] ** -0.5 * LOG2E)
    if first is not None:
        c = lax.broadcasted_iota(jnp.int32, s.shape, 1) + first
        s = jnp.where(lax.broadcasted_iota(jnp.int32, s.shape, 0) <= c, s, NEG)
    p = jnp.exp2(s - lse)
    ds = (p * (dot(v, do, 1, 1) - inner)).astype(BF)
    return p.astype(BF), ds


def by_lane(columns):
    lane = lax.broadcasted_iota(jnp.int32, (columns[0].shape[0], 128), 1)
    wide = jnp.zeros((columns[0].shape[0], 128), F32)
    for i, column in enumerate(columns):
        wide = jnp.where(lane == i, column, wide)
    return wide


def row_products(a, b):
    return jnp.sum(a.astype(F32) * b.astype(F32), axis=-1, keepdims=True)


SM = pl.BlockSpec(memory_space=pltpu.SMEM)
VM = pl.BlockSpec(memory_space=pltpu.VMEM)
HB = pl.BlockSpec(memory_space=pltpu.HBM)
ANY = pl.BlockSpec(memory_space=pl.ANY)


class Far:
    def __init__(self, array, *index, later=False):
        self.array, self.index, self.later = array, index, later
        self.shape, self.dtype = array.shape[len(index) :], array.dtype


class Raw:
    def __init__(self, array):
        self.array, self.shape, self.dtype = array, array.shape, array.dtype


class Arriving:
    def __init__(self, ref, index, buffer, sem):
        source = ref.at[index] if index else ref
        self.copy, self.buffer, self.waited = (
            pltpu.make_async_copy(source, buffer, sem),
            buffer,
            False,
        )
        self.shape = buffer.shape
        self.started = False

    def start(self):
        if not self.started:
            self.copy.start()
            self.started = True

    def ready(self):
        self.start()
        if not self.waited:
            self.copy.wait()
            self.waited = True
        return self.buffer

    def __getitem__(self, at):
        return self.ready()[at]


class Leaving:
    def __init__(self, ref, buffer, sem):
        self.copy, self.buffer, self.sent = pltpu.make_async_copy(buffer, ref, sem), buffer, False
        self.shape, self.dtype = buffer.shape, buffer.dtype

    def send(self):
        if not self.sent:
            self.copy.start()
            self.sent = True

    def __getitem__(self, at):
        return self.buffer[at]

    def __setitem__(self, at, value):
        self.buffer[at] = value


def ready_all(*refs):
    for ref in refs:
        if isinstance(ref, Arriving):
            ref.ready()


def start_all(*refs):
    for ref in refs:
        if isinstance(ref, Arriving):
            ref.start()


def pinned(array):
    return pltpu.with_memory_space_constraint(array, pltpu.HBM)


def stays(array):
    return array.shape == (8, 128) or array.ndim > 2


def nbytes(shape, dtype):
    size = jnp.dtype(dtype).itemsize
    for x in shape[:-1]:
        size *= x
    return size * (-(-shape[-1] // 128) * 128)


def call(
    body, scal, ins, outs, scratch=(), flops=0, extra=13, after=(), active=None, passing=None
):
    far_in = [k for k, x in enumerate(ins) if isinstance(x, Far)]
    far_out = [k for k, x in enumerate(outs) if len(x) > 2 and x[2]]
    shapes = [
        jax.ShapeDtypeStruct(*x) if len(x) == 2 else pltpu.HBM(*x[:2]) if x[2] else pltpu.VMEM(*x[:2])
        for x in outs
    ]
    shapes.append(pltpu.HBM((8, 128), F32))
    buffers = [pltpu.VMEM(ins[k].shape, ins[k].dtype) for k in far_in]
    buffers += [pltpu.VMEM(outs[k][0], outs[k][1]) for k in far_out]
    sems = [pltpu.SemaphoreType.DMA(())] * len(buffers)
    count, waits = 1 + len(ins), len(after)
    held = sum(nbytes(b.shape, b.dtype) for b in buffers + list(scratch) if "sem" not in str(b.dtype))
    moved = sum(nbytes(a.shape, a.dtype) for a in list(ins) + shapes)

    def whole(*refs):
        scal, in_refs = refs[0], list(refs[1:count])
        rest = refs[count + waits :]
        out_refs, rest = list(rest[: len(outs)]), rest[len(outs) + 1 :]
        in_raw, out_raw = list(in_refs), list(out_refs)
        own, rest = rest[: len(scratch)], rest[len(scratch) :]
        space, signals = rest[: len(buffers)], rest[len(buffers) :]

        def run():
            arrivals, departures = [], []
            for at, k in enumerate(far_in):
                in_refs[k] = Arriving(in_refs[k], ins[k].index, space[at], signals[at])
                arrivals.append(in_refs[k])
                if not ins[k].later:
                    in_refs[k].start()
            for at, k in enumerate(far_out, len(far_in)):
                out_refs[k] = Leaving(out_refs[k], space[at], signals[at])
                departures.append(out_refs[k])
            body(scal, *in_refs, *out_refs, *own)
            for a in arrivals:
                a.ready()
            for d in departures:
                d.send()
            for d in departures:
                d.copy.wait()

        if active is None:
            run()
        else:
            pl.when(scal[1] == active)(run)
        if passing is not None:
            given, made = passing
            at = len(far_in) + far_out.index(made)

            @pl.when(scal[1] != active)
            def _():
                for source, target in ((in_raw[given], space[at]), (space[at], out_raw[made])):
                    copy = pltpu.make_async_copy(source, target, signals[at])
                    copy.start()
                    copy.wait()

    specs = [HB if isinstance(x, (Far, Raw)) else VM for x in ins]
    arrays = [pinned(x.array) if isinstance(x, (Far, Raw)) else x for x in ins]
    return pl.pallas_call(
        whole,
        out_shape=shapes,
        in_specs=[SM] + specs + [HB if stays(a) else ANY for a in after],
        out_specs=[HB if len(x) > 2 and x[2] else VM for x in outs] + [HB],
        scratch_shapes=list(scratch) + buffers + sems,
        compiler_params=pltpu.CompilerParams(vmem_limit_bytes=held + (extra << 20)),
        cost_estimate=pl.CostEstimate(flops=flops, bytes_accessed=moved, transcendentals=0),
        name=getattr(body, "func", body).__name__,
    )(scal, *arrays, *[pinned(a) if stays(a) else a for a in after])


def gains_body(micro, scal, *refs):
    out = refs[-1]
    ready_all(*refs[:-1])
    first, refs = refs[:micro], refs[micro : -1]
    out[0:1] = sum(r[...] for r in first)
    for section in (0, 1):

        @pl.when(scal[1] == section)
        def _():
            mine = refs[2 * micro * section : 2 * micro * (section + 1)]
            out[1:2] = sum(r[...] for r in mine[:micro])
            out[2:3] = sum(r[...] for r in mine[micro:])


def place_body(n, el, capp, scal, labels, *outs):
    me = scal[0]
    tokens = labels.shape[1]
    r = lax.broadcasted_iota(jnp.int32, (tokens, tokens), 0)
    c = lax.broadcasted_iota(jnp.int32, (tokens, tokens), 1)
    lower = (c < r).astype(BF)
    experts = n * el
    for m in range(labels.shape[0]):
        lab = labels[m]
        hot = lab == lax.broadcasted_iota(jnp.int32, (tokens, experts), 1)
        hot = jnp.where(hot, 1.0, 0.0)
        before = dot(lower, hot.astype(BF))
        slot = jnp.sum(before * hot, axis=1, keepdims=True).astype(jnp.int32)
        where = ((lab // el) ^ me) * (el * capp) + (lab % el) * capp + slot
        wide = jnp.where(
            where == lax.broadcasted_iota(jnp.int32, (tokens, n * el * capp), 1), 1.0, 0.0
        )
        outs[m][...] = wide.T.astype(BF)


def send_slots(d_ref, rows, outs):
    size = outs[0].shape[0]
    for j, out in enumerate(outs):
        out[...] = dot(d_ref[j * size : (j + 1) * size, :], rows).astype(BF)


def self_fwd_body(n, hl, hs, scal, *refs):
    xs, (gains, w), refs = refs[:n], refs[n : n + 2], refs[n + 2 :]
    a, qkv, o, lse = refs[:4]
    parts = refs[4:]
    me, dec = scal[0], scal[1]
    tokens = xs[0].shape[0]
    group = n * tokens
    hw = hl * hs
    g = gains[0, 0:1]
    for j in range(n):
        unit, _ = norm_parts(xs[j][...].astype(F32))
        a[pl.ds((me ^ j) * tokens, tokens), :] = (unit * g).astype(BF)
    a.send()
    qkv[...] = dot(a[...], w[:, : 3 * hw]).astype(BF)
    qkv.send()

    def run(causal):
        for base in range(0, group, SEQ):
            logs = {}
            for h in range(hl):
                cols = slice(h * hs, (h + 1) * hs)
                k = qkv[base : base + SEQ, hw + h * hs : hw + (h + 1) * hs]
                v = qkv[base : base + SEQ, 2 * hw + h * hs : 2 * hw + (h + 1) * hs]
                for first in range(0, SEQ, QB):
                    rows = slice(base + first, base + first + QB)
                    width = first + QB if causal else SEQ
                    o[rows, cols], logs[first, h] = attend_tile(
                        qkv[rows, cols], k[:width], v[:width], first if causal else None
                    )
            for first in range(0, SEQ, QB):
                lse[base + first : base + first + QB, :] = by_lane(
                    [logs[first, h] for h in range(hl)]
                )

    pl.when(dec == 1)(lambda: run(True))
    pl.when(dec == 0)(lambda: run(False))
    for j in range(n):
        rows = o[pl.ds((me ^ j) * tokens, tokens), :]
        parts[j][...] = dot(rows, w[:, 3 * hw :], 1, 1).astype(BF)


def self_bwd_body(n, hl, hs, add, scal, *refs):
    gs, refs = refs[:n], refs[n:]
    a, qkv, o, lse, gains, w = refs[:6]
    olds, refs = refs[6 : 6 + add], [*refs[:6], *refs[6 + add :]]
    parts, (dw, dgain) = refs[6 : 6 + n], refs[6 + n : 8 + n]
    dso, do, dqkv, ps, dss = refs[8 + n :]
    me, dec = scal[0], scal[1]
    tokens = gs[0].shape[0]
    group = n * tokens
    hw = hl * hs
    scale = hs**-0.5
    for j in range(n):
        dso[pl.ds((me ^ j) * tokens, tokens), :] = gs[j][...]
    do[...] = dot(dso[...], w[:, 3 * hw :]).astype(BF)
    ready_all(o, lse, qkv)
    start_all(a, *olds)

    def run(causal):
        for base in range(0, group, SEQ):
            keys = slice(base, base + SEQ)
            rows_of = [slice(base + f, base + f + QB) for f in range(0, SEQ, QB)]
            logs = [lse[rows, :].T for rows in rows_of]
            inners = [
                by_lane(
                    [
                        row_products(
                            do[rows, h * hs : (h + 1) * hs], o[rows, h * hs : (h + 1) * hs]
                        )
                        for h in range(hl)
                    ]
                ).T
                for rows in rows_of
            ]
            dqs = []
            for h in range(hl):
                cols = slice(h * hs, (h + 1) * hs)
                q, dh = qkv[keys, cols], do[keys, cols]
                k = qkv[keys, hw + h * hs : hw + (h + 1) * hs]
                v = qkv[keys, 2 * hw + h * hs : 2 * hw + (h + 1) * hs]
                for i, first in enumerate(range(0, SEQ, QB)):
                    width = first + QB if causal else SEQ
                    block = slice(first, first + QB)
                    p, ds = attend_tile_back(
                        q[block],
                        k[:width],
                        v[:width],
                        dh[block],
                        logs[i][h : h + 1],
                        inners[i][h : h + 1],
                        first if causal else None,
                    )
                    ps[:width, block] = p
                    dss[:width, block] = ds
                kt = (k.astype(F32) * scale).astype(BF).T
                if causal:
                    dk = [dot(dss[f : f + QB, f:], q[f:]) for f in range(0, SEQ, QB)]
                    dv = [dot(ps[f : f + QB, f:], dh[f:]) for f in range(0, SEQ, QB)]
                    dk, dv = jnp.concatenate(dk, axis=0), jnp.concatenate(dv, axis=0)
                    dq = [
                        dot(kt[:, : f + QB], dss[: f + QB, f : f + QB]) for f in range(0, SEQ, QB)
                    ]
                    dqs.append(jnp.concatenate(dq, axis=1))
                else:
                    dk, dv = dot(dss[...], q), dot(ps[...], dh)
                    dqs.append(dot(kt, dss[...]))
                dqkv[keys, hw + h * hs : hw + (h + 1) * hs] = (dk * scale).astype(BF)
                dqkv[keys, 2 * hw + h * hs : 2 * hw + (h + 1) * hs] = dv.astype(BF)
            dqkv[keys, :hw] = jnp.concatenate(dqs, axis=0).T.astype(BF)

    pl.when(dec == 1)(lambda: run(True))
    pl.when(dec == 0)(lambda: run(False))
    total = jnp.zeros((1, a.shape[1]), F32)
    for j in range(n):
        rows = pl.ds((me ^ j) * tokens, tokens)
        da = dot(dqkv[rows, :], w[:, : 3 * hw], 1, 1)
        parts[j][...] = da.astype(BF)
        total += jnp.sum(da * a[rows, :].astype(F32), axis=0, keepdims=True)
    dgain[...] = total / gains[0, 0:1]
    grads = dot(a[...], dqkv[...], 0, 0), dot(dso[...], o[...], 0, 0)
    for h in range(hl):
        for t in range(4):
            at = (t % 3) * hw + h * hs
            to = slice((4 * h + t) * hs, (4 * h + t + 1) * hs)
            part = grads[0][:, at : at + hs] if t < 3 else grads[1][:, h * hs : (h + 1) * hs]
            dw[:, to] = ((part + olds[0][:, to]) if add else part).astype(dw.dtype)


def after_self_body(n, pieces, scal, *refs):
    x, refs = refs[0], refs[1:]
    ps, (gains, d, cot), (h1,), outs = (
        refs[:pieces],
        refs[pieces : pieces + 3],
        refs[pieces + 3 : pieces + 4],
        refs[pieces + 4 :],
    )
    rows = x[...].astype(F32)
    for p in ps:
        rows = rows + p[...].astype(F32)
    h1[...] = rows
    h1.send()
    unit, _ = norm_parts(rows)
    u = (unit * gains[0, 2:3]).astype(BF)
    chosen = jnp.where(scal[1] == 0, u.astype(F32), cot[...].astype(F32)).astype(BF)
    send_slots(d, chosen, outs)


def memory_body(n, scal, *refs):
    rs, (h1, d, gains), (y, m) = refs[:n], refs[n : n + 3], refs[n + 3 :]
    stacked = jnp.concatenate([r[...] for r in rs], axis=0)
    rows = h1[...] + dot(d[...], stacked, 0, 0)
    y[...] = rows
    y.send()
    unit, _ = norm_parts(rows)
    m[...] = (unit * gains[0, 1:2]).astype(BF)


def final_body(n, micro, scal, *refs):
    out = refs[-1]
    for m in range(micro):
        rs, (h2, d, ye) = refs[:n], refs[n : n + 3]
        refs = refs[n + 3 :]
        ready_all(h2, d, ye)

        @pl.when(scal[1] == 0)
        def _():
            out[0, m] = ye[...].astype(BF)

        @pl.when(scal[1] == 1)
        def _():
            stacked = jnp.concatenate([r[...] for r in rs], axis=0)
            out[0, m] = (h2[...] + dot(d[...], stacked, 0, 0)).astype(BF)


def cross_fwd_body(n, per, hl, hs, scal, *refs):
    ms, refs = refs[:per], refs[per:]
    wx, wkv, (h1, gains, d), refs = refs[:n], refs[n : 2 * n], refs[2 * n : 2 * n + 3], refs[2 * n + 3 :]
    h2, c, mem, qc, kv, oc, lse = refs[:7]
    outs = refs[7:]
    hw = hl * hs
    tokens = h1.shape[0]
    for j in range(per):
        mem[j * tokens : (j + 1) * tokens, :] = ms[j][...]
    mem.send()
    unit, _ = norm_parts(h1[...])
    start_all(*wkv)
    c[...] = (unit * gains[0, 1:2]).astype(BF)
    c.send()
    for j in range(n):
        qc[:, j * hw : (j + 1) * hw] = dot(c[...], wx[j][:, :hw]).astype(BF)
    qc.send()
    for j in range(n):
        kv[:, 2 * j * hw : 2 * (j + 1) * hw] = dot(mem[...], wkv[j][...]).astype(BF)
    kv.send()
    total = h1[...]
    logs = []
    for j in range(n):
        for h in range(hl):
            at = j * hw + h * hs
            k = kv[:, 2 * j * hw + h * hs : 2 * j * hw + (h + 1) * hs]
            v = kv[:, (2 * j + 1) * hw + h * hs : (2 * j + 1) * hw + (h + 1) * hs]
            oc[:, at : at + hs], log = attend_tile(qc[:, at : at + hs], k, v, None)
            logs.append(log)
        total = total + dot(oc[:, j * hw : (j + 1) * hw], wx[j][:, hw:], 1, 1)
    oc.send()
    lse[...] = by_lane(logs)
    lse.send()
    h2[...] = total
    h2.send()
    unit, _ = norm_parts(total)
    send_slots(d, (unit * gains[0, 2:3]).astype(BF), outs)


def cross_bwd_body(n, per, hl, hs, scal, *refs):
    dus, wx, wkv, refs = refs[:n], refs[n : 2 * n], refs[2 * n : 3 * n], refs[3 * n :]
    h2, gains, d, cot, qc, kv, oc, lse = refs[:8]
    refs = refs[8:]
    dh2, dco, dqc, dkv, dgain = refs[:5]
    dms, (doc,) = refs[5 : 5 + per], refs[5 + per :]
    hw = hl * hs
    tokens = h2.shape[0]
    stacked = jnp.concatenate([r[...] for r in dus], axis=0)
    unit, inverse = norm_parts(h2[...])
    start_all(*wx, oc, lse, qc, kv, *wkv)
    back, gained = norm_back(dot(d[...], stacked, 0, 0), unit, inverse, gains[0, 2:3])
    dgain[...] = gained
    total = cot[...].astype(F32) + back
    dh2[...] = total
    dh2.send()
    dco[...] = total.astype(BF)
    dco.send()
    for j in range(n):
        doc[:, j * hw : (j + 1) * hw] = dot(dco[...], wx[j][:, hw:]).astype(BF)
    logs = lse[...].T
    places = [slice(i * hs, (i + 1) * hs) for i in range(n * hl)]
    inner = by_lane([row_products(doc[:, at], oc[:, at]) for at in places]).T
    scale = hs**-0.5
    dqs = []
    for i, at in enumerate(places):
        j, h = i // hl, i % hl
        k_at = slice(2 * j * hw + h * hs, 2 * j * hw + (h + 1) * hs)
        v_at = slice((2 * j + 1) * hw + h * hs, (2 * j + 1) * hw + (h + 1) * hs)
        q, k, do = qc[:, at], kv[:, k_at], doc[:, at]
        p, ds = attend_tile_back(q, k, kv[:, v_at], do, logs[i : i + 1], inner[i : i + 1], None)
        dkv[:, k_at] = (dot(ds, q) * scale).astype(BF)
        dkv[:, v_at] = dot(p, do).astype(BF)
        dqs.append(dot((k.astype(F32) * scale).astype(BF).T, ds))
    dkv.send()
    dqc[...] = jnp.concatenate(dqs, axis=0).T.astype(BF)
    dqc.send()
    for i in range(per):
        rows = slice(i * tokens, (i + 1) * tokens)
        total = 0.0
        for j in range(n):
            total += dot(dkv[rows, 2 * j * hw : 2 * (j + 1) * hw], wkv[j][...], 1, 1)
        dms[i][...] = total.astype(BF)


def cross_late_body(n, hl, hs, count, scal, *refs):
    wx, (dh2, dco, dqc, dkv, oc, c, mem, h1, gains) = refs[:n], refs[n : n + 9]
    olds, refs = refs[n + 9 : n + 9 + count], refs[n + 9 + count :]
    dh1, dgain, dws = refs[0], refs[1], refs[2:]
    hw = hl * hs
    dc = jnp.zeros(h1.shape, F32)
    for j in range(n):
        dc += dot(dqc[:, j * hw : (j + 1) * hw], wx[j][:, :hw], 1, 1)
    unit, inverse = norm_parts(h1[...])
    back, gained = norm_back(dc, unit, inverse, gains[0, 1:2])
    dh1[...] = dh2[...] + back
    dh1.send()
    dgain[...] = gained
    ct, dt, mt = c[...].T, dco[...].T, mem[...].T
    for j in range(n):
        dq = dot(ct, dqc[:, j * hw : (j + 1) * hw])
        de = dot(dt, oc[:, j * hw : (j + 1) * hw])
        dkv_j = dot(mt, dkv[:, 2 * j * hw : 2 * (j + 1) * hw])
        for h in range(hl):
            at = slice(h * hs, (h + 1) * hs)
            parts = dq[:, at], de[:, at], dkv_j[:, at], dkv_j[:, hw + h * hs : hw + (h + 1) * hs]
            for t, part in enumerate(parts):
                to = (t // 2) * 2 * hw + (2 * h + t % 2) * hs
                if count:
                    part = part + olds[j][:, to : to + hs].astype(F32)
                dws[j][:, to : to + hs] = part.astype(BF)


def sum_body(scal, *refs):
    total = refs[0][...].astype(F32)
    for ref in refs[1:-1]:
        total = total + ref[...].astype(F32)
    refs[-1][...] = total.astype(refs[-1].dtype)


def halves_body(scal, *refs):
    *parts, left, right = refs
    total = parts[0][...].astype(F32)
    for ref in parts[1:]:
        total = total + ref[...].astype(F32)
    half = total.shape[1] // 2
    left[...] = total[:, :half].astype(BF)
    right[...] = total[:, half:].astype(BF)


def pick_body(scal, first, second, out):
    out[...] = jnp.where(scal[1] == 1, first[...].astype(F32), second[...].astype(F32)).astype(BF)


def memory_back_body(n, scal, *refs):
    (dm, y, gains, cot, d), (dy, dgain), outs = refs[:5], refs[5:7], refs[7:]
    unit, inverse = norm_parts(y[...])
    back, gained = norm_back(dm[...].astype(F32), unit, inverse, gains[0, 1:2])
    dgain[...] = gained
    rows = cot[...].astype(F32) + back
    dy[...] = rows
    dy.send()
    send_slots(d, rows.astype(BF), outs)


def before_self_body(n, scal, *refs):
    dus, (d, dy, h1, gains, given), (dh1, dso, dgain) = refs[:n], refs[n : n + 5], refs[n + 5 :]
    ready_all(gains, h1, d, dy, given)

    @pl.when(scal[1] == 0)
    def _():
        stacked = jnp.concatenate([r[...] for r in dus], axis=0)
        unit, inverse = norm_parts(h1[...])
        back, gained = norm_back(dot(d[...], stacked, 0, 0), unit, inverse, gains[0, 2:3])
        rows = dy[...] + back
        dh1[...] = rows
        dso[...] = rows.astype(BF)
        dgain[...] = gained

    @pl.when(scal[1] == 1)
    def _():
        dh1[...] = given[...]
        dso[...] = given[...].astype(BF)
        dgain[...] = jnp.zeros(dgain.shape, F32)


def finish_body(pieces, micro, scal, *refs):
    gains, out, refs = refs[0], refs[-1], refs[1:-1]
    for m in range(micro):
        ps, (dh1, x), refs = refs[:pieces], refs[pieces : pieces + 2], refs[pieces + 2 :]
        da = ps[0][...].astype(F32)
        for p in ps[1:]:
            da = da + p[...].astype(F32)
        unit, inverse = norm_parts(x[...].astype(F32))
        back, _ = norm_back(da, unit, inverse, gains[0, 0:1])
        out[0, m] = dh1[...] + back


def gelu_low(z):
    z = z.astype(BF)

    def c(value):
        return jnp.asarray(value, BF)

    inner = c(ROOT) + c(ROOT * 0.044715) * (z * z)
    half = c(0.5) + c(0.5) * jnp.tanh(z * inner)
    value = z * half
    return value, half + (value - value * half) * (c(6.0) * inner - c(4.0 * ROOT))


def expert_body(n, el, capp, block, mode, passed, scal, *refs):
    us, refs = refs[:n], refs[n:]
    drs = ()
    if mode != "fwd":
        drs, refs = refs[:n], refs[n:]
    (wi, wo), refs = refs[:2], refs[2 + passed :]
    rs, dus = (), ()
    if mode != "back":
        rs, refs = refs[:n], refs[n:]
    if mode != "fwd":
        dus, refs = refs[:n], refs[n:]
    u_all = dr_all = None
    if mode != "back":
        u_all, refs = refs[0], refs[1:]
    if mode != "fwd":
        dr_all, refs = refs[0], refs[1:]
    ff = wi.shape[3]
    rows_u = [
        jnp.concatenate([us[j][e * capp : (e + 1) * capp, :] for j in range(n)], axis=0)
        for e in range(el)
    ]
    rows_dr = [
        jnp.concatenate([drs[j][e * capp : (e + 1) * capp, :] for j in range(n)], axis=0)
        for e in range(el if drs else 0)
    ]
    for e in range(el):
        if u_all is not None:
            u_all[e] = rows_u[e]
        if dr_all is not None:
            dr_all[e] = rows_dr[e]
    for ref in (u_all, dr_all):
        if ref is not None:
            ref.send()
    for e in range(el):
        racc = dacc = 0.0
        for f in range(0, ff, block):
            part = slice(f, f + block)
            wi_f, wo_f = wi[0, e, :, part], wo[0, e, part, :]
            z = dot(rows_u[e], wi_f)
            if drs:
                g, slope = (gelu_low if CFG.get("low") else gelu_parts)(z)
            else:
                g = gelu_value(z)
            if rs:
                racc += dot(g.astype(BF), wo_f)
            if dus:
                dz = (dot(rows_dr[e], wo_f, 1, 1).astype(slope.dtype) * slope).astype(BF)
                dacc += dot(dz, wi_f, 1, 1)
        for j in range(n):
            part, at = slice(j * capp, (j + 1) * capp), slice(e * capp, (e + 1) * capp)
            if rs:
                rs[j][at, :] = racc[part].astype(BF)
            if dus:
                dus[j][at, :] = dacc[part].astype(BF)


def experts(step, us, drs, w_in, w_out, capp, active, mode, other=None):
    n, el = len(us), w_in.shape[1]
    width, ff = w_in.shape[2:]
    block = 1024
    outs = n * (2 if mode == "both" else 1)
    products = {"fwd": 2, "both": 4, "back": 3}[mode]
    result = step(
        functools.partial(expert_body, n, el, capp, block, mode, int(other is not None)),
        [*us, *drs, w_in, w_out, *([] if other is None else [Raw(other)])],
        [((el * capp, width), BF)] * outs
        + [((el, n * capp, width), BF, True)] * (2 if mode == "both" else 1),
        flops=products * 2 * el * n * capp * width * ff,
        active=active,
        passing=None if other is None else (len(us) + len(drs) + 2, outs),
    )
    return [result[i : i + n] for i in range(0, outs, n)], result[outs:]


def expert_grad_body(add, *refs):
    u_ref, dr_ref, wi, wo = refs[:4]
    refs = refs[4:]
    olds, refs = (refs[:2], refs[2:]) if add else ((), refs)
    dwi, dwo, ut = refs[-3:]
    lead, _, rows, width = u_ref.shape
    chunk = 1
    while 2 * chunk * rows <= 1024 and lead % (2 * chunk) == 0:
        chunk *= 2
    size = chunk * rows

    @pl.when(pl.program_id(1) == 0)
    def _():
        for at in range(0, lead, chunk):
            u = u_ref[at : at + chunk, 0].reshape(size, width)
            ut[:, at * rows : at * rows + size] = u.T

    for at in range(0, lead, chunk):
        u = u_ref[at : at + chunk, 0].reshape(size, width)
        dr = dr_ref[at : at + chunk, 0].reshape(size, width)
        g, slope = gelu_low(dot(u, wi[0, 0]))
        dz = dot(dr, wo[0, 0], 1, 1).astype(BF) * slope
        di = dot(ut[:, at * rows : at * rows + size], dz)
        do = dot(g, dr, 0, 0)
        if at:
            dwi[0, 0] += di
            dwo[0, 0] += do
        elif add:
            dwi[0, 0] = olds[0][0, 0] + di
            dwo[0, 0] = olds[1][0, 0] + do
        else:
            dwi[0, 0] = di
            dwo[0, 0] = do


def expert_grads(u, dr, w_in, w_out, olds, after, first, many, add):
    lead, _, rows, width = u.shape
    ff = w_in.shape[3]
    block = 512
    spec = pl.BlockSpec((lead, 1, rows, width), lambda e, f: (0, first + e, 0, 0))
    into = pl.BlockSpec((1, 1, width, block), lambda e, f: (0, first + e, 0, f))
    back = pl.BlockSpec((1, 1, block, width), lambda e, f: (0, first + e, f, 0))
    body = functools.partial(expert_grad_body, add)
    given = 4 + (len(olds) if add else 0)
    count = 4 + len(olds) + len(after)

    def trimmed(*refs):
        dwi, dwo, _, ut = refs[count:]
        body(*refs[:given], dwi, dwo, ut)

    arrays = [pinned(x) for x in (u, dr, w_in, w_out, *olds)]
    after = [pinned(a) if stays(a) else a for a in after]
    return pl.pallas_call(
        trimmed,
        grid=(many, ff // block),
        in_specs=[spec] * 2
        + [into, back]
        + ([into, back] if add else [HB, HB])[: len(olds)]
        + [HB if stays(a) else ANY for a in after],
        out_specs=[into, back, HB],
        out_shape=[
            pltpu.HBM(w_in.shape, F32),
            pltpu.HBM(w_out.shape, F32),
            pltpu.HBM((8, 128), F32),
        ],
        scratch_shapes=[pltpu.VMEM((width, lead * rows), BF)],
        input_output_aliases={4: 0, 5: 1} if olds else {},
        compiler_params=pltpu.CompilerParams(
            vmem_limit_bytes=(22 << 20) + 10 * lead * rows * width
        ),
        cost_estimate=pl.CostEstimate(
            flops=8 * lead * many * rows * width * ff, bytes_accessed=0, transcendentals=0
        ),
        name="expert_grads",
    )(*arrays, *after)


def on_device(inputs, cotangent, expert_ids, self_proj, cross_proj, gains, w_in, w_out):
    micro, tokens, width = inputs.shape[1:]
    n = lax.axis_size("mp")
    hl = self_proj.shape[2]
    hs = self_proj.shape[3] // 4
    hw = hl * hs
    el = w_in.shape[1]
    capacity = max(2, 3 * tokens // (2 * n * el))
    capp = -(-capacity // 16) * 16
    slots = el * capp
    per = SEQ // tokens
    group = n * tokens
    M = range(micro)
    decoder = lax.axis_index("section") == 1
    scal = jnp.stack([lax.axis_index("mp"), lax.axis_index("section")]).astype(jnp.int32)
    last = []

    def step(body, ins, outs, **more):
        *res, token = call(body, scal, ins, outs, after=list(last), **more)
        last[:] = [token]
        return res

    def swap(x, k, sections=(0, 1)):
        pairs = [(s * n + i, s * n + (i ^ k)) for s in sections for i in range(n)]
        return lax.ppermute(x, ("section", "mp"), pairs)

    def gather(x, count, sections=(0, 1), gated=False):
        blocks = {0: x}
        bit = count // 2
        while bit:
            blocks.update({j ^ bit: swap(b, bit, sections) for j, b in list(blocks.items())})
            if gated and bit == count // 2:
                (blocks[bit],) = gate([blocks[bit]])
            bit //= 2
        return [blocks[j] for j in range(count)]

    def total(pieces, dtype):
        return call(sum_body, scal, pieces, [(pieces[0].shape, dtype)])[0]

    def scatter(blocks, hold=False, sections=(0, 1)):
        live = {j: [b] for j, b in enumerate(blocks)}
        bit = 1
        while bit < len(blocks):
            for j in [j for j in live if j & bit]:
                pieces = live.pop(j)
                out = pieces[0]
                if len(pieces) > 1:
                    out = sum(p.astype(F32) for p in pieces).astype(BF)
                    if hold:
                        last.append(out)
                live[j ^ bit].append(swap(out, bit, sections))
            bit *= 2
        return live[0]

    def exchange(blocks):
        return [blocks[0]] + [swap(blocks[j], j) for j in range(1, n)]

    def gate(arrays, waits=(), space=ANY):
        count = len(arrays)
        waits = [*last, *waits]
        *arrays, token = pl.pallas_call(
            lambda *refs: None,
            out_shape=[
                (pltpu.HBM if space is HB else jax.ShapeDtypeStruct)(a.shape, a.dtype)
                for a in arrays
            ]
            + [pltpu.HBM((8, 128), F32)],
            in_specs=[space] * count + [HB if stays(a) else ANY for a in waits],
            out_specs=[space] * count + [HB],
            input_output_aliases={i: i for i in range(count)},
            compiler_params=pltpu.CompilerParams(vmem_limit_bytes=1 << 20),
            name="gate",
        )(
            *[pinned(a) if space is HB else a for a in arrays],
            *[pinned(a) if stays(a) else a for a in waits],
        )
        last[:] = [token]
        return arrays

    def lazy(fars):
        return [Far(f.array, *f.index, later=True) for f in fars]

    def to_decoder(x):
        return lax.ppermute(x, "section", [(0, 1)])

    def to_encoder(x):
        return lax.ppermute(x, "section", [(1, 0)])

    xs = [inputs[0, m] for m in M]
    ws = self_proj[0].reshape(width, hl, 4, hs).transpose(0, 2, 1, 3).reshape(width, 4 * hw)
    wc = cross_proj[0].reshape(width, hl, 2, hs).transpose(0, 2, 1, 3).reshape(width, 2 * hw)
    row, wide, line = ((tokens, width), BF), ((tokens, width), F32, True), ((1, width), F32, True)
    slot = ((slots, width), BF)

    def far(shape, dtype=BF):
        return (shape, dtype, True)

    last.extend([ws, wc])
    routes = step(
        functools.partial(place_body, n, el, capp),
        [expert_ids[0]],
        [far((n * slots, tokens))] * micro,
    )
    routes = [Far(r) for r in routes]
    gain = Far(gains)
    x_far = [Far(inputs, 0, m) for m in M]
    cots = [Far(cotangent, 0, m) for m in M]

    x_all = [gather(xs[m], n, gated=m == 0) for m in M]
    saved, self_parts = [], []
    for m in M:
        res = step(
            functools.partial(self_fwd_body, n, hl, hs),
            [*x_all[m], gain, Far(ws)],
            [
                far((group, width)),
                far((group, 3 * hw)),
                far((group, hw)),
                far((group, 128), F32),
            ]
            + [row] * n,
            flops=2 * group * width * 4 * hw + 4 * 4 * group * SEQ * hw,
        )
        saved.append(res[:4])
        parts = res[4:]
        if m:
            last.extend(self_parts[-1])
            parts = gate(parts)
        self_parts.append(scatter(parts, m < micro - 1))
    h1, first_slots, ye, mem_all, rs, enc_u = [], [], [], [], [], []

    def after_self(m):
        res = step(
            functools.partial(after_self_body, n, len(self_parts[m])),
            [x_far[m], *self_parts[m], gain, routes[m], cots[m]],
            [wide] + [slot] * n,
            flops=2 * n * slots * tokens * width,
        )
        h1.append(Far(res[0]))
        first_slots.append(exchange(res[1:]))

    def encoder_experts(m):
        (r,), (u,) = experts(step, first_slots[m], (), w_in, w_out, capp, 0, "fwd")
        rs.append(exchange(r))
        enc_u.append(u)

    def memory(m):
        y, mem = step(
            functools.partial(memory_body, n),
            [*rs[m], h1[m], routes[m], gain],
            [wide, row],
            flops=2 * n * slots * tokens * width,
            active=0,
        )
        ye.append(Far(y))
        mem_all.append(to_decoder(mem))

    if CFG.get("eorder") == 1:
        for m in M:
            after_self(m)
            encoder_experts(m)
            if m:
                memory(m - 1)
        memory(micro - 1)
    elif CFG.get("eorder") == 2:
        after_self(0)
        for m in M:
            encoder_experts(m)
            if m < micro - 1:
                after_self(m + 1)
            memory(m)
    else:
        for m in M:
            after_self(m)
        for m in M:
            encoder_experts(m)
        for m in M:
            memory(m)
    if CFG.get("wlast", 1):
        wx_all = [Far(b) for b in gather(wc, n, (1,))]
        wkv_all = [Far(b, later=True) for b in gather(to_decoder(wc), n, (1,))]

    crossed, second_slots, mem_got = [], [], [gather(mem_all[0], per)]
    rs, dus, dec_u, dec_dr = [], [], [], []
    late, gain_parts, kept, pieces, dms = [], [[], [], []], [], [], []

    def cross(m):
        if m:
            mem_got.append(gather(mem_all[m], per))
        res = step(
            functools.partial(cross_fwd_body, n, per, hl, hs),
            [*mem_got[m], *([f.array for f in (*wx_all, *wkv_all)] if CFG.get("dvm") else (*wx_all, *wkv_all)), h1[m], gain, routes[m]],
            [
                wide,
                far((tokens, width)),
                far((SEQ, width)),
                far((tokens, n * hw)),
                far((SEQ, 2 * n * hw)),
                far((tokens, n * hw)),
                far((tokens, 128), F32),
            ]
            + [slot] * n,
            flops=4 * SEQ * width * n * hw + 4 * 4 * tokens * SEQ * n * hw,
            active=1,
        )
        crossed.append([Far(r) for r in res[:7]])
        second_slots.append(exchange(res[7:]))

    def decoder_experts(m):
        (r, du), (u, dr) = experts(
            step,
            second_slots[m],
            [Far(b) for b in first_slots[m]],
            w_in,
            w_out,
            capp,
            1,
            "both",
            enc_u[m],
        )
        dus.append(exchange(du))
        rs.append(r)
        dec_u.append(u)
        dec_dr.append(dr)

    def cross_back(m):
        h2, c, mem, qc, kv, oc, lse = crossed[m]
        res = step(
            functools.partial(cross_bwd_body, n, per, hl, hs),
            [*dus[m], *([f.array for f in (*wx_all, *wkv_all)] if CFG.get("fvm") else (*lazy(wx_all), *wkv_all)), h2, gain, routes[m], cots[m]]
            + lazy((qc, kv, oc, lse)),
            [wide, far((tokens, width)), far((tokens, n * hw)), far((SEQ, 2 * n * hw)), line]
            + [row] * per,
            scratch=[pltpu.VMEM((tokens, n * hw), BF)],
            flops=4 * SEQ * width * n * hw + 4 * 10 * tokens * SEQ * n * hw,
            active=1,
        )
        kept.append([Far(r) for r in res[:4]])
        gain_parts[2].append(res[4])
        parts = res[5:]
        if m and CFG.get("pgate", 1):
            last.extend(pieces[-1])
            parts = gate(parts)
        pieces.append(scatter(parts, m < micro - 1))
        dms.append(to_encoder(sum(p.astype(F32) for p in pieces[m]).astype(BF)))

    if CFG.get("order") == 1:
        cross(0)
        decoder_experts(0)
        for m in range(1, micro):
            cross(m)
            cross_back(m - 1)
            decoder_experts(m)
        cross_back(micro - 1)
    elif CFG.get("order") == 2:
        for m in M:
            cross(m)
        for m in M:
            decoder_experts(m)
            cross_back(m)
    else:
        for m in M:
            cross(m)
        for m in M:
            decoder_experts(m)
        for m in M:
            cross_back(m)

    def rows_of(encoder_rows, decoder_rows, forward=False):
        whole = (decoder_rows if forward else encoder_rows)[None]
        return lax.all_gather(whole, "dp", axis=0, tiled=True)

    u_rows = [rows_of(enc_u[m], dec_u[m], True) for m in M]

    dso_raw = []
    memory_gain, dr_rows, dh1, dso, parts_a, self_total = [], [], [], [], [], None

    def experts_back(m):
        res = step(
            functools.partial(memory_back_body, n),
            [dms[m], ye[m], gain, cots[m], routes[m]],
            [wide, line] + [slot] * n,
            active=0,
        )
        memory_gain.append(res[1])
        third = exchange(res[2:])
        (du,), (dr,) = experts(
            step,
            [Far(b) for b in first_slots[m]],
            third,
            w_in,
            w_out,
            capp,
            0,
            "back",
            dec_dr[m],
        )
        dr_rows.append(rows_of(dr, dec_dr[m]))
        return res[0], exchange(du)

    def cross_late(m):
        h2, c, mem, qc, kv, oc, lse = crossed[m]
        olds = late[m - 1][2:] if m else []
        late.append(
            step(
                functools.partial(cross_late_body, n, hl, hs, len(olds)),
                [*wx_all, *kept[m], oc, c, mem, h1[m], gain, *[Far(x) for x in olds]],
                [wide, line] + [far((width, 4 * hw))] * n,
                flops=8 * SEQ * width * n * hw,
                active=1,
            )
        )

    def before_self(m, dy, du):
        res = step(
            functools.partial(before_self_body, n),
            [*du, routes[m], Far(dy), h1[m], gain, Far(late[m][0])],
            [wide, row, line],
        )
        dh1.append(res[0])
        dso_raw.append(res[1])
        dso.append(gather(res[1], n) if m < micro - 1 or not CFG.get("w0") else None)
        gain_parts[2].append(res[2])

    def self_back(m, before):
        a, qkv, o, lse = saved[m]
        res = step(
            functools.partial(self_bwd_body, n, hl, hs, bool(before)),
            [*dso[m], Far(a, later=True)]
            + [Far(x) for x in (qkv, o, lse)]
            + [gain, Far(ws)]
            + [Far(x, later=True) for x in before],
            [row] * n + [far((width, 4 * hw), BF if m == micro - 1 else F32), line],
            scratch=[
                pltpu.VMEM((group, width), BF),
                pltpu.VMEM((group, hw), BF),
                pltpu.VMEM((group, 3 * hw), BF),
                pltpu.VMEM((SEQ, SEQ), BF),
                pltpu.VMEM((SEQ, SEQ), BF),
            ],
            flops=2 * group * width * 8 * hw + 4 * 10 * group * SEQ * hw,
        )
        parts_a.append(scatter(res[:n], m < micro - 1))
        gain_parts[0].append(res[n + 1])
        return [res[n]]

    totals = []

    def grads_of(m, first, many):
        *new, token = expert_grads(
            u_rows[m], dr_rows[m], w_in, w_out, totals, list(last), first, many, m > 0
        )
        totals[:], last[:] = new, [token]

    only = (1,) if CFG.get("donly") else (0, 1)
    grads = []
    for m in M:
        dy, du = experts_back(m)
        if m:
            grads = self_back(m - 1, grads)
            if not CFG.get("late"):
                cross_late(m)
        else:
            cross_late(0)
            if CFG.get("late"):
                cross_late(1)
                cross_pieces = scatter(late[-1][2:], False, only)
        before_self(m, dy, du)
    if not CFG.get("late"):
        cross_pieces = scatter(late[-1][2:], False, only)
    if CFG.get("early"):
        own, remote = step(halves_body, cross_pieces, [((width, 2 * hw), BF)] * 2)
        remote = to_encoder(remote)
    if CFG.get("w0"):
        grads_of(0, 0, 1)
        dso[-1] = gather(dso_raw[-1], n, gated=True)
    elif CFG.get("lazyd"):
        dso[-1] = gather(dso_raw[-1], n)
    grads = self_back(micro - 1, grads)
    if not CFG.get("early"):
        own, remote = step(halves_body, cross_pieces, [((width, 2 * hw), BF)] * 2)
        remote = to_encoder(remote)
    else:
        (cross_total,) = step(pick_body, [own, remote], [far((width, 2 * hw))])
        sums = lax.psum(tuple(gate([*grads, cross_total], [*u_rows, *dr_rows], HB)), "dp")
        sums = lax.optimization_barrier(sums)
    (gain_total,) = step(
        functools.partial(gains_body, micro),
        [Far(g) for g in (*gain_parts[0], *memory_gain, *gain_parts[2][micro:])]
        + [Far(g) for g in (*[x[1] for x in late], *gain_parts[2][:micro])],
        [((3, width), F32)],
    )

    hops = [(axis, 1 << b) for axis in ("mp", "dp") for b in range(lax.axis_size(axis).bit_length() - 1)]

    def hop(x):
        axis, bit = hops.pop(0)
        return x, lax.ppermute(x, axis, [(i, i ^ bit) for i in range(lax.axis_size(axis))])

    def land(pair):
        return step(sum_body, pair, [((3, width), F32)])[0]

    pair = hop(gain_total)
    if not CFG.get("w0"):
        grads_of(0, 0, 1)
    if not CFG.get("early"):
        (cross_total,) = step(pick_body, [own, remote], [far((width, 2 * hw))])
        sums = lax.psum(tuple(gate([*grads, cross_total], [*u_rows, *dr_rows], HB)), "dp")
        sums = lax.optimization_barrier(sums)
    pair = hop(land(pair))
    rs[0] = exchange(gate(rs[0]))
    grads_of(0, 1, el - 1)
    (input_grads,) = step(
        functools.partial(finish_body, len(parts_a[0]), micro),
        [gain] + [x for i in M for x in (*parts_a[i], Far(dh1[i]), x_far[i])],
        [((1, micro, tokens, width), F32, True)],
    )
    rs[1:] = [exchange(r) for r in rs[1:]]
    for m in range(1, micro):
        for e in range(el):
            pair = hop(land(pair))
            grads_of(m, e, 1)
            if m == 1 and e == 0:
                (outs,) = step(
                    functools.partial(final_body, n, micro),
                    [x for m in M for x in (*rs[m], crossed[m][0], routes[m], ye[m])],
                    [((1, micro, tokens, width), BF, True)],
                )
    gain_total = land(pair)
    while hops:
        gain_total = land(hop(gain_total))
    first_total, second_total = totals
    self_total = sums[0].astype(F32).reshape(width, hl, 4 * hs)
    cross_total = sums[1].astype(F32).reshape(width, hl, 2 * hs)
    return (
        outs,
        input_grads,
        self_total[None],
        cross_total[None],
        gain_total[None],
        first_total,
        second_total,
    )


def solution(mesh):
    rows = P("section", None, ("dp", "mp"), None)
    heads = P("section", None, "mp", None)
    expert = P("section", "mp", None, None)
    return jax.shard_map(
        on_device,
        mesh=mesh,
        in_specs=(rows, rows, rows, heads, heads, P("section", None, None), expert, expert),
        out_specs=(rows, rows, heads, heads, P("section", None, None), expert, expert),
        check_vma=False,
    )
```

```python
import functools

import jax
import jax.numpy as jnp
from jax import lax
from jax.experimental import pallas as pl
from jax.experimental.pallas import tpu as pltpu
from jax.sharding import PartitionSpec as P

SEQ = 1024
EPS = 1e-05
ROOT = 0.7978845608028654
NEG = -1000000000.0
BF = jnp.bfloat16
F32 = jnp.float32
QB = 256


def dot(a, b, ca=1, cb=0):
    return lax.dot_general(a, b, (((ca,), (cb,)), ((), ())), preferred_element_type=F32)


def norm_parts(rows):
    centred = rows - jnp.mean(rows, axis=-1, keepdims=True)
    inverse = lax.rsqrt(jnp.mean(centred * centred, axis=-1, keepdims=True) + EPS)
    return centred * inverse, inverse


def norm_back(upstream, unit, inverse, gain):
    scaled = upstream * gain
    inner = (
        scaled
        - jnp.mean(scaled, axis=-1, keepdims=True)
        - unit * jnp.mean(scaled * unit, axis=-1, keepdims=True)
    )
    return inverse * inner, jnp.sum(upstream * unit, axis=0, keepdims=True)


def gelu_parts(z):
    square = z * z
    t = jnp.tanh(z * (0.7978845608028654 + (0.7978845608028654 * 0.044715) * square))
    half = 0.5 + 0.5 * t
    slope = half + (0.5 * z) * (1.0 - t * t) * (
        0.7978845608028654 + (3.0 * 0.7978845608028654 * 0.044715) * square
    )
    return z * half, slope


def gelu_value(z):
    t = jnp.tanh(z * (0.7978845608028654 + (0.7978845608028654 * 0.044715) * (z * z)))
    return z * (0.5 + 0.5 * t)


LOG2E = 1.4426950408889634


def attend_tile(q, k, v, first):
    s = dot(q, k, 1, 1) * (q.shape[1] ** -0.5 * LOG2E)
    if first is not None:
        r = lax.broadcasted_iota(jnp.int32, s.shape, 0) + first
        s = jnp.where(lax.broadcasted_iota(jnp.int32, s.shape, 1) <= r, s, NEG)
    peak = jnp.max(s, axis=-1, keepdims=True)
    p = jnp.exp2(s - peak)
    total = jnp.sum(p, axis=-1, keepdims=True)
    o = dot(p.astype(BF), v) / total
    return o.astype(BF), peak + jnp.log2(total)


def attend_tile_back(q, k, v, do, lse, inner, first):
    s = dot(k, q, 1, 1) * (q.shape[1] ** -0.5 * LOG2E)
    if first is not None:
        c = lax.broadcasted_iota(jnp.int32, s.shape, 1) + first
        s = jnp.where(lax.broadcasted_iota(jnp.int32, s.shape, 0) <= c, s, NEG)
    p = jnp.exp2(s - lse)
    ds = (p * (dot(v, do, 1, 1) - inner)).astype(BF)
    return p.astype(BF), ds


def by_lane(columns):
    lane = lax.broadcasted_iota(jnp.int32, (columns[0].shape[0], 128), 1)
    wide = jnp.zeros((columns[0].shape[0], 128), F32)
    for i, column in enumerate(columns):
        wide = jnp.where(lane == i, column, wide)
    return wide


def row_products(a, b):
    return jnp.sum(a.astype(F32) * b.astype(F32), axis=-1, keepdims=True)


SM = pl.BlockSpec(memory_space=pltpu.SMEM)
VM = pl.BlockSpec(memory_space=pltpu.VMEM)
HB = pl.BlockSpec(memory_space=pltpu.HBM)
ANY = pl.BlockSpec(memory_space=pl.ANY)


class Far:
    def __init__(self, array, *index, later=False):
        self.array, self.index, self.later = array, index, later
        self.shape, self.dtype = array.shape[len(index) :], array.dtype


class Raw:
    def __init__(self, array):
        self.array, self.shape, self.dtype = array, array.shape, array.dtype


class Arriving:
    def __init__(self, ref, index, buffer, sem):
        source = ref.at[index] if index else ref
        self.copy, self.buffer, self.waited = (
            pltpu.make_async_copy(source, buffer, sem),
            buffer,
            False,
        )
        self.shape = buffer.shape
        self.started = False

    def start(self):
        if not self.started:
            self.copy.start()
            self.started = True

    def ready(self):
        self.start()
        if not self.waited:
            self.copy.wait()
            self.waited = True
        return self.buffer

    def __getitem__(self, at):
        return self.ready()[at]


class Leaving:
    def __init__(self, ref, buffer, sem):
        self.copy, self.buffer, self.sent = pltpu.make_async_copy(buffer, ref, sem), buffer, False
        self.shape, self.dtype = buffer.shape, buffer.dtype

    def send(self):
        if not self.sent:
            self.copy.start()
            self.sent = True

    def __getitem__(self, at):
        return self.buffer[at]

    def __setitem__(self, at, value):
        self.buffer[at] = value


def ready_all(*refs):
    for ref in refs:
        if isinstance(ref, Arriving):
            ref.ready()


def start_all(*refs):
    for ref in refs:
        if isinstance(ref, Arriving):
            ref.start()


def pinned(array):
    return pltpu.with_memory_space_constraint(array, pltpu.HBM)


def stays(array):
    return array.shape == (8, 128) or array.ndim > 2


def nbytes(shape, dtype):
    size = jnp.dtype(dtype).itemsize
    for x in shape[:-1]:
        size *= x
    return size * (-(-shape[-1] // 128) * 128)


def call(
    body, scal, ins, outs, scratch=(), flops=0, extra=13, after=(), active=None, passing=None
):
    far_in = [k for k, x in enumerate(ins) if isinstance(x, Far)]
    far_out = [k for k, x in enumerate(outs) if len(x) > 2 and x[2]]
    shapes = [
        jax.ShapeDtypeStruct(*x) if len(x) == 2 else pltpu.HBM(*x[:2]) if x[2] else pltpu.VMEM(*x[:2])
        for x in outs
    ]
    shapes.append(pltpu.HBM((8, 128), F32))
    buffers = [pltpu.VMEM(ins[k].shape, ins[k].dtype) for k in far_in]
    buffers += [pltpu.VMEM(outs[k][0], outs[k][1]) for k in far_out]
    sems = [pltpu.SemaphoreType.DMA(())] * len(buffers)
    count, waits = 1 + len(ins), len(after)
    held = sum(nbytes(b.shape, b.dtype) for b in buffers + list(scratch) if "sem" not in str(b.dtype))
    moved = sum(nbytes(a.shape, a.dtype) for a in list(ins) + shapes)

    def whole(*refs):
        scal, in_refs = refs[0], list(refs[1:count])
        rest = refs[count + waits :]
        out_refs, rest = list(rest[: len(outs)]), rest[len(outs) + 1 :]
        in_raw, out_raw = list(in_refs), list(out_refs)
        own, rest = rest[: len(scratch)], rest[len(scratch) :]
        space, signals = rest[: len(buffers)], rest[len(buffers) :]

        def run():
            arrivals, departures = [], []
            for at, k in enumerate(far_in):
                in_refs[k] = Arriving(in_refs[k], ins[k].index, space[at], signals[at])
                arrivals.append(in_refs[k])
                if not ins[k].later:
                    in_refs[k].start()
            for at, k in enumerate(far_out, len(far_in)):
                out_refs[k] = Leaving(out_refs[k], space[at], signals[at])
                departures.append(out_refs[k])
            body(scal, *in_refs, *out_refs, *own)
            for a in arrivals:
                a.ready()
            for d in departures:
                d.send()
            for d in departures:
                d.copy.wait()

        if active is None:
            run()
        else:
            pl.when(scal[1] == active)(run)
        if passing is not None:
            given, made = passing
            at = len(far_in) + far_out.index(made)

            @pl.when(scal[1] != active)
            def _():
                for source, target in ((in_raw[given], space[at]), (space[at], out_raw[made])):
                    copy = pltpu.make_async_copy(source, target, signals[at])
                    copy.start()
                    copy.wait()

    specs = [HB if isinstance(x, (Far, Raw)) else VM for x in ins]
    arrays = [pinned(x.array) if isinstance(x, (Far, Raw)) else x for x in ins]
    return pl.pallas_call(
        whole,
        out_shape=shapes,
        in_specs=[SM] + specs + [HB if stays(a) else ANY for a in after],
        out_specs=[HB if len(x) > 2 and x[2] else VM for x in outs] + [HB],
        scratch_shapes=list(scratch) + buffers + sems,
        compiler_params=pltpu.CompilerParams(vmem_limit_bytes=held + (extra << 20)),
        cost_estimate=pl.CostEstimate(flops=flops, bytes_accessed=moved, transcendentals=0),
        name=getattr(body, "func", body).__name__,
    )(scal, *arrays, *[pinned(a) if stays(a) else a for a in after])


def gains_body(micro, scal, *refs):
    out = refs[-1]
    ready_all(*refs[:-1])
    first, refs = refs[:micro], refs[micro : -1]
    out[0:1] = sum(r[...] for r in first)
    for section in (0, 1):

        @pl.when(scal[1] == section)
        def _():
            mine = refs[2 * micro * section : 2 * micro * (section + 1)]
            out[1:2] = sum(r[...] for r in mine[:micro])
            out[2:3] = sum(r[...] for r in mine[micro:])


def place_body(n, el, capp, scal, labels, *outs):
    me = scal[0]
    tokens = labels.shape[1]
    r = lax.broadcasted_iota(jnp.int32, (tokens, tokens), 0)
    c = lax.broadcasted_iota(jnp.int32, (tokens, tokens), 1)
    lower = (c < r).astype(BF)
    experts = n * el
    for m in range(labels.shape[0]):
        lab = labels[m]
        hot = lab == lax.broadcasted_iota(jnp.int32, (tokens, experts), 1)
        hot = jnp.where(hot, 1.0, 0.0)
        before = dot(lower, hot.astype(BF))
        slot = jnp.sum(before * hot, axis=1, keepdims=True).astype(jnp.int32)
        where = ((lab // el) ^ me) * (el * capp) + (lab % el) * capp + slot
        wide = jnp.where(
            where == lax.broadcasted_iota(jnp.int32, (tokens, n * el * capp), 1), 1.0, 0.0
        )
        outs[m][...] = wide.T.astype(BF)


def send_slots(d_ref, rows, outs):
    size = outs[0].shape[0]
    for j, out in enumerate(outs):
        out[...] = dot(d_ref[j * size : (j + 1) * size, :], rows).astype(BF)


def self_fwd_body(n, hl, hs, scal, *refs):
    xs, (gains, w), refs = refs[:n], refs[n : n + 2], refs[n + 2 :]
    a, qkv, o, lse = refs[:4]
    parts = refs[4:]
    me, dec = scal[0], scal[1]
    tokens = xs[0].shape[0]
    group = n * tokens
    hw = hl * hs
    g = gains[0, 0:1]
    for j in range(n):
        unit, _ = norm_parts(xs[j][...].astype(F32))
        a[pl.ds((me ^ j) * tokens, tokens), :] = (unit * g).astype(BF)
    a.send()
    qkv[...] = dot(a[...], w[:, : 3 * hw]).astype(BF)
    qkv.send()

    def run(causal):
        for base in range(0, group, SEQ):
            logs = {}
            for h in range(hl):
                cols = slice(h * hs, (h + 1) * hs)
                k = qkv[base : base + SEQ, hw + h * hs : hw + (h + 1) * hs]
                v = qkv[base : base + SEQ, 2 * hw + h * hs : 2 * hw + (h + 1) * hs]
                for first in range(0, SEQ, QB):
                    rows = slice(base + first, base + first + QB)
                    width = first + QB if causal else SEQ
                    o[rows, cols], logs[first, h] = attend_tile(
                        qkv[rows, cols], k[:width], v[:width], first if causal else None
                    )
            for first in range(0, SEQ, QB):
                lse[base + first : base + first + QB, :] = by_lane(
                    [logs[first, h] for h in range(hl)]
                )

    pl.when(dec == 1)(lambda: run(True))
    pl.when(dec == 0)(lambda: run(False))
    for j in range(n):
        rows = o[pl.ds((me ^ j) * tokens, tokens), :]
        parts[j][...] = dot(rows, w[:, 3 * hw :], 1, 1).astype(BF)


def self_bwd_body(n, hl, hs, add, scal, *refs):
    gs, refs = refs[:n], refs[n:]
    a, qkv, o, lse, gains, w = refs[:6]
    olds, refs = refs[6 : 6 + add], [*refs[:6], *refs[6 + add :]]
    parts, (dw, dgain) = refs[6 : 6 + n], refs[6 + n : 8 + n]
    dso, do, dqkv, ps, dss = refs[8 + n :]
    me, dec = scal[0], scal[1]
    tokens = gs[0].shape[0]
    group = n * tokens
    hw = hl * hs
    scale = hs**-0.5
    for j in range(n):
        dso[pl.ds((me ^ j) * tokens, tokens), :] = gs[j][...]
    do[...] = dot(dso[...], w[:, 3 * hw :]).astype(BF)
    ready_all(o, lse, qkv)
    start_all(a, *olds)

    def run(causal):
        for base in range(0, group, SEQ):
            keys = slice(base, base + SEQ)
            rows_of = [slice(base + f, base + f + QB) for f in range(0, SEQ, QB)]
            logs = [lse[rows, :].T for rows in rows_of]
            inners = [
                by_lane(
                    [
                        row_products(
                            do[rows, h * hs : (h + 1) * hs], o[rows, h * hs : (h + 1) * hs]
                        )
                        for h in range(hl)
                    ]
                ).T
                for rows in rows_of
            ]
            dqs = []
            for h in range(hl):
                cols = slice(h * hs, (h + 1) * hs)
                q, dh = qkv[keys, cols], do[keys, cols]
                k = qkv[keys, hw + h * hs : hw + (h + 1) * hs]
                v = qkv[keys, 2 * hw + h * hs : 2 * hw + (h + 1) * hs]
                for i, first in enumerate(range(0, SEQ, QB)):
                    width = first + QB if causal else SEQ
                    block = slice(first, first + QB)
                    p, ds = attend_tile_back(
                        q[block],
                        k[:width],
                        v[:width],
                        dh[block],
                        logs[i][h : h + 1],
                        inners[i][h : h + 1],
                        first if causal else None,
                    )
                    ps[:width, block] = p
                    dss[:width, block] = ds
                kt = (k.astype(F32) * scale).astype(BF).T
                if causal:
                    dk = [dot(dss[f : f + QB, f:], q[f:]) for f in range(0, SEQ, QB)]
                    dv = [dot(ps[f : f + QB, f:], dh[f:]) for f in range(0, SEQ, QB)]
                    dk, dv = jnp.concatenate(dk, axis=0), jnp.concatenate(dv, axis=0)
                    dq = [
                        dot(kt[:, : f + QB], dss[: f + QB, f : f + QB]) for f in range(0, SEQ, QB)
                    ]
                    dqs.append(jnp.concatenate(dq, axis=1))
                else:
                    dk, dv = dot(dss[...], q), dot(ps[...], dh)
                    dqs.append(dot(kt, dss[...]))
                dqkv[keys, hw + h * hs : hw + (h + 1) * hs] = (dk * scale).astype(BF)
                dqkv[keys, 2 * hw + h * hs : 2 * hw + (h + 1) * hs] = dv.astype(BF)
            dqkv[keys, :hw] = jnp.concatenate(dqs, axis=0).T.astype(BF)

    pl.when(dec == 1)(lambda: run(True))
    pl.when(dec == 0)(lambda: run(False))
    total = jnp.zeros((1, a.shape[1]), F32)
    for j in range(n):
        rows = pl.ds((me ^ j) * tokens, tokens)
        da = dot(dqkv[rows, :], w[:, : 3 * hw], 1, 1)
        parts[j][...] = da.astype(BF)
        total += jnp.sum(da * a[rows, :].astype(F32), axis=0, keepdims=True)
    dgain[...] = total / gains[0, 0:1]
    grads = dot(a[...], dqkv[...], 0, 0), dot(dso[...], o[...], 0, 0)
    for h in range(hl):
        for t in range(4):
            at = (t % 3) * hw + h * hs
            to = slice((4 * h + t) * hs, (4 * h + t + 1) * hs)
            part = grads[0][:, at : at + hs] if t < 3 else grads[1][:, h * hs : (h + 1) * hs]
            dw[:, to] = ((part + olds[0][:, to]) if add else part).astype(dw.dtype)


def after_self_body(n, pieces, scal, *refs):
    x, refs = refs[0], refs[1:]
    ps, (gains, d, cot), (h1,), outs = (
        refs[:pieces],
        refs[pieces : pieces + 3],
        refs[pieces + 3 : pieces + 4],
        refs[pieces + 4 :],
    )
    rows = x[...].astype(F32)
    for p in ps:
        rows = rows + p[...].astype(F32)
    h1[...] = rows
    h1.send()
    unit, _ = norm_parts(rows)
    u = (unit * gains[0, 2:3]).astype(BF)
    chosen = jnp.where(scal[1] == 0, u.astype(F32), cot[...].astype(F32)).astype(BF)
    send_slots(d, chosen, outs)


def memory_body(n, scal, *refs):
    rs, (h1, d, gains), (y, m) = refs[:n], refs[n : n + 3], refs[n + 3 :]
    stacked = jnp.concatenate([r[...] for r in rs], axis=0)
    rows = h1[...] + dot(d[...], stacked, 0, 0)
    y[...] = rows
    y.send()
    unit, _ = norm_parts(rows)
    m[...] = (unit * gains[0, 1:2]).astype(BF)


def final_body(n, micro, scal, *refs):
    out = refs[-1]
    for m in range(micro):
        rs, (h2, d, ye) = refs[:n], refs[n : n + 3]
        refs = refs[n + 3 :]
        ready_all(h2, d, ye)

        @pl.when(scal[1] == 0)
        def _():
            out[0, m] = ye[...].astype(BF)

        @pl.when(scal[1] == 1)
        def _():
            stacked = jnp.concatenate([r[...] for r in rs], axis=0)
            out[0, m] = (h2[...] + dot(d[...], stacked, 0, 0)).astype(BF)


def cross_fwd_body(n, per, hl, hs, scal, *refs):
    ms, refs = refs[:per], refs[per:]
    wx, wkv, (h1, gains, d), refs = refs[:n], refs[n : 2 * n], refs[2 * n : 2 * n + 3], refs[2 * n + 3 :]
    h2, c, mem, qc, kv, oc, lse = refs[:7]
    outs = refs[7:]
    hw = hl * hs
    tokens = h1.shape[0]
    for j in range(per):
        mem[j * tokens : (j + 1) * tokens, :] = ms[j][...]
    mem.send()
    unit, _ = norm_parts(h1[...])
    start_all(*wkv)
    c[...] = (unit * gains[0, 1:2]).astype(BF)
    c.send()
    for j in range(n):
        qc[:, j * hw : (j + 1) * hw] = dot(c[...], wx[j][:, :hw]).astype(BF)
    qc.send()
    for j in range(n):
        kv[:, 2 * j * hw : 2 * (j + 1) * hw] = dot(mem[...], wkv[j][...]).astype(BF)
    kv.send()
    total = h1[...]
    logs = []
    for j in range(n):
        for h in range(hl):
            at = j * hw + h * hs
            k = kv[:, 2 * j * hw + h * hs : 2 * j * hw + (h + 1) * hs]
            v = kv[:, (2 * j + 1) * hw + h * hs : (2 * j + 1) * hw + (h + 1) * hs]
            oc[:, at : at + hs], log = attend_tile(qc[:, at : at + hs], k, v, None)
            logs.append(log)
        total = total + dot(oc[:, j * hw : (j + 1) * hw], wx[j][:, hw:], 1, 1)
    oc.send()
    lse[...] = by_lane(logs)
    lse.send()
    h2[...] = total
    h2.send()
    unit, _ = norm_parts(total)
    send_slots(d, (unit * gains[0, 2:3]).astype(BF), outs)


def cross_bwd_body(n, per, hl, hs, scal, *refs):
    dus, wx, wkv, refs = refs[:n], refs[n : 2 * n], refs[2 * n : 3 * n], refs[3 * n :]
    h2, gains, d, cot, qc, kv, oc, lse = refs[:8]
    refs = refs[8:]
    dh2, dco, dqc, dkv, dgain = refs[:5]
    dms, (doc,) = refs[5 : 5 + per], refs[5 + per :]
    hw = hl * hs
    tokens = h2.shape[0]
    stacked = jnp.concatenate([r[...] for r in dus], axis=0)
    unit, inverse = norm_parts(h2[...])
    start_all(*wx, oc, lse, qc, kv, *wkv)
    back, gained = norm_back(dot(d[...], stacked, 0, 0), unit, inverse, gains[0, 2:3])
    dgain[...] = gained
    total = cot[...].astype(F32) + back
    dh2[...] = total
    dh2.send()
    dco[...] = total.astype(BF)
    dco.send()
    for j in range(n):
        doc[:, j * hw : (j + 1) * hw] = dot(dco[...], wx[j][:, hw:]).astype(BF)
    logs = lse[...].T
    places = [slice(i * hs, (i + 1) * hs) for i in range(n * hl)]
    inner = by_lane([row_products(doc[:, at], oc[:, at]) for at in places]).T
    scale = hs**-0.5
    dqs = []
    for i, at in enumerate(places):
        j, h = i // hl, i % hl
        k_at = slice(2 * j * hw + h * hs, 2 * j * hw + (h + 1) * hs)
        v_at = slice((2 * j + 1) * hw + h * hs, (2 * j + 1) * hw + (h + 1) * hs)
        q, k, do = qc[:, at], kv[:, k_at], doc[:, at]
        p, ds = attend_tile_back(q, k, kv[:, v_at], do, logs[i : i + 1], inner[i : i + 1], None)
        dkv[:, k_at] = (dot(ds, q) * scale).astype(BF)
        dkv[:, v_at] = dot(p, do).astype(BF)
        dqs.append(dot((k.astype(F32) * scale).astype(BF).T, ds))
    dkv.send()
    dqc[...] = jnp.concatenate(dqs, axis=0).T.astype(BF)
    dqc.send()
    for i in range(per):
        rows = slice(i * tokens, (i + 1) * tokens)
        total = 0.0
        for j in range(n):
            total += dot(dkv[rows, 2 * j * hw : 2 * (j + 1) * hw], wkv[j][...], 1, 1)
        dms[i][...] = total.astype(BF)


def cross_late_body(n, hl, hs, count, scal, *refs):
    wx, (dh2, dco, dqc, dkv, oc, c, mem, h1, gains) = refs[:n], refs[n : n + 9]
    olds, refs = refs[n + 9 : n + 9 + count], refs[n + 9 + count :]
    dh1, dgain, dws = refs[0], refs[1], refs[2:]
    hw = hl * hs
    dc = jnp.zeros(h1.shape, F32)
    for j in range(n):
        dc += dot(dqc[:, j * hw : (j + 1) * hw], wx[j][:, :hw], 1, 1)
    unit, inverse = norm_parts(h1[...])
    back, gained = norm_back(dc, unit, inverse, gains[0, 1:2])
    dh1[...] = dh2[...] + back
    dh1.send()
    dgain[...] = gained
    ct, dt, mt = c[...].T, dco[...].T, mem[...].T
    for j in range(n):
        dq = dot(ct, dqc[:, j * hw : (j + 1) * hw])
        de = dot(dt, oc[:, j * hw : (j + 1) * hw])
        dkv_j = dot(mt, dkv[:, 2 * j * hw : 2 * (j + 1) * hw])
        for h in range(hl):
            at = slice(h * hs, (h + 1) * hs)
            parts = dq[:, at], de[:, at], dkv_j[:, at], dkv_j[:, hw + h * hs : hw + (h + 1) * hs]
            for t, part in enumerate(parts):
                to = (t // 2) * 2 * hw + (2 * h + t % 2) * hs
                if count:
                    part = part + olds[j][:, to : to + hs].astype(F32)
                dws[j][:, to : to + hs] = part.astype(BF)


def sum_body(scal, *refs):
    total = refs[0][...].astype(F32)
    for ref in refs[1:-1]:
        total = total + ref[...].astype(F32)
    refs[-1][...] = total.astype(refs[-1].dtype)


def halves_body(scal, *refs):
    *parts, left, right = refs
    total = parts[0][...].astype(F32)
    for ref in parts[1:]:
        total = total + ref[...].astype(F32)
    half = total.shape[1] // 2
    left[...] = total[:, :half].astype(BF)
    right[...] = total[:, half:].astype(BF)


def pick_body(scal, first, second, gains, out):
    width, wide = first.shape
    out[:width, :] = jnp.where(
        scal[1] == 1, first[...].astype(F32), second[...].astype(F32)
    ).astype(BF)
    rows = [
        gains[i : i + 1, c : c + wide]
        for i in range(gains.shape[0])
        for c in range(0, gains.shape[1], wide)
    ]
    rows.append(jnp.zeros((out.shape[0] - width - len(rows), wide), F32))
    out[width:, :] = jnp.concatenate(rows, axis=0).astype(BF)


def memory_back_body(n, scal, *refs):
    (dm, y, gains, cot, d), (dy, dgain), outs = refs[:5], refs[5:7], refs[7:]
    unit, inverse = norm_parts(y[...])
    back, gained = norm_back(dm[...].astype(F32), unit, inverse, gains[0, 1:2])
    dgain[...] = gained
    rows = cot[...].astype(F32) + back
    dy[...] = rows
    dy.send()
    send_slots(d, rows.astype(BF), outs)


def before_self_body(n, scal, *refs):
    dus, (d, dy, h1, gains, given), (dh1, dso, dgain) = refs[:n], refs[n : n + 5], refs[n + 5 :]
    ready_all(gains, h1, d, dy, given)

    @pl.when(scal[1] == 0)
    def _():
        stacked = jnp.concatenate([r[...] for r in dus], axis=0)
        unit, inverse = norm_parts(h1[...])
        back, gained = norm_back(dot(d[...], stacked, 0, 0), unit, inverse, gains[0, 2:3])
        rows = dy[...] + back
        dh1[...] = rows
        dso[...] = rows.astype(BF)
        dgain[...] = gained

    @pl.when(scal[1] == 1)
    def _():
        dh1[...] = given[...]
        dso[...] = given[...].astype(BF)
        dgain[...] = jnp.zeros(dgain.shape, F32)


def finish_body(pieces, micro, scal, *refs):
    gains, out, refs = refs[0], refs[-1], refs[1:-1]
    for m in range(micro):
        ps, (dh1, x), refs = refs[:pieces], refs[pieces : pieces + 2], refs[pieces + 2 :]
        da = ps[0][...].astype(F32)
        for p in ps[1:]:
            da = da + p[...].astype(F32)
        unit, inverse = norm_parts(x[...].astype(F32))
        back, _ = norm_back(da, unit, inverse, gains[0, 0:1])
        out[0, m] = dh1[...] + back


def gelu_low(z):
    z = z.astype(BF)

    def c(value):
        return jnp.asarray(value, BF)

    inner = c(ROOT) + c(ROOT * 0.044715) * (z * z)
    half = c(0.5) + c(0.5) * jnp.tanh(z * inner)
    value = z * half
    return value, half + (value - value * half) * (c(6.0) * inner - c(4.0 * ROOT))


def expert_body(n, el, capp, block, mode, passed, scal, *refs):
    us, refs = refs[:n], refs[n:]
    drs = ()
    if mode != "fwd":
        drs, refs = refs[:n], refs[n:]
    (wi, wo), refs = refs[:2], refs[2 + passed :]
    rs, dus = (), ()
    if mode != "back":
        rs, refs = refs[:n], refs[n:]
    if mode != "fwd":
        dus, refs = refs[:n], refs[n:]
    u_all = dr_all = None
    if mode != "back":
        u_all, refs = refs[0], refs[1:]
    if mode != "fwd":
        dr_all, refs = refs[0], refs[1:]
    ff = wi.shape[3]
    rows_u = [
        jnp.concatenate([us[j][e * capp : (e + 1) * capp, :] for j in range(n)], axis=0)
        for e in range(el)
    ]
    rows_dr = [
        jnp.concatenate([drs[j][e * capp : (e + 1) * capp, :] for j in range(n)], axis=0)
        for e in range(el if drs else 0)
    ]
    for e in range(el):
        if u_all is not None:
            u_all[e] = rows_u[e]
        if dr_all is not None:
            dr_all[e] = rows_dr[e]
    for ref in (u_all, dr_all):
        if ref is not None:
            ref.send()
    for e in range(el):
        racc = dacc = 0.0
        for f in range(0, ff, block):
            part = slice(f, f + block)
            wi_f, wo_f = wi[0, e, :, part], wo[0, e, part, :]
            z = dot(rows_u[e], wi_f)
            if drs:
                g, slope = gelu_low(z)
            else:
                g = gelu_value(z)
            if rs:
                racc += dot(g.astype(BF), wo_f)
            if dus:
                dz = (dot(rows_dr[e], wo_f, 1, 1).astype(slope.dtype) * slope).astype(BF)
                dacc += dot(dz, wi_f, 1, 1)
        for j in range(n):
            part, at = slice(j * capp, (j + 1) * capp), slice(e * capp, (e + 1) * capp)
            if rs:
                rs[j][at, :] = racc[part].astype(BF)
            if dus:
                dus[j][at, :] = dacc[part].astype(BF)


def experts(step, us, drs, w_in, w_out, capp, active, mode, other=None):
    n, el = len(us), w_in.shape[1]
    width, ff = w_in.shape[2:]
    block = 1024
    outs = n * (2 if mode == "both" else 1)
    products = {"fwd": 2, "both": 4, "back": 3}[mode]
    result = step(
        functools.partial(expert_body, n, el, capp, block, mode, int(other is not None)),
        [*us, *drs, w_in, w_out, *([] if other is None else [Raw(other)])],
        [((el * capp, width), BF)] * outs
        + [((el, n * capp, width), BF, True)] * (2 if mode == "both" else 1),
        flops=products * 2 * el * n * capp * width * ff,
        active=active,
        passing=None if other is None else (len(us) + len(drs) + 2, outs),
    )
    return [result[i : i + n] for i in range(0, outs, n)], result[outs:]


def expert_grad_body(add, *refs):
    u_ref, dr_ref, wi, wo = refs[:4]
    refs = refs[4:]
    olds, refs = (refs[:2], refs[2:]) if add else ((), refs)
    dwi, dwo, ut = refs[-3:]
    lead, _, rows, width = u_ref.shape
    chunk = 1
    while 2 * chunk * rows <= 1024 and lead % (2 * chunk) == 0:
        chunk *= 2
    size = chunk * rows

    @pl.when(pl.program_id(1) == 0)
    def _():
        for at in range(0, lead, chunk):
            u = u_ref[at : at + chunk, 0].reshape(size, width)
            ut[:, at * rows : at * rows + size] = u.T

    for at in range(0, lead, chunk):
        u = u_ref[at : at + chunk, 0].reshape(size, width)
        dr = dr_ref[at : at + chunk, 0].reshape(size, width)
        g, slope = gelu_low(dot(u, wi[0, 0]))
        dz = dot(dr, wo[0, 0], 1, 1).astype(BF) * slope
        di = dot(ut[:, at * rows : at * rows + size], dz)
        do = dot(g, dr, 0, 0)
        if at:
            dwi[0, 0] += di
            dwo[0, 0] += do
        elif add:
            dwi[0, 0] = olds[0][0, 0] + di
            dwo[0, 0] = olds[1][0, 0] + do
        else:
            dwi[0, 0] = di
            dwo[0, 0] = do


def expert_grads(u, dr, w_in, w_out, olds, after, first, many, add):
    lead, _, rows, width = u.shape
    ff = w_in.shape[3]
    block = 512
    spec = pl.BlockSpec((lead, 1, rows, width), lambda e, f: (0, first + e, 0, 0))
    into = pl.BlockSpec((1, 1, width, block), lambda e, f: (0, first + e, 0, f))
    back = pl.BlockSpec((1, 1, block, width), lambda e, f: (0, first + e, f, 0))
    body = functools.partial(expert_grad_body, add)
    given = 4 + (len(olds) if add else 0)
    count = 4 + len(olds) + len(after)

    def trimmed(*refs):
        dwi, dwo, _, ut = refs[count:]
        body(*refs[:given], dwi, dwo, ut)

    arrays = [pinned(x) for x in (u, dr, w_in, w_out, *olds)]
    after = [pinned(a) if stays(a) else a for a in after]
    return pl.pallas_call(
        trimmed,
        grid=(many, ff // block),
        in_specs=[spec] * 2
        + [into, back]
        + ([into, back] if add else [HB, HB])[: len(olds)]
        + [HB if stays(a) else ANY for a in after],
        out_specs=[into, back, HB],
        out_shape=[
            pltpu.HBM(w_in.shape, F32),
            pltpu.HBM(w_out.shape, F32),
            pltpu.HBM((8, 128), F32),
        ],
        scratch_shapes=[pltpu.VMEM((width, lead * rows), BF)],
        input_output_aliases={4: 0, 5: 1} if olds else {},
        compiler_params=pltpu.CompilerParams(
            vmem_limit_bytes=(22 << 20) + 10 * lead * rows * width
        ),
        cost_estimate=pl.CostEstimate(
            flops=8 * lead * many * rows * width * ff, bytes_accessed=0, transcendentals=0
        ),
        name="expert_grads",
    )(*arrays, *after)


def on_device(inputs, cotangent, expert_ids, self_proj, cross_proj, gains, w_in, w_out):
    micro, tokens, width = inputs.shape[1:]
    n = lax.axis_size("mp")
    hl = self_proj.shape[2]
    hs = self_proj.shape[3] // 4
    hw = hl * hs
    el = w_in.shape[1]
    capacity = max(2, 3 * tokens // (2 * n * el))
    capp = -(-capacity // 16) * 16
    slots = el * capp
    per = SEQ // tokens
    group = n * tokens
    M = range(micro)
    decoder = lax.axis_index("section") == 1
    scal = jnp.stack([lax.axis_index("mp"), lax.axis_index("section")]).astype(jnp.int32)
    last = []

    def step(body, ins, outs, **more):
        *res, token = call(body, scal, ins, outs, after=list(last), **more)
        last[:] = [token]
        return res

    def swap(x, k, sections=(0, 1)):
        pairs = [(s * n + i, s * n + (i ^ k)) for s in sections for i in range(n)]
        return lax.ppermute(x, ("section", "mp"), pairs)

    def gather(x, count, sections=(0, 1), gated=False):
        blocks = {0: x}
        bit = count // 2
        while bit:
            blocks.update({j ^ bit: swap(b, bit, sections) for j, b in list(blocks.items())})
            if gated and bit == count // 2:
                (blocks[bit],) = gate([blocks[bit]])
            bit //= 2
        return [blocks[j] for j in range(count)]

    def total(pieces, dtype):
        return call(sum_body, scal, pieces, [(pieces[0].shape, dtype)])[0]

    def scatter(blocks, hold=False):
        live = {j: [b] for j, b in enumerate(blocks)}
        bit = 1
        while bit < len(blocks):
            for j in [j for j in live if j & bit]:
                pieces = live.pop(j)
                out = pieces[0]
                if len(pieces) > 1:
                    out = sum(p.astype(F32) for p in pieces).astype(BF)
                    if hold:
                        last.append(out)
                live[j ^ bit].append(swap(out, bit))
            bit *= 2
        return live[0]

    def exchange(blocks):
        return [blocks[0]] + [swap(blocks[j], j) for j in range(1, n)]

    def gate(arrays, waits=(), space=ANY):
        count = len(arrays)
        waits = [*last, *waits]
        *arrays, token = pl.pallas_call(
            lambda *refs: None,
            out_shape=[
                (pltpu.HBM if space is HB else jax.ShapeDtypeStruct)(a.shape, a.dtype)
                for a in arrays
            ]
            + [pltpu.HBM((8, 128), F32)],
            in_specs=[space] * count + [HB if stays(a) else ANY for a in waits],
            out_specs=[space] * count + [HB],
            input_output_aliases={i: i for i in range(count)},
            compiler_params=pltpu.CompilerParams(vmem_limit_bytes=1 << 20),
            name="gate",
        )(
            *[pinned(a) if space is HB else a for a in arrays],
            *[pinned(a) if stays(a) else a for a in waits],
        )
        last[:] = [token]
        return arrays

    def lazy(fars):
        return [Far(f.array, *f.index, later=True) for f in fars]

    def to_decoder(x):
        return lax.ppermute(x, "section", [(0, 1)])

    def to_encoder(x):
        return lax.ppermute(x, "section", [(1, 0)])

    xs = [inputs[0, m] for m in M]
    ws = self_proj[0].reshape(width, hl, 4, hs).transpose(0, 2, 1, 3).reshape(width, 4 * hw)
    wc = cross_proj[0].reshape(width, hl, 2, hs).transpose(0, 2, 1, 3).reshape(width, 2 * hw)
    row, wide, line = ((tokens, width), BF), ((tokens, width), F32, True), ((1, width), F32, True)
    slot = ((slots, width), BF)

    def far(shape, dtype=BF):
        return (shape, dtype, True)

    last.extend([ws, wc])
    routes = step(
        functools.partial(place_body, n, el, capp),
        [expert_ids[0]],
        [far((n * slots, tokens))] * micro,
    )
    routes = [Far(r) for r in routes]
    gain = Far(gains)
    x_far = [Far(inputs, 0, m) for m in M]
    cots = [Far(cotangent, 0, m) for m in M]

    x_all = [gather(xs[m], n, gated=m == 0) for m in M]
    saved, self_parts = [], []
    for m in M:
        res = step(
            functools.partial(self_fwd_body, n, hl, hs),
            [*x_all[m], gain, Far(ws)],
            [
                far((group, width)),
                far((group, 3 * hw)),
                far((group, hw)),
                far((group, 128), F32),
            ]
            + [row] * n,
            flops=2 * group * width * 4 * hw + 4 * 4 * group * SEQ * hw,
        )
        saved.append(res[:4])
        parts = res[4:]
        if m:
            last.extend(self_parts[-1])
            parts = gate(parts)
        self_parts.append(scatter(parts, m < micro - 1))
    h1, first_slots, ye, mem_all, rs, enc_u = [], [], [], [], [], []

    def after_self(m):
        res = step(
            functools.partial(after_self_body, n, len(self_parts[m])),
            [x_far[m], *self_parts[m], gain, routes[m], cots[m]],
            [wide] + [slot] * n,
            flops=2 * n * slots * tokens * width,
        )
        h1.append(Far(res[0]))
        first_slots.append(exchange(res[1:]))

    def encoder_experts(m):
        (r,), (u,) = experts(step, first_slots[m], (), w_in, w_out, capp, 0, "fwd")
        rs.append(exchange(r))
        enc_u.append(u)

    def memory(m):
        y, mem = step(
            functools.partial(memory_body, n),
            [*rs[m], h1[m], routes[m], gain],
            [wide, row],
            flops=2 * n * slots * tokens * width,
            active=0,
        )
        ye.append(Far(y))
        mem_all.append(to_decoder(mem))

    after_self(0)
    for m in M:
        encoder_experts(m)
        if m < micro - 1:
            after_self(m + 1)
        memory(m)
    wx_all = [Far(b) for b in gather(wc, n, (1,))]
    wkv_all = [Far(b, later=True) for b in gather(to_decoder(wc), n, (1,))]

    crossed, second_slots, mem_got = [], [], [gather(mem_all[0], per)]
    rs, dus, dec_u, dec_dr = [], [], [], []
    late, gain_parts, kept, pieces, dms = [], [[], [], []], [], [], []

    def cross(m):
        if m:
            mem_got.append(gather(mem_all[m], per))
        res = step(
            functools.partial(cross_fwd_body, n, per, hl, hs),
            [*mem_got[m], *[f.array for f in (*wx_all, *wkv_all)], h1[m], gain, routes[m]],
            [
                wide,
                far((tokens, width)),
                far((SEQ, width)),
                far((tokens, n * hw)),
                far((SEQ, 2 * n * hw)),
                far((tokens, n * hw)),
                far((tokens, 128), F32),
            ]
            + [slot] * n,
            flops=4 * SEQ * width * n * hw + 4 * 4 * tokens * SEQ * n * hw,
            active=1,
        )
        crossed.append([Far(r) for r in res[:7]])
        second_slots.append(exchange(res[7:]))

    def decoder_experts(m):
        (r, du), (u, dr) = experts(
            step,
            second_slots[m],
            [Far(b) for b in first_slots[m]],
            w_in,
            w_out,
            capp,
            1,
            "both",
            enc_u[m],
        )
        dus.append(exchange(du))
        rs.append(r)
        dec_u.append(u)
        dec_dr.append(dr)

    def cross_back(m):
        h2, c, mem, qc, kv, oc, lse = crossed[m]
        res = step(
            functools.partial(cross_bwd_body, n, per, hl, hs),
            [*dus[m], *lazy(wx_all), *wkv_all, h2, gain, routes[m], cots[m]]
            + lazy((qc, kv, oc, lse)),
            [wide, far((tokens, width)), far((tokens, n * hw)), far((SEQ, 2 * n * hw)), line]
            + [row] * per,
            scratch=[pltpu.VMEM((tokens, n * hw), BF)],
            flops=4 * SEQ * width * n * hw + 4 * 10 * tokens * SEQ * n * hw,
            active=1,
        )
        kept.append([Far(r) for r in res[:4]])
        gain_parts[2].append(res[4])
        parts = res[5:]
        if m:
            last.extend(pieces[-1])
            parts = gate(parts)
        pieces.append(scatter(parts, m < micro - 1))
        dms.append(to_encoder(sum(p.astype(F32) for p in pieces[m]).astype(BF)))

    for m in M:
        cross(m)
    for m in M:
        decoder_experts(m)
        cross_back(m)

    def rows_of(encoder_rows, decoder_rows, forward=False):
        whole = (decoder_rows if forward else encoder_rows)[None]
        return lax.all_gather(whole, "dp", axis=0, tiled=True)

    u_rows = [rows_of(enc_u[m], dec_u[m], True) for m in M]

    memory_gain, dr_rows, dh1, dso, parts_a, self_total = [], [], [], [], [], None

    def experts_back(m):
        res = step(
            functools.partial(memory_back_body, n),
            [dms[m], ye[m], gain, cots[m], routes[m]],
            [wide, line] + [slot] * n,
            active=0,
        )
        memory_gain.append(res[1])
        third = exchange(res[2:])
        (du,), (dr,) = experts(
            step,
            [Far(b) for b in first_slots[m]],
            third,
            w_in,
            w_out,
            capp,
            0,
            "back",
            dec_dr[m],
        )
        dr_rows.append(rows_of(dr, dec_dr[m]))
        return res[0], exchange(du)

    def cross_late(m):
        h2, c, mem, qc, kv, oc, lse = crossed[m]
        olds = late[m - 1][2:] if m else []
        late.append(
            step(
                functools.partial(cross_late_body, n, hl, hs, len(olds)),
                [*wx_all, *kept[m], oc, c, mem, h1[m], gain, *[Far(x) for x in olds]],
                [wide, line] + [far((width, 4 * hw))] * n,
                flops=8 * SEQ * width * n * hw,
                active=1,
            )
        )

    def before_self(m, dy, du):
        res = step(
            functools.partial(before_self_body, n),
            [*du, routes[m], Far(dy), h1[m], gain, Far(late[m][0])],
            [wide, row, line],
        )
        dh1.append(res[0])
        dso.append(gather(res[1], n))
        gain_parts[2].append(res[2])

    def self_back(m, before):
        a, qkv, o, lse = saved[m]
        res = step(
            functools.partial(self_bwd_body, n, hl, hs, bool(before)),
            [*dso[m], Far(a, later=True)]
            + [Far(x) for x in (qkv, o, lse)]
            + [gain, Far(ws)]
            + [Far(x, later=True) for x in before],
            [row] * n + [far((width, 4 * hw), BF if m == micro - 1 else F32), line],
            scratch=[
                pltpu.VMEM((group, width), BF),
                pltpu.VMEM((group, hw), BF),
                pltpu.VMEM((group, 3 * hw), BF),
                pltpu.VMEM((SEQ, SEQ), BF),
                pltpu.VMEM((SEQ, SEQ), BF),
            ],
            flops=2 * group * width * 8 * hw + 4 * 10 * group * SEQ * hw,
        )
        parts_a.append(scatter(res[:n], m < micro - 1))
        gain_parts[0].append(res[n + 1])
        return [res[n]]

    totals = []

    def grads_of(m, first, many):
        *new, token = expert_grads(
            u_rows[m], dr_rows[m], w_in, w_out, totals, list(last), first, many, m > 0
        )
        totals[:], last[:] = new, [token]

    grads = []
    for m in M:
        dy, du = experts_back(m)
        if m:
            grads = self_back(m - 1, grads)
        cross_late(m)
        before_self(m, dy, du)
    cross_pieces = scatter(late[-1][2:])
    grads = self_back(micro - 1, grads)
    own, remote = step(halves_body, cross_pieces, [((width, 2 * hw), BF)] * 2)
    remote = to_encoder(remote)
    (gain_total,) = step(
        functools.partial(gains_body, micro),
        [Far(g) for g in (*gain_parts[0], *memory_gain, *gain_parts[2][micro:])]
        + [Far(g) for g in (*[x[1] for x in late], *gain_parts[2][:micro])],
        [((3, width), F32)],
    )

    def hop(x, bit):
        return x, lax.ppermute(x, "mp", [(i, i ^ bit) for i in range(n)])

    def land(pair):
        return step(sum_body, pair, [((3, width), F32)])[0]

    bit = 1
    while 2 * bit < n:
        gain_total = land(hop(gain_total, bit))
        bit *= 2
    pair = hop(gain_total, bit)
    grads_of(0, 0, 1)
    gain_total = land(pair)
    gain_rows = 3 * width // (2 * hw)
    under = -(-gain_rows // 16) * 16
    (cross_total,) = step(
        pick_body, [own, remote, gain_total], [far((width + under, 2 * hw))]
    )
    sums = lax.psum(tuple(gate([*grads, cross_total], [*u_rows, *dr_rows], HB)), "dp")
    sums = lax.optimization_barrier(sums)
    rs[0] = exchange(gate(rs[0]))
    grads_of(0, 1, el - 1)
    (input_grads,) = step(
        functools.partial(finish_body, len(parts_a[0]), micro),
        [gain] + [x for i in M for x in (*parts_a[i], Far(dh1[i]), x_far[i])],
        [((1, micro, tokens, width), F32, True)],
    )
    rs[1:] = [exchange(r) for r in rs[1:]]
    for m in range(1, micro):
        for e in range(el):
            grads_of(m, e, 1)
            if m == 1 and e == 0:
                (outs,) = step(
                    functools.partial(final_body, n, micro),
                    [x for m in M for x in (*rs[m], crossed[m][0], routes[m], ye[m])],
                    [((1, micro, tokens, width), BF, True)],
                )
    gain_total = sums[1][width : width + gain_rows].reshape(3, width).astype(F32)
    first_total, second_total = totals
    self_total = sums[0].astype(F32).reshape(width, hl, 4 * hs)
    cross_total = sums[1][:width].astype(F32).reshape(width, hl, 2 * hs)
    return (
        outs,
        input_grads,
        self_total[None],
        cross_total[None],
        gain_total[None],
        first_total,
        second_total,
    )


def solution(mesh):
    rows = P("section", None, ("dp", "mp"), None)
    heads = P("section", None, "mp", None)
    expert = P("section", "mp", None, None)
    return jax.shard_map(
        on_device,
        mesh=mesh,
        in_specs=(rows, rows, rows, heads, heads, P("section", None, None), expert, expert),
        out_specs=(rows, rows, heads, heads, P("section", None, None), expert, expert),
        check_vma=False,
    )
```
